512 devices in a mesh: brick: 32 (over y, x, z_hi), chan: 16 (over z_lo, core).
Axes of the slice: x: 4, y: 4, z: 16 (z_hi: 2, z_lo: 8; z = z_hi * 8 + z_lo), core: 2. Of those that a mesh axis runs over, the one named last changes fastest.
Arguments:
- node_x: bfloat16 [49, 128, 4096], P(None, 'chan', 'brick'), may hold values from -6 to 6
- cotangent: bfloat16 [49, 128, 4096], P(None, 'chan', 'brick'), may hold values from -6 to 6
- wigner: bfloat16 [235, 32768], P(None, 'brick'), may hold values from -4 to 4
- src_index: int32 [32768], P('brick'), may hold values from 0 to 191
- dst_index: int32 [32768], P('brick'), may hold values from 0 to 127
- edge_scale: float32 [32768], P('brick'), may hold values from 0.1 to 1
- edge_count: int32 [32], P('brick'), may hold values from 341 to 1024, as said below
- w_zero: bfloat16 [7, 128, 7, 128], P(None, 'chan'), may hold values from -0.1875 to 0.1875
- w_one: bfloat16 [2, 6, 128, 6, 128], P(None, None, 'chan'), may hold values from -0.15625 to 0.15625
- w_two: bfloat16 [2, 5, 128, 5, 128], P(None, None, 'chan'), may hold values from -0.15625 to 0.15625
Outputs:
- grad_x: float32 [49, 128, 4096], P(None, 'chan', 'brick')
- grad_w_zero: float32 [7, 128, 7, 128], P(None, 'chan', None, 'brick')
- grad_w_one: float32 [2, 6, 128, 6, 128], P(None, None, 'chan', None, 'brick')
- grad_w_two: float32 [2, 5, 128, 5, 128], P(None, None, 'chan', None, 'brick')
The draws below stay inside these ranges and needn't reach their ends.
Inputs may be any that keep to these rules, and one draw needn't show every extreme that they name: Slots 0 to edge_count[b] - 1 of brick b hold edges, the rest are padding; one brick's list is full.
All inputs are finite; a program needn't handle non-finite values.
Results may differ from the reference program's by a relative error of at most 0.0065.
Values may be sent and summed in bfloat16 or wider, within the bound.
No kernel may reach another device: no remote copies, remote signals or barrier semaphores. Data moves between devices by JAX's collectives and lax.ppermute only.
A program may use at most 64 MiB of HBM per device.

```python
import jax
import jax.numpy as jnp
import numpy as np
from jax import lax

C = 128
COEF = 49
ROT = 235
L0 = 7
L1 = 6
L2 = 5
A_DEV = 128
RIM = 32
EDGE_CAP = 1024
BRICKS = 32
ATOMS = 4096
EDGES = 32768


def wigner_scales():
    scales = []
    for degree in range(7):
        max_order = min(degree, 2)
        span_cols = 2 * degree + 1
        scales += [span_cols ** (-0.5)] * ((2 * max_order + 1) * span_cols)
    return np.array(scales, dtype=np.float32)


def draw_wigner(key, part):
    key = jax.random.fold_in(key, 11)
    scales = jnp.asarray(wigner_scales())[:, None]
    samples = jnp.clip(jax.random.normal(key, (ROT, EDGES), jnp.float32), -4.0, 4.0)
    return (samples * scales).astype(jnp.bfloat16)


def draw_edge_count(key, part):
    key = jax.random.fold_in(key, 5)
    key_counts, key_full = jax.random.split(key)
    counts = jax.random.randint(key_counts, (BRICKS,), EDGE_CAP // 3, EDGE_CAP // 2 + 1, jnp.int32)
    fullest = jax.random.randint(key_full, (), 0, BRICKS, jnp.int32)
    return jnp.where(jnp.arange(BRICKS, dtype=jnp.int32) == fullest, EDGE_CAP, counts).astype(jnp.int32)


def set_ends(result, key, low, largest):
    spot = [jax.random.randint(jax.random.fold_in(key, axis), (), 0, length) for axis, length in enumerate(result.shape)]
    longest = result.shape.index(max(result.shape))
    neighbour = spot[:longest] + [(spot[longest] + 1) % result.shape[longest]] + spot[longest + 1:]
    return result.at[tuple(spot)].set(low).at[tuple(neighbour)].set(largest)


def block_scale(stream_key, extent, shards, low, top_value):
    def one(dim, blocks):
        steps = jax.random.uniform(jax.random.fold_in(jax.random.fold_in(stream_key, 6), dim), (blocks,), jnp.float32, low / len(shards), top_value / len(shards))
        return jnp.repeat(jnp.exp(steps), extent[dim] // blocks).reshape((-1,) + (1,) * (len(extent) - dim - 1))

    gain = one(*shards[0])
    for cut in shards[1:]:
        gain = gain * one(*cut)
    return gain


def normal_values(rng, shape, width, limit, cuts=(), held_as=jnp.bfloat16):
    entries = width * jax.random.normal(rng, shape, jnp.float32)
    if cuts:
        entries = entries * block_scale(rng, shape, cuts, -0.22, 0.18)
    return jnp.clip(entries, -limit, limit).astype(held_as)


def setup_inputs(seed: int = 0) -> dict:
    seeds = jax.random.split(jax.random.key(seed), 11)
    return {
        "node_x": normal_values(seeds[0], (COEF, C, ATOMS), 1.0, 6.0, ((1, 16), (2, 32))),
        "cotangent": normal_values(seeds[1], (COEF, C, ATOMS), 1.0, 6.0, ((1, 16), (2, 32))),
        "wigner": draw_wigner(jax.random.fold_in(seeds[10], 71), 0),
        "src_index": set_ends(jax.random.randint(seeds[3], (EDGES,), 0, A_DEV + 2 * RIM), jax.random.fold_in(seeds[3], 1), 0, (A_DEV + 2 * RIM) - 1).astype(jnp.int32),
        "dst_index": set_ends(jax.random.randint(seeds[4], (EDGES,), 0, A_DEV), jax.random.fold_in(seeds[4], 1), 0, A_DEV - 1).astype(jnp.int32),
        "edge_scale": jnp.clip(0.1 + 0.9 * jax.random.uniform(seeds[5], (EDGES,), jnp.float32) ** block_scale(seeds[5], (EDGES,), ((0, 32),), -0.2, 0.2), 0.1, 1.0),
        "edge_count": draw_edge_count(jax.random.fold_in(seeds[10], 71), 0),
        "w_zero": normal_values(seeds[7], (L0, C, L0, C), (L0 * C) ** -0.5, 0.1875, ((1, 16),)),
        "w_one": normal_values(seeds[8], (2, L1, C, L1, C), (2 * L1 * C) ** -0.5, 0.15625, ((2, 16),)),
        "w_two": normal_values(seeds[9], (2, L2, C, L2, C), (2 * L2 * C) ** -0.5, 0.15625, ((2, 16),)),
    }


def kept_row(degree, azimuth):
    if azimuth == 0:
        return degree
    if azimuth == 1:
        return 6 + degree
    if azimuth == -1:
        return 12 + degree
    if azimuth == 2:
        return 17 + degree
    return 22 + degree


def to_edge_frame(values, wigner):
    kept_rows = [None] * 29
    offset = 0
    for degree in range(7):
        max_order = min(degree, 2)
        span_cols = 2 * degree + 1
        for azimuth in range(-max_order, max_order + 1):
            running = jnp.zeros(values.shape[1:], jnp.float32)
            for column in range(span_cols):
                factor = wigner[offset + (azimuth + max_order) * span_cols + column].astype(jnp.float32)
                running = running + factor[None, :] * values[degree * degree + column].astype(jnp.float32)
            kept_rows[kept_row(degree, azimuth)] = running
        offset += (2 * max_order + 1) * span_cols
    return jnp.stack(kept_rows)


def from_edge_frame(kept_rows, wigner):
    full_rows = []
    offset = 0
    for degree in range(7):
        max_order = min(degree, 2)
        span_cols = 2 * degree + 1
        for column in range(span_cols):
            running = jnp.zeros(kept_rows.shape[1:], jnp.float32)
            for azimuth in range(-max_order, max_order + 1):
                factor = wigner[offset + (azimuth + max_order) * span_cols + column].astype(jnp.float32)
                running = running + factor[None, :] * kept_rows[kept_row(degree, azimuth)]
            full_rows.append(running)
        offset += (2 * max_order + 1) * span_cols
    return jnp.stack(full_rows)


def contract(weights, grads):
    return lax.dot_general(weights.astype(jnp.float32), grads.astype(jnp.float32),
                           (((2, 3), (0, 1)), ((), ())), precision=lax.Precision.HIGHEST)


def outer(inputs, grads):
    return lax.dot_general(inputs.astype(jnp.float32), grads.astype(jnp.float32),
                           (((2,), (2,)), ((), ())), precision=lax.Precision.HIGHEST)


def so2_back(w_zero, w_one, w_two, edge_grad, edge_in):
    back_rows = [contract(w_zero, edge_grad[0:7])]
    term_zero = outer(edge_in[0:7], edge_grad[0:7])
    weight_terms = []
    for weights, bottom, middle, ceiling in ((w_one, 7, 13, 19), (w_two, 19, 24, 29)):
        grad_plus = edge_grad[bottom:middle]
        grad_minus = edge_grad[middle:ceiling]
        in_plus = edge_in[bottom:middle]
        in_minus = edge_in[middle:ceiling]
        back_rows.append(contract(weights[0], grad_plus) + contract(weights[1], grad_minus))
        back_rows.append(contract(weights[0], grad_minus) - contract(weights[1], grad_plus))
        weight_terms.append(jnp.stack([outer(in_plus, grad_plus) + outer(in_minus, grad_minus),
                                       outer(in_plus, grad_minus) - outer(in_minus, grad_plus)]))
    return jnp.concatenate(back_rows, axis=0), term_zero, weight_terms[0], weight_terms[1]


def reference(node_x, cotangent, wigner, src_index, dst_index, edge_scale, edge_count, w_zero, w_one, w_two):
    rim_len = A_DEV // 4
    position = lax.iota(jnp.int32, EDGE_CAP)

    def brick_step(folded, brick_idx):
        grad_x, sum_zero, sum_one, sum_two = folded
        first_slot = (brick_idx * EDGE_CAP).astype(jnp.int32)
        src_here = lax.dynamic_slice_in_dim(src_index, first_slot, EDGE_CAP)
        dst_here = lax.dynamic_slice_in_dim(dst_index, first_slot, EDGE_CAP)
        scale_here = lax.dynamic_slice_in_dim(edge_scale, first_slot, EDGE_CAP)
        wig_here = lax.dynamic_slice_in_dim(wigner, first_slot, EDGE_CAP, 1)
        count_here = lax.dynamic_slice_in_dim(edge_count, brick_idx, 1)[0]
        base_atom = brick_idx * A_DEV
        src_atom = ((base_atom + src_here - rim_len + ATOMS) % ATOMS).astype(jnp.int32)
        dst_atom = (base_atom + dst_here).astype(jnp.int32)
        factor = jnp.where(position < count_here, 0.25 * scale_here, 0.0)
        edge_grad = (to_edge_frame(jnp.take(cotangent, dst_atom, axis=2), wig_here) * factor).astype(jnp.bfloat16)
        edge_in = to_edge_frame(jnp.take(node_x, src_atom, axis=2), wig_here).astype(jnp.bfloat16)
        back_rows, term_zero, term_one, term_two = so2_back(w_zero, w_one, w_two, edge_grad, edge_in)
        full_rows = from_edge_frame(back_rows, wig_here)
        grad_x = grad_x.at[:, :, src_atom].add(full_rows)
        return (grad_x, sum_zero + term_zero, sum_one + term_one, sum_two + term_two), None

    initial = (jnp.zeros((COEF, C, ATOMS), jnp.float32),
               jnp.zeros((L0, C, L0, C), jnp.float32),
               jnp.zeros((2, L1, C, L1, C), jnp.float32),
               jnp.zeros((2, L2, C, L2, C), jnp.float32))
    folded, ignored = lax.scan(brick_step, initial, jnp.arange(BRICKS, dtype=jnp.int32))
    return folded[0], folded[1], folded[2], folded[3]
```

```python
import functools

import jax
import jax.numpy as jnp
from jax import lax
from jax.experimental import pallas as pl
from jax.experimental.pallas import tpu as pltpu
from jax.sharding import PartitionSpec as P

BF = jnp.bfloat16
F32 = jnp.float32
EB = 256
LANES = 128
VMEM_LIMIT = 48 * 1024 * 1024
ZORD = (0, 2, 4, 6, 1, 3, 5)

NN = (((1,), (0,)), ((), ()))
NT = (((1,), (1,)), ((), ()))


def mm(a, b, dims=NN):
    return lax.dot_general(a, b, dims, preferred_element_type=F32)


def kept_row(degree, azimuth):
    if azimuth == 0:
        return degree
    if azimuth == 1:
        return 6 + degree
    if azimuth == -1:
        return 12 + degree
    if azimuth == 2:
        return 17 + degree
    return 22 + degree


def wig_row(degree, azimuth, column):
    start = sum((2 * min(k, 2) + 1) * (2 * k + 1) for k in range(degree))
    return start + (azimuth + min(degree, 2)) * (2 * degree + 1) + column


def orders(degree):
    reach = min(degree, 2)
    return range(-reach, reach + 1)


def eg_place(row):
    return ZORD.index(row) if row < 7 else row


def x_place(row):
    if row < 7:
        return row * 8
    if row < 13:
        return 64 + (row - 7) * 8
    if row < 19:
        return 112 + (row - 13) * 8
    if row < 24:
        return 160 + (row - 19) * 8
    return 208 + (row - 24) * 8


def iota(shape, axis):
    return lax.broadcasted_iota(jnp.int32, shape, axis)


def hot(match):
    return jnp.where(match, 1.0, 0.0).astype(BF)


def source_hots(src):
    width = src.shape[1]
    atom = iota((LANES, width), 0)
    own = hot(atom == src - 32)
    before = [hot(atom == jnp.where(src < 32, src + 32 * q, -1)) for q in range(4)]
    after = [hot(atom == jnp.where(src >= 160, src - 160 + 32 * q, -1)) for q in range(4)]
    return own, before, after


def pack_kernel(h_ref, node_ref, a_ref, b_ref):
    h = h_ref[0]
    base_a = jnp.where(h == 0, 96, 0)
    base_b = 96 - base_a
    node = node_ref[...]
    atom, lane = iota((LANES, LANES), 0), iota((LANES, LANES), 1)
    parts = []
    for q in range(4):
        inside = (lane >= 32 * q) & (lane < 32 * q + 32)
        pick_a = hot(inside & (atom == lane - 32 * q + base_a))
        pick_b = hot(inside & (atom == lane - 32 * q + base_b))
        parts.append(mm(node, jnp.concatenate([pick_a, pick_b], axis=1)))
    rows = []
    for g in range(14):
        total = jnp.zeros((8, 2 * LANES), F32)
        for q in range(4):
            coef = 4 * g + q
            if coef < 49:
                total = total + parts[q][coef * 8 : coef * 8 + 8]
        rows.append(total)
    packed = jnp.concatenate(rows, axis=0).astype(BF)
    a_ref[...] = packed[:, :LANES]
    b_ref[...] = packed[:, LANES:]


def edge_in_kernel(h_ref, node_ref, ra_ref, rb_ref, src_ref, wig_ref, x_ref, rot, gathered):
    h = h_ref[0]
    src = src_ref[...]
    own, before, after = source_hots(src)
    gathered[...] = mm(node_ref[...], own)
    rot[...] = wig_ref[...].astype(F32)
    first, second = ra_ref[...], rb_ref[...]
    from_before = jnp.where(h == 0, second, first)
    from_after = jnp.where(h == 0, first, second)
    for q in range(4):
        part = mm(from_before, before[q]) + mm(from_after, after[q])
        for g in range(13):
            coef = 4 * g + q
            if coef < 49:
                gathered[coef * 8 : coef * 8 + 8, :] += part[g * 8 : g * 8 + 8]
    rows = {}
    for degree in range(7):
        span = 2 * degree + 1
        vals = [gathered[(degree * degree + j) * 8 : (degree * degree + j + 1) * 8, :] for j in range(span)]
        for m in orders(degree):
            total = None
            for j in range(span):
                at = wig_row(degree, m, j)
                term = rot[at : at + 1, :] * vals[j]
                total = term if total is None else total + term
            rows[kept_row(degree, m)] = total
    blank = jnp.zeros((8, EB), F32)
    groups = [
        (0, [rows[r] for r in range(7)] + [blank]),
        (64, [rows[r] for r in range(7, 13)]),
        (112, [rows[r] for r in range(13, 19)]),
        (160, [rows[r] for r in range(19, 24)] + [blank]),
        (208, [rows[r] for r in range(24, 29)] + [blank]),
    ]
    for start, members in groups:
        x_ref[start : start + 8 * len(members), :] = jnp.concatenate(members, axis=0).astype(BF)


def weight_kernel(k_ref, own_ref, sib_ref, zero_ref, one_ref, two_ref):
    k = k_ref[0]
    chan, lane = iota((LANES, LANES), 0), iota((LANES, LANES), 1)

    def pick(offset):
        spot = lane - offset
        wanted = (spot // 8) * 16 + k * 8 + spot % 8
        return hot((spot >= 0) & (spot < 64) & (chan == wanted))

    low, high = pick(0), pick(64)
    own, sib = own_ref[...], sib_ref[...]
    sides = [(mm(own, low), mm(own, high)), (mm(sib, low), mm(sib, high))]

    def tile(entries, place):
        halves = []
        for side in sides:
            total = None
            for half, entry in enumerate(entries):
                if entry is None:
                    continue
                sign, at = entry
                piece = side[half][at * 8 : at * 8 + 8]
                piece = piece if sign > 0 else -piece
                total = piece if total is None else total + piece
            halves.append(total)
        return jnp.concatenate(halves, axis=0).astype(BF)

    for lp in range(7):
        for p in range(4):
            entries = [
                (1, lp * 7 + ZORD[n]) if n < 7 else None for n in (2 * p, 2 * p + 1)
            ]
            zero_ref[lp * 16 : lp * 16 + 16, p * 128 : p * 128 + 128] = tile(entries, p)
    for ref, count, base in ((one_ref, 6, 49), (two_ref, 5, 121)):
        for out in range(2):
            for lp in range(count):
                for p in range(count):
                    entries = []
                    for n in (2 * p, 2 * p + 1):
                        inp, l = n // count, n % count
                        which = 0 if inp == out else 1
                        sign = -1 if (out == 1 and inp == 0) else 1
                        entries.append((sign, base + which * count * count + lp * count + l))
                    row = (out * count + lp) * 16
                    ref[row : row + 16, p * 128 : p * 128 + 128] = tile(entries, p)


def grad_kernel(
    z_ref, count_ref, blk0, blk1, blk2, blk3, blk4, blk5, blk6, blk7,
    dst_ref, scale_ref, wig_ref, xo_ref, xs_ref,
    eg_ref, so_ref, ss_ref,
    vals, gathered, rot, acc, sem,
):
    step = pl.program_id(0)
    blocks = (blk0, blk1, blk2, blk3, blk4, blk5, blk6, blk7)

    @pl.when(step == 0)
    def _():
        z = z_ref[0]
        copies = [
            pltpu.make_async_copy(blk, vals.at[z ^ j], sem.at[j]) for j, blk in enumerate(blocks)
        ]
        for copy in copies:
            copy.start()
        acc[...] = jnp.zeros_like(acc)
        for copy in copies:
            copy.wait()

    slot = step * EB + iota((1, EB), 1)
    factor = jnp.where(slot < count_ref[0], 0.25 * scale_ref[...], 0.0)
    rot[...] = wig_ref[...].astype(F32) * factor
    dest = hot(iota((LANES, EB), 0) == dst_ref[...])

    def pair(zp, carry):
        for side in range(2):
            gathered[side] = mm(vals[2 * zp + side], dest)
        for half in range(EB // LANES):
            lanes = slice(half * LANES, half * LANES + LANES)
            for degree in range(7):
                span = 2 * degree + 1
                at0 = degree * degree
                cols = [
                    [gathered[side, (at0 + j) * 8 : (at0 + j + 1) * 8, lanes] for j in range(span)]
                    for side in range(2)
                ]
                for m in orders(degree):
                    totals = [None, None]
                    for j in range(span):
                        at = wig_row(degree, m, j)
                        coeff = jnp.broadcast_to(rot[at : at + 1, lanes], (8, LANES))
                        for side in range(2):
                            term = coeff * cols[side][j]
                            totals[side] = term if totals[side] is None else totals[side] + term
                    place = eg_place(kept_row(degree, m)) * 64
                    rows = pl.ds(pl.multiple_of(place + zp * 16, 16), 16)
                    eg_ref[rows, lanes] = jnp.concatenate(totals, axis=0).astype(BF)
        return carry

    lax.fori_loop(0, 4, pair, 0)

    def stacked(*pieces):
        return jnp.concatenate(pieces, axis=0)

    def blank(rows):
        return jnp.zeros((rows, EB), BF)

    xo, xs = xo_ref[...], xs_ref[...]
    even = stacked(xo[:64], blank(64), xs[:64], blank(64))
    odd = stacked(blank(64), xo[:64], blank(64), xs[:64])
    acc[0:256] += mm(eg_ref[0:256], even, NT)
    acc[256:448] += mm(eg_ref[256:448], odd, NT)
    for start, count, plus, minus in ((448, 6, 64, 112), (1216, 5, 160, 208)):
        ahead = stacked(
            xo[plus : plus + 48], -xo[minus : minus + 48], blank(32),
            xs[plus : plus + 48], -xs[minus : minus + 48], blank(32),
        )
        cross = stacked(
            xo[minus : minus + 48], xo[plus : plus + 48], blank(32),
            xs[minus : minus + 48], xs[plus : plus + 48], blank(32),
        )
        size = count * 64
        at = 448 if count == 6 else 832
        acc[at : at + size] += mm(eg_ref[start : start + size], ahead, NT) + mm(
            eg_ref[start + size : start + 2 * size], cross, NT
        )

    @pl.when(step == pl.num_programs(0) - 1)
    def _():
        for zb in range(8):
            tiles = []
            for t in range(4):
                tile = acc[t * 64 + zb * 8 : t * 64 + zb * 8 + 8]
                if t < 3:
                    tile = tile + acc[256 + t * 64 + zb * 8 : 256 + t * 64 + zb * 8 + 8]
                tiles.append(tile)
            for n in range(11):
                tiles.append(acc[448 + n * 64 + zb * 8 : 448 + n * 64 + zb * 8 + 8])
            tiles.append(jnp.zeros((8, 2 * LANES), F32))
            whole = jnp.concatenate(tiles, axis=0).astype(BF)
            so_ref[zb] = whole[:, :LANES]
            ss_ref[zb] = whole[:, LANES:]


def back_kernel(
    eg_ref, zero_ref, one_ref, two_ref, src_ref, wig_ref, own_ref, sib_ref, rot, back, full, acc, rims
):
    step = pl.program_id(0)

    @pl.when(step == 0)
    def _():
        acc[...] = jnp.zeros_like(acc)
        rims[...] = jnp.zeros_like(rims)

    rot[...] = wig_ref[...].astype(F32)
    back[0:112] = mm(zero_ref[:, 0:448], eg_ref[0:448])
    back[112:304] = mm(one_ref[...], eg_ref[448:1216])
    back[304:464] = mm(two_ref[...], eg_ref[1216:1856])
    quarter_start = (0, 13, 25, 37)
    for half in range(EB // LANES):
        lanes = slice(half * LANES, half * LANES + LANES)
        for degree in range(7):
            vals = {m: back[kept_row(degree, m) * 16 : kept_row(degree, m) * 16 + 16, lanes] for m in orders(degree)}
            for j in range(2 * degree + 1):
                total = None
                for m in orders(degree):
                    at = wig_row(degree, m, j)
                    term = rot[at : at + 1, lanes] * vals[m]
                    total = term if total is None else total + term
                coef = degree * degree + j
                row = (quarter_start[coef % 4] + coef // 4) * 16
                full[row : row + 16, lanes] = total.astype(BF)
    own, before, after = source_hots(src_ref[...])
    for q in range(4):
        start, size = quarter_start[q] * 16, (13 if q == 0 else 12) * 16
        rows = full[start : start + size]
        acc[start : start + size] += mm(rows, own, NT)
        rims[0:size] += mm(rows, jnp.concatenate([before[q], after[q]], axis=0), NT)

    @pl.when(step == pl.num_programs(0) - 1)
    def _():
        for side, ref, kind in ((0, own_ref, F32), (1, sib_ref, BF)):
            tiles = []
            for coef in range(49):
                row = (quarter_start[coef % 4] + coef // 4) * 16 + side * 8
                tiles.append(acc[row : row + 8])
            tiles.append(jnp.zeros((8, LANES), F32))
            for rim in range(2):
                for g in range(13):
                    tiles.append(rims[g * 16 + side * 8 : g * 16 + side * 8 + 8, rim * LANES : rim * LANES + LANES])
                tiles.append(jnp.zeros((8, LANES), F32))
            ref[...] = jnp.concatenate(tiles, axis=0).astype(kind)


def join_kernel(h_ref, own_ref, ra_ref, rb_ref, out_ref):
    h = h_ref[0]
    base_a = jnp.where(h == 0, 96, 0)
    base_b = 96 - base_a
    lane, atom = iota((LANES, LANES), 0), iota((LANES, LANES), 1)
    ra, rb = ra_ref[...], rb_ref[...]
    for q in range(4):
        inside = (lane >= 32 * q) & (lane < 32 * q + 32)
        put_a = hot(inside & (atom == lane - 32 * q + base_a))
        put_b = hot(inside & (atom == lane - 32 * q + base_b))
        part = mm(ra, put_a) + mm(rb, put_b)
        for g in range(13):
            coef = 4 * g + q
            if coef < 49:
                out_ref[coef] = own_ref[coef * 8 : coef * 8 + 8] + part[g * 8 : g * 8 + 8]


def smem():
    return pl.BlockSpec(memory_space=pltpu.SMEM)


def params():
    return pltpu.CompilerParams(vmem_limit_bytes=VMEM_LIMIT)


def whole(shape):
    return pl.BlockSpec(shape, lambda *_: (0,) * len(shape))


def sds(shape, dtype):
    return jax.ShapeDtypeStruct(shape, dtype)


def body(
    node_x, cotangent, wigner, src_index, dst_index, edge_scale, edge_count, w_zero, w_one, w_two
):
    chan = lax.axis_index("chan")
    brick = lax.axis_index("brick")
    z, core = chan // 2, chan % 2
    high = brick % 2
    z_s = z.astype(jnp.int32).reshape(1)
    k_s = core.astype(jnp.int32).reshape(1)
    h_s = high.astype(jnp.int32).reshape(1)
    slots = src_index.shape[0]
    steps = slots // EB
    src = src_index.reshape(1, slots)
    dst = dst_index.reshape(1, slots)
    scale = edge_scale.reshape(1, slots)

    def across(x, mask):
        return lax.ppermute(x, "chan", [(i, i ^ mask) for i in range(16)])

    def swap_a(x):
        return lax.ppermute(x, "brick", [(i, i ^ 1) for i in range(32)])

    def swap_b(x):
        route = [(i, (i - 1) % 32 if i % 2 == 0 else (i + 1) % 32) for i in range(32)]
        return lax.ppermute(x, "brick", route)

    def padded(x):
        return jnp.pad(x.reshape(392, 128), ((0, 8), (0, 0)))

    b0 = padded(cotangent)
    b4 = across(b0, 8)
    b2 = across(b0, 4)
    b1 = across(b0, 2)
    b6 = across(b4, 4)
    b5 = across(b4, 2)
    b3 = across(b2, 2)
    b7 = across(b6, 2)

    node = padded(node_x)
    send_a, send_b = pl.pallas_call(
        pack_kernel,
        out_shape=(sds((112, 128), BF), sds((112, 128), BF)),
        in_specs=[smem(), whole((400, 128))],
        out_specs=(whole((112, 128)), whole((112, 128))),
        grid=(1,),
        compiler_params=params(),
        name="pack_rims",
    )(h_s, node)
    got_a, got_b = swap_a(send_a), swap_b(send_b)
    row_spec = pl.BlockSpec((1, EB), lambda i: (0, i))
    wig_spec = pl.BlockSpec((235, EB), lambda i: (0, i))
    x_spec = pl.BlockSpec((256, EB), lambda i: (0, i))
    x_own = pl.pallas_call(
        edge_in_kernel,
        out_shape=sds((256, slots), BF),
        grid=(steps,),
        in_specs=[smem(), whole((400, 128)), whole((112, 128)), whole((112, 128)), row_spec, wig_spec],
        out_specs=x_spec,
        scratch_shapes=[pltpu.VMEM((235, EB), F32), pltpu.VMEM((400, EB), F32)],
        compiler_params=params(),
        name="edge_in",
    )(h_s, node, got_a, got_b, src, wigner)
    x_sib = across(x_own, 1)

    w_own = jnp.concatenate(
        [
            w_zero.transpose(0, 2, 1, 3).reshape(392, 128),
            w_one.transpose(0, 1, 3, 2, 4).reshape(576, 128),
            w_two.transpose(0, 1, 3, 2, 4).reshape(400, 128),
            jnp.zeros((8, 128), BF),
        ],
        axis=0,
    )
    w_sib = across(w_own, 1)
    wz, wo, wt = pl.pallas_call(
        weight_kernel,
        out_shape=(sds((112, 512), BF), sds((192, 768), BF), sds((160, 640), BF)),
        grid=(1,),
        in_specs=[smem(), whole((1376, 128)), whole((1376, 128))],
        out_specs=(whole((112, 512)), whole((192, 768)), whole((160, 640))),
        compiler_params=params(),
        name="weights",
    )(k_s, w_own, w_sib)

    any_spec = pl.BlockSpec(memory_space=pl.ANY)
    eg_spec = pl.BlockSpec((1856, EB), lambda i: (0, i))
    eg, s_own, s_sib = pl.pallas_call(
        grad_kernel,
        out_shape=(sds((1856, slots), BF), sds((8, 128, 128), BF), sds((8, 128, 128), BF)),
        grid=(steps,),
        in_specs=[smem(), smem()] + [any_spec] * 8 + [row_spec, row_spec, wig_spec, x_spec, x_spec],
        out_specs=(eg_spec, whole((8, 128, 128)), whole((8, 128, 128))),
        scratch_shapes=[
            pltpu.VMEM((8, 400, 128), BF),
            pltpu.VMEM((2, 400, EB), F32),
            pltpu.VMEM((235, EB), F32),
            pltpu.VMEM((1152, 256), F32),
            pltpu.SemaphoreType.DMA((8,)),
        ],
        compiler_params=params(),
        name="edge_grad",
    )(z_s, edge_count, b0, b1, b2, b3, b4, b5, b6, b7, dst, scale, wigner, x_own, x_sib)

    s_got = across(s_sib, 1)
    is_even = core == 0
    send = jnp.stack(
        [jnp.where(is_even, s_own, s_got), jnp.where(is_even, s_got, s_own)], axis=1
    ).reshape(16, 128, 128)
    groups = [[2 * j + h for j in range(16)] for h in range(2)]
    pieces = lax.all_to_all(send, "brick", 0, 0, axis_index_groups=groups)
    summed = pieces.astype(F32).sum(axis=0).reshape(16, 2, 4, 128)
    mine = jnp.where(high == 0, summed[:, 0], summed[:, 1])
    other = jnp.where(high == 0, summed[:, 1], summed[:, 0])
    final = mine + swap_a(other.astype(BF).reshape(64, 128)).astype(F32).reshape(16, 4, 128)

    zero_rows = [None] * 7
    for n, degree in enumerate(ZORD):
        zero_rows[degree] = final[n, :, 0:56] if n < 4 else final[n - 4, :, 64:120]
    grad_zero = jnp.stack(zero_rows).reshape(7, 4, 7, 8).transpose(2, 3, 0, 1)
    grad_one = final[4:10, :, 0:96].reshape(6, 4, 2, 6, 8).transpose(2, 3, 4, 0, 1)
    two = jnp.stack([final[10:15, :, 0:40], final[10:15, :, 48:88]], axis=2)
    grad_two = two.reshape(5, 4, 2, 5, 8).transpose(2, 3, 4, 0, 1)

    g_own, g_sib = pl.pallas_call(
        back_kernel,
        out_shape=(sds((624, 128), F32), sds((624, 128), BF)),
        grid=(steps,),
        in_specs=[eg_spec, whole((112, 512)), whole((192, 768)), whole((160, 640)), row_spec, wig_spec],
        out_specs=(whole((624, 128)), whole((624, 128))),
        scratch_shapes=[
            pltpu.VMEM((235, EB), F32),
            pltpu.VMEM((464, EB), F32),
            pltpu.VMEM((784, EB), BF),
            pltpu.VMEM((784, LANES), F32),
            pltpu.VMEM((208, 2 * LANES), F32),
        ],
        compiler_params=params(),
        name="back",
    )(eg, wz, wo, wt, src, wigner)
    g_all = g_own + across(g_sib, 1).astype(F32)
    left, right = g_all[400:512].astype(BF), g_all[512:624].astype(BF)
    rim_a = swap_a(jnp.where(high == 0, right, left))
    rim_b = swap_b(jnp.where(high == 0, left, right))
    grad_x = pl.pallas_call(
        join_kernel,
        out_shape=sds((49, 8, 128), F32),
        grid=(1,),
        in_specs=[smem(), whole((400, 128)), whole((112, 128)), whole((112, 128))],
        out_specs=whole((49, 8, 128)),
        compiler_params=params(),
        name="join",
    )(h_s, g_all[:400], rim_a, rim_b)
    return grad_x, grad_zero, grad_one, grad_two


def solution(mesh):
    in_specs = (
        P(None, "chan", "brick"),
        P(None, "chan", "brick"),
        P(None, "brick"),
        P("brick"),
        P("brick"),
        P("brick"),
        P("brick"),
        P(None, "chan", None, None),
        P(None, None, "chan", None, None),
        P(None, None, "chan", None, None),
    )
    out_specs = (
        P(None, "chan", "brick"),
        P(None, "chan", None, "brick"),
        P(None, None, "chan", None, "brick"),
        P(None, None, "chan", None, "brick"),
    )
    return jax.shard_map(body, mesh=mesh, in_specs=in_specs, out_specs=out_specs, check_vma=False)
```

```python
import functools

import jax
import jax.numpy as jnp
from jax import lax
from jax.experimental import pallas as pl
from jax.experimental.pallas import tpu as pltpu
from jax.sharding import PartitionSpec as P

BF = jnp.bfloat16
F32 = jnp.float32
EB = 256
LANES = 128
VMEM_LIMIT = 60 * 1024 * 1024
ZORD = (0, 2, 4, 6, 1, 3, 5)

NN = (((1,), (0,)), ((), ()))
NT = (((1,), (1,)), ((), ()))


def mm(a, b, dims=NN):
    return lax.dot_general(a, b, dims, preferred_element_type=F32)


def kept_row(degree, azimuth):
    if azimuth == 0:
        return degree
    if azimuth == 1:
        return 6 + degree
    if azimuth == -1:
        return 12 + degree
    if azimuth == 2:
        return 17 + degree
    return 22 + degree


def wig_row(degree, azimuth, column):
    start = sum((2 * min(k, 2) + 1) * (2 * k + 1) for k in range(degree))
    return start + (azimuth + min(degree, 2)) * (2 * degree + 1) + column


def orders(degree):
    reach = min(degree, 2)
    return range(-reach, reach + 1)


def eg_place(row):
    return ZORD.index(row) if row < 7 else row


def x_place(row):
    if row < 7:
        return row * 8
    if row < 13:
        return 64 + (row - 7) * 8
    if row < 19:
        return 112 + (row - 13) * 8
    if row < 24:
        return 160 + (row - 19) * 8
    return 208 + (row - 24) * 8


def iota(shape, axis):
    return lax.broadcasted_iota(jnp.int32, shape, axis)


def hot(match):
    return jnp.where(match, 1.0, 0.0).astype(BF)


def source_hots(src):
    width = src.shape[1]
    atom = iota((LANES, width), 0)
    own = hot(atom == src - 32)
    before = [hot(atom == jnp.where(src < 32, src + 32 * q, -1)) for q in range(4)]
    after = [hot(atom == jnp.where(src >= 160, src - 160 + 32 * q, -1)) for q in range(4)]
    return own, before, after


def pack_kernel(node_ref, cot_ref, node_out, cot_out, rim_out):
    blank = jnp.zeros((8, LANES), F32)

    def rows(ref):
        return jnp.concatenate([ref[...].astype(F32).reshape(392, LANES), blank], axis=0).astype(BF)

    cot_out[...] = rows(cot_ref)
    node = rows(node_ref)
    node_out[...] = node
    atom, lane = iota((LANES, LANES), 0), iota((LANES, LANES), 1)
    parts = []
    for q in range(4):
        inside = (lane >= 32 * q) & (lane < 32 * q + 32)
        last = hot(inside & (atom == lane - 32 * q + 96))
        first = hot(inside & (atom == lane - 32 * q))
        parts.append(mm(node, jnp.concatenate([last, first], axis=1)))
    total = []
    for g in range(13):
        members = [parts[q][(4 * g + q) * 8 : (4 * g + q) * 8 + 8] for q in range(4) if 4 * g + q < 49]
        total.append(sum(members[1:], members[0]))
    total.append(jnp.zeros((8, 2 * LANES), F32))
    packed = jnp.concatenate(total, axis=0).astype(BF)
    rim_out[:112] = packed[:, :LANES]
    rim_out[112:] = packed[:, LANES:]


def edge_in_kernel(h_ref, node_ref, near_ref, far_ref, src_ref, wig_ref, x_ref, rot, gathered):
    h = h_ref[0]
    src = src_ref[...]
    own, before, after = source_hots(src)
    gathered[...] = mm(node_ref[...], own)
    rot[...] = wig_ref[...].astype(F32)
    far = far_ref[...]
    from_before = jnp.where(h == 0, far, near_ref[:112])
    from_after = jnp.where(h == 0, near_ref[112:], far)
    for q in range(4):
        part = mm(from_before, before[q]) + mm(from_after, after[q])
        for g in range(13):
            coef = 4 * g + q
            if coef < 49:
                gathered[coef * 8 : coef * 8 + 8, :] += part[g * 8 : g * 8 + 8]
    rows = {}
    for degree in range(7):
        span = 2 * degree + 1
        vals = [gathered[(degree * degree + j) * 8 : (degree * degree + j + 1) * 8, :] for j in range(span)]
        for m in orders(degree):
            total = None
            for j in range(span):
                at = wig_row(degree, m, j)
                term = rot[at : at + 1, :] * vals[j]
                total = term if total is None else total + term
            rows[kept_row(degree, m)] = total
    blank = jnp.zeros((8, EB), F32)
    groups = [
        (0, [rows[r] for r in range(7)] + [blank]),
        (64, [rows[r] for r in range(7, 13)]),
        (112, [rows[r] for r in range(13, 19)]),
        (160, [rows[r] for r in range(19, 24)] + [blank]),
        (208, [rows[r] for r in range(24, 29)] + [blank]),
    ]
    for start, members in groups:
        x_ref[start : start + 8 * len(members), :] = jnp.concatenate(members, axis=0).astype(BF)


def weight_kernel(k_ref, own_ref, sib_ref, zero_ref, one_ref, two_ref):
    k = k_ref[0]
    chan, lane = iota((LANES, LANES), 0), iota((LANES, LANES), 1)

    def pick(offset):
        spot = lane - offset
        wanted = (spot // 8) * 16 + k * 8 + spot % 8
        return hot((spot >= 0) & (spot < 64) & (chan == wanted))

    low, high = pick(0), pick(64)
    own, sib = own_ref[...], sib_ref[...]
    sides = [(mm(own, low), mm(own, high)), (mm(sib, low), mm(sib, high))]

    def tile(entries, place):
        halves = []
        for side in sides:
            total = None
            for half, entry in enumerate(entries):
                if entry is None:
                    continue
                sign, at = entry
                piece = side[half][at * 8 : at * 8 + 8]
                piece = piece if sign > 0 else -piece
                total = piece if total is None else total + piece
            halves.append(total)
        return jnp.concatenate(halves, axis=0).astype(BF)

    for lp in range(7):
        for p in range(4):
            entries = [
                (1, lp * 7 + ZORD[n]) if n < 7 else None for n in (2 * p, 2 * p + 1)
            ]
            zero_ref[lp * 16 : lp * 16 + 16, p * 128 : p * 128 + 128] = tile(entries, p)
    for ref, count, base in ((one_ref, 6, 49), (two_ref, 5, 121)):
        for out in range(2):
            for lp in range(count):
                for p in range(count):
                    entries = []
                    for n in (2 * p, 2 * p + 1):
                        inp, l = n // count, n % count
                        which = 0 if inp == out else 1
                        sign = -1 if (out == 1 and inp == 0) else 1
                        entries.append((sign, base + which * count * count + lp * count + l))
                    row = (out * count + lp) * 16
                    ref[row : row + 16, p * 128 : p * 128 + 128] = tile(entries, p)


def grad_kernel(
    z_ref, count_ref, blk0, blk1, blk2, blk3, blk4, blk5, blk6, blk7,
    dst_ref, scale_ref, wig_ref, xo_ref, xs_ref,
    eg_ref, so_ref, ss_ref,
    vals, gathered, rot, acc, sem,
):
    step = pl.program_id(0)
    blocks = (blk0, blk1, blk2, blk3, blk4, blk5, blk6, blk7)

    @pl.when(step == 0)
    def _():
        z = z_ref[0]
        copies = [
            pltpu.make_async_copy(blk, vals.at[z ^ j], sem.at[j]) for j, blk in enumerate(blocks)
        ]
        for copy in copies:
            copy.start()
        acc[...] = jnp.zeros_like(acc)
        for copy in copies:
            copy.wait()

    slot = step * EB + iota((1, EB), 1)
    factor = jnp.where(slot < count_ref[0], 0.25 * scale_ref[...], 0.0)
    rot[...] = wig_ref[...].astype(F32) * factor
    dest = hot(iota((LANES, EB), 0) == dst_ref[...])

    def pair(zp, carry):
        for side in range(2):
            gathered[side] = mm(vals[2 * zp + side], dest)
        for half in range(EB // LANES):
            lanes = slice(half * LANES, half * LANES + LANES)
            for degree in range(7):
                span = 2 * degree + 1
                at0 = degree * degree
                cols = [
                    [gathered[side, (at0 + j) * 8 : (at0 + j + 1) * 8, lanes] for j in range(span)]
                    for side in range(2)
                ]
                for m in orders(degree):
                    totals = [None, None]
                    for j in range(span):
                        at = wig_row(degree, m, j)
                        coeff = jnp.broadcast_to(rot[at : at + 1, lanes], (8, LANES))
                        for side in range(2):
                            term = coeff * cols[side][j]
                            totals[side] = term if totals[side] is None else totals[side] + term
                    place = eg_place(kept_row(degree, m)) * 64
                    rows = pl.ds(pl.multiple_of(place + zp * 16, 16), 16)
                    eg_ref[rows, lanes] = jnp.concatenate(totals, axis=0).astype(BF)
        return carry

    lax.fori_loop(0, 4, pair, 0)

    def stacked(*pieces):
        return jnp.concatenate(pieces, axis=0)

    def blank(rows):
        return jnp.zeros((rows, EB), BF)

    xo, xs = xo_ref[...], xs_ref[...]
    even = stacked(xo[:64], blank(64), xs[:64], blank(64))
    odd = stacked(blank(64), xo[:64], blank(64), xs[:64])
    acc[0:256] += mm(eg_ref[0:256], even, NT)
    acc[256:448] += mm(eg_ref[256:448], odd, NT)
    for start, count, plus, minus in ((448, 6, 64, 112), (1216, 5, 160, 208)):
        ahead = stacked(
            xo[plus : plus + 48], -xo[minus : minus + 48], blank(32),
            xs[plus : plus + 48], -xs[minus : minus + 48], blank(32),
        )
        cross = stacked(
            xo[minus : minus + 48], xo[plus : plus + 48], blank(32),
            xs[minus : minus + 48], xs[plus : plus + 48], blank(32),
        )
        size = count * 64
        at = 448 if count == 6 else 832
        acc[at : at + size] += mm(eg_ref[start : start + size], ahead, NT) + mm(
            eg_ref[start + size : start + 2 * size], cross, NT
        )

    @pl.when(step == pl.num_programs(0) - 1)
    def _():
        for zb in range(8):
            tiles = []
            for t in range(4):
                tile = acc[t * 64 + zb * 8 : t * 64 + zb * 8 + 8]
                if t < 3:
                    tile = tile + acc[256 + t * 64 + zb * 8 : 256 + t * 64 + zb * 8 + 8]
                tiles.append(tile)
            for n in range(11):
                tiles.append(acc[448 + n * 64 + zb * 8 : 448 + n * 64 + zb * 8 + 8])
            tiles.append(jnp.zeros((8, 2 * LANES), F32))
            whole = jnp.concatenate(tiles, axis=0).astype(BF)
            so_ref[zb] = whole[:, :LANES]
            ss_ref[zb] = whole[:, LANES:]


def back_kernel(
    eg_ref, zero_ref, one_ref, two_ref, src_ref, wig_ref, own_ref, sib_ref, rot, back, full, acc, rims
):
    step = pl.program_id(0)

    @pl.when(step == 0)
    def _():
        acc[...] = jnp.zeros_like(acc)
        rims[...] = jnp.zeros_like(rims)

    rot[...] = wig_ref[...].astype(F32)
    back[0:112] = mm(zero_ref[:, 0:448], eg_ref[0:448])
    back[112:304] = mm(one_ref[...], eg_ref[448:1216])
    back[304:464] = mm(two_ref[...], eg_ref[1216:1856])
    quarter_start = (0, 13, 25, 37)
    for half in range(EB // LANES):
        lanes = slice(half * LANES, half * LANES + LANES)
        for degree in range(7):
            vals = {m: back[kept_row(degree, m) * 16 : kept_row(degree, m) * 16 + 16, lanes] for m in orders(degree)}
            for j in range(2 * degree + 1):
                total = None
                for m in orders(degree):
                    at = wig_row(degree, m, j)
                    term = rot[at : at + 1, lanes] * vals[m]
                    total = term if total is None else total + term
                coef = degree * degree + j
                row = (quarter_start[coef % 4] + coef // 4) * 16
                full[row : row + 16, lanes] = total.astype(BF)
    own, before, after = source_hots(src_ref[...])
    for q in range(4):
        start, size = quarter_start[q] * 16, (13 if q == 0 else 12) * 16
        rows = full[start : start + size]
        acc[start : start + size] += mm(rows, own, NT)
        rims[0:size] += mm(rows, jnp.concatenate([before[q], after[q]], axis=0), NT)

    @pl.when(step == pl.num_programs(0) - 1)
    def _():
        for side, ref, kind in ((0, own_ref, F32), (1, sib_ref, BF)):
            tiles = []
            for coef in range(49):
                row = (quarter_start[coef % 4] + coef // 4) * 16 + side * 8
                tiles.append(acc[row : row + 8])
            tiles.append(jnp.zeros((8, LANES), F32))
            for rim in range(2):
                for g in range(13):
                    tiles.append(rims[g * 16 + side * 8 : g * 16 + side * 8 + 8, rim * LANES : rim * LANES + LANES])
                tiles.append(jnp.zeros((8, LANES), F32))
            ref[...] = jnp.concatenate(tiles, axis=0).astype(kind)


def join_kernel(h_ref, own_ref, rim_ref, out_ref):
    h = h_ref[0]
    base_a = jnp.where(h == 0, 96, 0)
    base_b = 96 - base_a
    lane, atom = iota((LANES, LANES), 0), iota((LANES, LANES), 1)
    ra, rb = rim_ref[0:112], rim_ref[112:224]
    for q in range(4):
        inside = (lane >= 32 * q) & (lane < 32 * q + 32)
        put_a = hot(inside & (atom == lane - 32 * q + base_a))
        put_b = hot(inside & (atom == lane - 32 * q + base_b))
        part = mm(ra, put_a) + mm(rb, put_b)
        for g in range(13):
            coef = 4 * g + q
            if coef < 49:
                out_ref[coef] = own_ref[coef * 8 : coef * 8 + 8] + part[g * 8 : g * 8 + 8]


def smem():
    return pl.BlockSpec(memory_space=pltpu.SMEM)


def params():
    return pltpu.CompilerParams(vmem_limit_bytes=VMEM_LIMIT)


def light():
    return pl.CostEstimate(flops=1, bytes_accessed=1, transcendentals=0)


def whole(shape):
    return pl.BlockSpec(shape, lambda *_: (0,) * len(shape))


def sds(shape, dtype):
    return jax.ShapeDtypeStruct(shape, dtype)


def body(
    node_x, cotangent, wigner, src_index, dst_index, edge_scale, edge_count, w_zero, w_one, w_two
):
    chan = lax.axis_index("chan")
    brick = lax.axis_index("brick")
    z, core = chan // 2, chan % 2
    high = brick % 2
    z_s = z.astype(jnp.int32).reshape(1)
    k_s = core.astype(jnp.int32).reshape(1)
    h_s = high.astype(jnp.int32).reshape(1)
    slots = src_index.shape[0]
    steps = slots // EB
    src = src_index.reshape(1, slots)
    dst = dst_index.reshape(1, slots)
    scale = edge_scale.reshape(1, slots)

    def across(x, mask):
        return lax.ppermute(x, "chan", [(i, i ^ mask) for i in range(16)])

    def cross(x):
        return lax.ppermute(x, "brick", [(i, i ^ 1) for i in range(32)])

    def shift(x, away):
        route = [(i, (i + (2 if (i % 2 == 0) == away else -2)) % 32) for i in range(32)]
        return lax.ppermute(x, "brick", route)

    node, b0, rims = pl.pallas_call(
        pack_kernel,
        out_shape=(sds((400, 128), BF), sds((400, 128), BF), sds((224, 128), BF)),
        in_specs=[whole((49, 8, 128)), whole((49, 8, 128))],
        out_specs=(whole((400, 128)), whole((400, 128)), whole((224, 128))),
        grid=(1,),
        compiler_params=params(),
        cost_estimate=light(),
        name="pack",
    )(node_x, cotangent)
    near = cross(rims)

    b4 = across(b0, 8)
    b2 = across(b0, 4)
    b1 = across(b0, 2)
    b6 = across(b4, 4)
    b5 = across(b4, 2)
    near, b2, b4 = lax.optimization_barrier((near, b2, b4))
    b3 = across(b2, 2)
    far = shift(lax.dynamic_slice_in_dim(near, 112 * high, 112, 0), True)
    far, b1, b3, b5, b6 = lax.optimization_barrier((far, b1, b3, b5, b6))
    b7 = across(b6, 2)

    row_spec = pl.BlockSpec((1, EB), lambda i: (0, i))
    wig_spec = pl.BlockSpec((235, EB), lambda i: (0, i))
    x_spec = pl.BlockSpec((256, EB), lambda i: (0, i))
    x_own = pl.pallas_call(
        edge_in_kernel,
        out_shape=sds((256, slots), BF),
        grid=(steps,),
        in_specs=[smem(), whole((400, 128)), whole((224, 128)), whole((112, 128)), row_spec, wig_spec],
        out_specs=x_spec,
        scratch_shapes=[pltpu.VMEM((235, EB), F32), pltpu.VMEM((400, EB), F32)],
        compiler_params=params(),
        cost_estimate=light(),
        name="edge_in",
    )(h_s, node, near, far, src, wigner)
    x_sib = across(x_own, 1)

    w_own = jnp.concatenate(
        [
            w_zero.transpose(0, 2, 1, 3).reshape(392, 128),
            w_one.transpose(0, 1, 3, 2, 4).reshape(576, 128),
            w_two.transpose(0, 1, 3, 2, 4).reshape(400, 128),
            jnp.zeros((8, 128), BF),
        ],
        axis=0,
    )
    w_sib = across(w_own, 1)
    wz, wo, wt = pl.pallas_call(
        weight_kernel,
        out_shape=(sds((112, 512), BF), sds((192, 768), BF), sds((160, 640), BF)),
        grid=(1,),
        in_specs=[smem(), whole((1376, 128)), whole((1376, 128))],
        out_specs=(whole((112, 512)), whole((192, 768)), whole((160, 640))),
        compiler_params=params(),
        cost_estimate=light(),
        name="weights",
    )(k_s, w_own, w_sib)

    any_spec = pl.BlockSpec(memory_space=pl.ANY)
    eg_spec = pl.BlockSpec((1856, EB), lambda i: (0, i))
    eg, s_own, s_sib = pl.pallas_call(
        grad_kernel,
        out_shape=(sds((1856, slots), BF), sds((8, 128, 128), BF), sds((8, 128, 128), BF)),
        grid=(steps,),
        in_specs=[smem(), smem()] + [any_spec] * 8 + [row_spec, row_spec, wig_spec, x_spec, x_spec],
        out_specs=(eg_spec, whole((8, 128, 128)), whole((8, 128, 128))),
        scratch_shapes=[
            pltpu.VMEM((8, 400, 128), BF),
            pltpu.VMEM((2, 400, EB), F32),
            pltpu.VMEM((235, EB), F32),
            pltpu.VMEM((1152, 256), F32),
            pltpu.SemaphoreType.DMA((8,)),
        ],
        compiler_params=params(),
        cost_estimate=light(),
        name="edge_grad",
    )(z_s, edge_count, b0, b1, b2, b3, b4, b5, b6, b7, dst, scale, wigner, x_own, x_sib)

    s_got = across(s_sib, 1)
    is_even = core == 0
    send = jnp.concatenate([jnp.where(is_even, s_own, s_got), jnp.where(is_even, s_got, s_own)], axis=0)
    groups = [[2 * (2 * zb + p) + h for p in range(2) for zb in range(8)] for h in range(2)]
    pieces = lax.all_to_all(send, "brick", 0, 0, axis_index_groups=groups)
    summed = pieces.astype(F32).sum(axis=0).reshape(16, 2, 4, 128)
    mine = jnp.where(high == 0, summed[:, 0], summed[:, 1])
    other = jnp.where(high == 0, summed[:, 1], summed[:, 0])

    eg, send = lax.optimization_barrier((eg, send))
    g_own, g_sib = pl.pallas_call(
        back_kernel,
        out_shape=(sds((624, 128), F32), sds((624, 128), BF)),
        grid=(steps,),
        in_specs=[eg_spec, whole((112, 512)), whole((192, 768)), whole((160, 640)), row_spec, wig_spec],
        out_specs=(whole((624, 128)), whole((624, 128))),
        scratch_shapes=[
            pltpu.VMEM((235, EB), F32),
            pltpu.VMEM((464, EB), F32),
            pltpu.VMEM((784, EB), BF),
            pltpu.VMEM((784, LANES), F32),
            pltpu.VMEM((208, 2 * LANES), F32),
        ],
        compiler_params=params(),
        cost_estimate=light(),
        name="back",
    )(eg, wz, wo, wt, src, wigner)
    g_all = g_own + across(g_sib, 1).astype(F32)
    left, right = g_all[400:512].astype(BF), g_all[512:624].astype(BF)
    near_rim = jnp.where(high == 0, right, left)
    far_rim = shift(jnp.where(high == 0, left, right), False)

    crossed = cross(jnp.concatenate([near_rim, far_rim, other.astype(BF).reshape(64, 128)], axis=0))
    final = mine + crossed[224:].astype(F32).reshape(16, 4, 128)
    grad_x = pl.pallas_call(
        join_kernel,
        out_shape=sds((49, 8, 128), F32),
        grid=(1,),
        in_specs=[smem(), whole((400, 128)), whole((288, 128))],
        out_specs=whole((49, 8, 128)),
        compiler_params=params(),
        cost_estimate=light(),
        name="join",
    )(h_s, g_all[:400], crossed)

    zero_rows = [None] * 7
    for n, degree in enumerate(ZORD):
        zero_rows[degree] = final[n, :, 0:56] if n < 4 else final[n - 4, :, 64:120]
    grad_zero = jnp.stack(zero_rows).reshape(7, 4, 7, 8).transpose(2, 3, 0, 1)
    grad_one = final[4:10, :, 0:96].reshape(6, 4, 2, 6, 8).transpose(2, 3, 4, 0, 1)
    two = jnp.stack([final[10:15, :, 0:40], final[10:15, :, 48:88]], axis=2)
    grad_two = two.reshape(5, 4, 2, 5, 8).transpose(2, 3, 4, 0, 1)

    return grad_x, grad_zero, grad_one, grad_two


def solution(mesh):
    in_specs = (
        P(None, "chan", "brick"),
        P(None, "chan", "brick"),
        P(None, "brick"),
        P("brick"),
        P("brick"),
        P("brick"),
        P("brick"),
        P(None, "chan", None, None),
        P(None, None, "chan", None, None),
        P(None, None, "chan", None, None),
    )
    out_specs = (
        P(None, "chan", "brick"),
        P(None, "chan", None, "brick"),
        P(None, None, "chan", None, "brick"),
        P(None, None, "chan", None, "brick"),
    )
    return jax.shard_map(body, mesh=mesh, in_specs=in_specs, out_specs=out_specs, check_vma=False)
```

```python
import functools

import jax
import jax.numpy as jnp
from jax import lax
from jax.experimental import pallas as pl
from jax.experimental.pallas import tpu as pltpu
from jax.sharding import PartitionSpec as P

BF = jnp.bfloat16
F32 = jnp.float32
EB = 256
LANES = 128
VMEM_LIMIT = 28 * 1024 * 1024
EDGE_VMEM = 60 * 1024 * 1024
ZORD = (0, 2, 4, 6, 1, 3, 5)

NN = (((1,), (0,)), ((), ()))
NT = (((1,), (1,)), ((), ()))


def mm(a, b, dims=NN):
    return lax.dot_general(a, b, dims, preferred_element_type=F32)


def kept_row(degree, azimuth):
    if azimuth == 0:
        return degree
    if azimuth == 1:
        return 6 + degree
    if azimuth == -1:
        return 12 + degree
    if azimuth == 2:
        return 17 + degree
    return 22 + degree


def wig_row(degree, azimuth, column):
    start = sum((2 * min(k, 2) + 1) * (2 * k + 1) for k in range(degree))
    return start + (azimuth + min(degree, 2)) * (2 * degree + 1) + column


def orders(degree):
    reach = min(degree, 2)
    return range(-reach, reach + 1)


def eg_place(row):
    return ZORD.index(row) if row < 7 else row


def x_place(row):
    if row < 7:
        return row * 8
    if row < 13:
        return 64 + (row - 7) * 8
    if row < 19:
        return 112 + (row - 13) * 8
    if row < 24:
        return 160 + (row - 19) * 8
    return 208 + (row - 24) * 8


def iota(shape, axis):
    return lax.broadcasted_iota(jnp.int32, shape, axis)


def hot(match):
    return jnp.where(match, 1.0, 0.0).astype(BF)


def source_hots(src):
    width = src.shape[1]
    atom = iota((LANES, width), 0)
    own = hot(atom == src - 32)
    before = [hot(atom == jnp.where(src < 32, src + 32 * q, -1)) for q in range(4)]
    after = [hot(atom == jnp.where(src >= 160, src - 160 + 32 * q, -1)) for q in range(4)]
    return own, before, after


def pack_kernel(node_ref, cot_ref, zero_ref, one_ref, two_ref, node_out, cot_out, rim_out, weight_out):
    blank = jnp.zeros((8, LANES), F32)

    def rows(ref):
        return jnp.concatenate([ref[...].astype(F32).reshape(392, LANES), blank], axis=0).astype(BF)

    cot_out[...] = rows(cot_ref)
    node = rows(node_ref)
    node_out[...] = node
    atom, lane = iota((LANES, LANES), 0), iota((LANES, LANES), 1)
    parts = []
    for q in range(4):
        inside = (lane >= 32 * q) & (lane < 32 * q + 32)
        last = hot(inside & (atom == lane - 32 * q + 96))
        first = hot(inside & (atom == lane - 32 * q))
        parts.append(mm(node, jnp.concatenate([last, first], axis=1)))
    total = []
    for g in range(13):
        members = [parts[q][(4 * g + q) * 8 : (4 * g + q) * 8 + 8] for q in range(4) if 4 * g + q < 49]
        total.append(sum(members[1:], members[0]))
    total.append(jnp.zeros((8, 2 * LANES), F32))
    packed = jnp.concatenate(total, axis=0).astype(BF)
    rim_out[:112] = packed[:, :LANES]
    rim_out[112:] = packed[:, LANES:]
    parts = [ref[...].astype(F32).reshape(-1, LANES) for ref in (zero_ref, one_ref, two_ref)]
    weight_out[...] = jnp.concatenate(parts + [blank], axis=0).astype(BF)


def edge_in_kernel(h_ref, node_ref, near_ref, far_ref, src_ref, wig_ref, x_ref, rot, gathered):
    h = h_ref[0]
    src = src_ref[...]
    own, before, after = source_hots(src)
    gathered[...] = mm(node_ref[...], own)
    rot[...] = wig_ref[...].astype(F32)
    far = far_ref[...]
    from_before = jnp.where(h == 0, far, near_ref[:112])
    from_after = jnp.where(h == 0, near_ref[112:], far)
    for q in range(4):
        part = mm(from_before, before[q]) + mm(from_after, after[q])
        for g in range(13):
            coef = 4 * g + q
            if coef < 49:
                gathered[coef * 8 : coef * 8 + 8, :] += part[g * 8 : g * 8 + 8]
    rows = {}
    for degree in range(7):
        span = 2 * degree + 1
        vals = [gathered[(degree * degree + j) * 8 : (degree * degree + j + 1) * 8, :] for j in range(span)]
        for m in orders(degree):
            total = None
            for j in range(span):
                at = wig_row(degree, m, j)
                term = rot[at : at + 1, :] * vals[j]
                total = term if total is None else total + term
            rows[kept_row(degree, m)] = total
    blank = jnp.zeros((8, EB), F32)
    groups = [
        (0, [rows[r] for r in range(7)] + [blank]),
        (64, [rows[r] for r in range(7, 13)]),
        (112, [rows[r] for r in range(13, 19)]),
        (160, [rows[r] for r in range(19, 24)] + [blank]),
        (208, [rows[r] for r in range(24, 29)] + [blank]),
    ]
    for start, members in groups:
        x_ref[start : start + 8 * len(members), :] = jnp.concatenate(members, axis=0).astype(BF)


def weight_kernel(k_ref, own_ref, sib_ref, zero_ref, one_ref, two_ref):
    k = k_ref[0]
    chan, lane = iota((LANES, LANES), 0), iota((LANES, LANES), 1)

    def pick(offset):
        spot = lane - offset
        wanted = (spot // 8) * 16 + k * 8 + spot % 8
        return hot((spot >= 0) & (spot < 64) & (chan == wanted))

    low, high = pick(0), pick(64)
    own, sib = own_ref[...], sib_ref[...]
    sides = [(mm(own, low), mm(own, high)), (mm(sib, low), mm(sib, high))]

    def tile(entries, place):
        halves = []
        for side in sides:
            total = None
            for half, entry in enumerate(entries):
                if entry is None:
                    continue
                sign, at = entry
                piece = side[half][at * 8 : at * 8 + 8]
                piece = piece if sign > 0 else -piece
                total = piece if total is None else total + piece
            halves.append(total)
        return jnp.concatenate(halves, axis=0).astype(BF)

    for lp in range(7):
        for p in range(4):
            entries = [
                (1, lp * 7 + ZORD[n]) if n < 7 else None for n in (2 * p, 2 * p + 1)
            ]
            zero_ref[lp * 16 : lp * 16 + 16, p * 128 : p * 128 + 128] = tile(entries, p)
    for ref, count, base in ((one_ref, 6, 49), (two_ref, 5, 121)):
        for out in range(2):
            for lp in range(count):
                for p in range(count):
                    entries = []
                    for n in (2 * p, 2 * p + 1):
                        inp, l = n // count, n % count
                        which = 0 if inp == out else 1
                        sign = -1 if (out == 1 and inp == 0) else 1
                        entries.append((sign, base + which * count * count + lp * count + l))
                    row = (out * count + lp) * 16
                    ref[row : row + 16, p * 128 : p * 128 + 128] = tile(entries, p)


def edge_kernel(
    z_ref, count_ref, blk0, blk4, blk26, blk15, blk37,
    dst_ref, src_ref, scale_ref, wig_ref, xo_ref, xs_ref, zero_ref, one_ref, two_ref,
    so_ref, go_ref, sib_ref,
    vals, gathered, rot, plain, eg, acc, back, full, atoms, rims, sem,
):
    step = pl.program_id(0)
    blocks = [(0, blk0), (4, blk4)]
    for n, pair_ref in ((2, blk26), (1, blk15), (3, blk37)):
        blocks += [(n, pair_ref.at[pl.ds(0, 400)]), (n + 4, pair_ref.at[pl.ds(400, 400)])]

    @pl.when(step == 0)
    def _():
        z = z_ref[0]
        copies = [
            pltpu.make_async_copy(blk, vals.at[z ^ j], sem.at[j]) for j, blk in blocks
        ]
        for copy in copies:
            copy.start()
        acc[...] = jnp.zeros_like(acc)
        atoms[...] = jnp.zeros_like(atoms)
        rims[...] = jnp.zeros_like(rims)
        for copy in copies:
            copy.wait()

    slot = step * EB + iota((1, EB), 1)
    factor = jnp.where(slot < count_ref[0], 0.25 * scale_ref[...], 0.0)
    entries = wig_ref[...].astype(F32)
    plain[...] = entries
    rot[...] = entries * factor
    dest = hot(iota((LANES, EB), 0) == dst_ref[...])
    for zp in range(4):
        for side in range(2):
            gathered[zp % 2, side] = mm(vals[2 * zp + side], dest)
        for half in range(EB // LANES):
            lanes = slice(half * LANES, half * LANES + LANES)
            for degree in range(7):
                span = 2 * degree + 1
                at0 = degree * degree
                cols = [
                    [gathered[zp % 2, side, (at0 + j) * 8 : (at0 + j + 1) * 8, lanes] for j in range(span)]
                    for side in range(2)
                ]
                for m in orders(degree):
                    totals = [None, None]
                    for j in range(span):
                        at = wig_row(degree, m, j)
                        coeff = jnp.broadcast_to(rot[at : at + 1, lanes], (8, LANES))
                        for side in range(2):
                            term = coeff * cols[side][j]
                            totals[side] = term if totals[side] is None else totals[side] + term
                    row = eg_place(kept_row(degree, m)) * 64 + zp * 16
                    eg[row : row + 16, lanes] = jnp.concatenate(totals, axis=0).astype(BF)

    def stacked(*pieces):
        return jnp.concatenate(pieces, axis=0)

    def blank(rows):
        return jnp.zeros((rows, EB), BF)

    xo, xs = xo_ref[...], xs_ref[...]
    acc[0:448] += mm(eg[0:448], stacked(xo[:64], blank(64), xs[:64], blank(64)), NT)
    for start, count, plus, minus in ((448, 6, 64, 112), (1216, 5, 160, 208)):
        ahead = stacked(
            xo[plus : plus + 48], -xo[minus : minus + 48], blank(32),
            xs[plus : plus + 48], -xs[minus : minus + 48], blank(32),
        )
        cross = stacked(
            xo[minus : minus + 48], xo[plus : plus + 48], blank(32),
            xs[minus : minus + 48], xs[plus : plus + 48], blank(32),
        )
        size = count * 64
        at = 448 if count == 6 else 832
        acc[at : at + size] += mm(eg[start : start + size], ahead, NT) + mm(
            eg[start + size : start + 2 * size], cross, NT
        )

    back[0:112] = mm(zero_ref[:, 0:448], eg[0:448])
    back[112:304] = mm(one_ref[...], eg[448:1216])
    back[304:464] = mm(two_ref[...], eg[1216:1856])
    quarter_start = (0, 13, 25, 37)
    for half in range(EB // LANES):
        lanes = slice(half * LANES, half * LANES + LANES)
        for degree in range(7):
            vals_m = {
                m: back[kept_row(degree, m) * 16 : kept_row(degree, m) * 16 + 16, lanes]
                for m in orders(degree)
            }
            for j in range(2 * degree + 1):
                total = None
                for m in orders(degree):
                    at = wig_row(degree, m, j)
                    term = plain[at : at + 1, lanes] * vals_m[m]
                    total = term if total is None else total + term
                coef = degree * degree + j
                row = (quarter_start[coef % 4] + coef // 4) * 16
                full[row : row + 16, lanes] = total.astype(BF)
    own, before, after = source_hots(src_ref[...])
    for q in range(4):
        start, size = quarter_start[q] * 16, (13 if q == 0 else 12) * 16
        rows = full[start : start + size]
        atoms[start : start + size] += mm(rows, own, NT)
        rims[0:size] += mm(rows, jnp.concatenate([before[q], after[q]], axis=0), NT)

    @pl.when(step == pl.num_programs(0) - 1)
    def _():
        for zb in range(8):
            tiles = []
            for t in range(4):
                tile = acc[t * 64 + zb * 8 : t * 64 + zb * 8 + 8]
                if t < 3:
                    odd = acc[256 + t * 64 + zb * 8 : 256 + t * 64 + zb * 8 + 8]
                    halves = [pltpu.roll(odd[:, n : n + LANES], 64, 1) for n in (0, LANES)]
                    tile = tile + jnp.concatenate(halves, axis=1)
                tiles.append(tile)
            for n in range(11):
                tiles.append(acc[448 + n * 64 + zb * 8 : 448 + n * 64 + zb * 8 + 8])
            tiles.append(jnp.zeros((8, 2 * LANES), F32))
            whole_tile = jnp.concatenate(tiles, axis=0).astype(BF)
            so_ref[zb * 128 : zb * 128 + 128] = whole_tile[:, :LANES]
            sib_ref[zb * 128 : zb * 128 + 128] = whole_tile[:, LANES:]
        for side in range(2):
            tiles = []
            for coef in range(49):
                row = (quarter_start[coef % 4] + coef // 4) * 16 + side * 8
                tiles.append(atoms[row : row + 8])
            tiles.append(jnp.zeros((8, LANES), F32))
            for rim in range(2):
                for g in range(13):
                    row = g * 16 + side * 8
                    tiles.append(rims[row : row + 8, rim * LANES : rim * LANES + LANES])
                tiles.append(jnp.zeros((8, LANES), F32))
            if side == 0:
                go_ref[...] = jnp.concatenate(tiles, axis=0)
            else:
                sib_ref[1024:1648] = jnp.concatenate(tiles, axis=0).astype(BF)


def edge_call(z_s, edge_count, blocks, dst, src, scale, wigner, x_own, x_sib, weights):
    slots = dst.shape[1]
    any_spec = pl.BlockSpec(memory_space=pl.ANY)
    row_spec = pl.BlockSpec((1, EB), lambda i: (0, i))
    wig_spec = pl.BlockSpec((235, EB), lambda i: (0, i))
    x_spec = pl.BlockSpec((256, EB), lambda i: (0, i))
    return pl.pallas_call(
        edge_kernel,
        out_shape=(sds((1024, 128), BF), sds((624, 128), F32), sds((1648, 128), BF)),
        grid=(slots // EB,),
        in_specs=[smem(), smem()]
        + [any_spec] * 5
        + [row_spec, row_spec, row_spec, wig_spec, x_spec, x_spec]
        + [whole((112, 512)), whole((192, 768)), whole((160, 640))],
        out_specs=(whole((1024, 128)), whole((624, 128)), whole((1648, 128))),
        scratch_shapes=[
            pltpu.VMEM((8, 400, 128), BF),
            pltpu.VMEM((2, 2, 400, EB), F32),
            pltpu.VMEM((235, EB), F32),
            pltpu.VMEM((235, EB), F32),
            pltpu.VMEM((1856, EB), BF),
            pltpu.VMEM((1152, 256), F32),
            pltpu.VMEM((464, EB), F32),
            pltpu.VMEM((784, EB), BF),
            pltpu.VMEM((784, LANES), F32),
            pltpu.VMEM((208, 2 * LANES), F32),
            pltpu.SemaphoreType.DMA((8,)),
        ],
        compiler_params=pltpu.CompilerParams(vmem_limit_bytes=EDGE_VMEM),
        name="edge",
    )(z_s, edge_count, *blocks, dst, src, scale, wigner, x_own, x_sib, *weights)


def join_kernel(h_ref, own_ref, rim_ref, out_ref):
    h = h_ref[0]
    base_a = jnp.where(h == 0, 96, 0)
    base_b = 96 - base_a
    lane, atom = iota((LANES, LANES), 0), iota((LANES, LANES), 1)
    ra, rb = rim_ref[0:112], rim_ref[112:224]
    for q in range(4):
        inside = (lane >= 32 * q) & (lane < 32 * q + 32)
        put_a = hot(inside & (atom == lane - 32 * q + base_a))
        put_b = hot(inside & (atom == lane - 32 * q + base_b))
        part = mm(ra, put_a) + mm(rb, put_b)
        for g in range(13):
            coef = 4 * g + q
            if coef < 49:
                out_ref[coef] = own_ref[coef * 8 : coef * 8 + 8] + part[g * 8 : g * 8 + 8]


def smem():
    return pl.BlockSpec(memory_space=pltpu.SMEM)


def params():
    return pltpu.CompilerParams(vmem_limit_bytes=VMEM_LIMIT)


def light():
    return pl.CostEstimate(flops=1, bytes_accessed=1, transcendentals=0)


def whole(shape):
    return pl.BlockSpec(shape, lambda *_: (0,) * len(shape))


def sds(shape, dtype):
    return jax.ShapeDtypeStruct(shape, dtype)


def body(
    node_x, cotangent, wigner, src_index, dst_index, edge_scale, edge_count, w_zero, w_one, w_two
):
    chan = lax.axis_index("chan")
    brick = lax.axis_index("brick")
    z, core = chan // 2, chan % 2
    high = brick % 2
    z_s = z.astype(jnp.int32).reshape(1)
    k_s = core.astype(jnp.int32).reshape(1)
    h_s = high.astype(jnp.int32).reshape(1)
    slots = src_index.shape[0]
    steps = slots // EB
    src = src_index.reshape(1, slots)
    dst = dst_index.reshape(1, slots)
    scale = edge_scale.reshape(1, slots)

    def across(x, mask):
        return lax.ppermute(x, "chan", [(i, i ^ mask) for i in range(16)])

    def cross(x):
        return lax.ppermute(x, "brick", [(i, i ^ 1) for i in range(32)])

    def shift(x, away):
        route = [(i, (i + (2 if (i % 2 == 0) == away else -2)) % 32) for i in range(32)]
        return lax.ppermute(x, "brick", route)

    w_tiles = (
        w_zero.transpose(0, 2, 1, 3).reshape(49, 8, 128),
        w_one.transpose(0, 1, 3, 2, 4).reshape(72, 8, 128),
        w_two.transpose(0, 1, 3, 2, 4).reshape(50, 8, 128),
    )
    node, b0, rims, w_own = pl.pallas_call(
        pack_kernel,
        out_shape=(sds((400, 128), BF), sds((400, 128), BF), sds((224, 128), BF), sds((1376, 128), BF)),
        in_specs=[whole((n, 8, 128)) for n in (49, 49, 49, 72, 50)],
        out_specs=(whole((400, 128)), whole((400, 128)), whole((224, 128)), whole((1376, 128))),
        grid=(1,),
        compiler_params=pltpu.CompilerParams(vmem_limit_bytes=EDGE_VMEM),
        cost_estimate=light(),
        name="pack",
    )(node_x, cotangent, *w_tiles)
    near = cross(rims)

    w_sib = across(w_own, 1)
    wz, wo, wt = pl.pallas_call(
        weight_kernel,
        out_shape=(sds((112, 512), BF), sds((192, 768), BF), sds((160, 640), BF)),
        grid=(1,),
        in_specs=[smem(), whole((1376, 128)), whole((1376, 128))],
        out_specs=(whole((112, 512)), whole((192, 768)), whole((160, 640))),
        compiler_params=params(),
        cost_estimate=light(),
        name="weights",
    )(k_s, w_own, w_sib)

    b4 = across(b0, 8)
    two = jnp.concatenate([b0, b4], axis=0)
    two, near = lax.optimization_barrier((two, near))
    b26 = across(two, 4)
    far = shift(lax.dynamic_slice_in_dim(near, 112 * high, 112, 0), True)
    b15 = across(two, 2)
    far, b15 = lax.optimization_barrier((far, b15))

    row_spec = pl.BlockSpec((1, EB), lambda i: (0, i))
    wig_spec = pl.BlockSpec((235, EB), lambda i: (0, i))
    x_spec = pl.BlockSpec((256, EB), lambda i: (0, i))
    x_own = pl.pallas_call(
        edge_in_kernel,
        out_shape=sds((256, slots), BF),
        grid=(steps,),
        in_specs=[smem(), whole((400, 128)), whole((224, 128)), whole((112, 128)), row_spec, wig_spec],
        out_specs=x_spec,
        scratch_shapes=[pltpu.VMEM((235, EB), F32), pltpu.VMEM((400, EB), F32)],
        compiler_params=params(),
        cost_estimate=light(),
        name="edge_in",
    )(h_s, node, near, far, src, wigner)
    x_own, b26 = lax.optimization_barrier((x_own, b26))
    b37 = across(b26, 2)
    x_sib = across(x_own, 1)

    s_own, g_own, to_sib = edge_call(
        z_s, edge_count, (b0, b4, b26, b15, b37), dst, src, scale, wigner, x_own, x_sib, (wz, wo, wt)
    )

    got = across(to_sib, 1)
    s_got = got[:1024].reshape(8, 128, 128)
    s_own = s_own.reshape(8, 128, 128)
    is_even = core == 0
    send = jnp.concatenate([jnp.where(is_even, s_own, s_got), jnp.where(is_even, s_got, s_own)], axis=0)
    groups = [[2 * (2 * zb + p) + h for p in range(2) for zb in range(8)] for h in range(2)]
    pieces = lax.all_to_all(send, "brick", 0, 0, axis_index_groups=groups)
    summed = pieces.astype(F32).sum(axis=0).reshape(16, 2, 4, 128)
    mine = jnp.where(high == 0, summed[:, 0], summed[:, 1])
    other = jnp.where(high == 0, summed[:, 1], summed[:, 0])

    g_all = g_own + got[1024:].astype(F32)
    left, right = g_all[400:512].astype(BF), g_all[512:624].astype(BF)
    near_rim = jnp.where(high == 0, right, left)
    far_rim = shift(jnp.where(high == 0, left, right), False)

    crossed = cross(jnp.concatenate([near_rim, far_rim, other.astype(BF).reshape(64, 128)], axis=0))
    final = mine + crossed[224:].astype(F32).reshape(16, 4, 128)
    grad_x = pl.pallas_call(
        join_kernel,
        out_shape=sds((49, 8, 128), F32),
        grid=(1,),
        in_specs=[smem(), whole((400, 128)), whole((288, 128))],
        out_specs=whole((49, 8, 128)),
        compiler_params=params(),
        cost_estimate=light(),
        name="join",
    )(h_s, g_all[:400], crossed)

    zero_rows = [None] * 7
    for n, degree in enumerate(ZORD):
        zero_rows[degree] = final[n, :, 0:56] if n < 4 else final[n - 4, :, 64:120]
    grad_zero = jnp.stack(zero_rows).reshape(7, 4, 7, 8).transpose(2, 3, 0, 1)
    grad_one = final[4:10, :, 0:96].reshape(6, 4, 2, 6, 8).transpose(2, 3, 4, 0, 1)
    two = jnp.stack([final[10:15, :, 0:40], final[10:15, :, 48:88]], axis=2)
    grad_two = two.reshape(5, 4, 2, 5, 8).transpose(2, 3, 4, 0, 1)

    return grad_x, grad_zero, grad_one, grad_two


def solution(mesh):
    in_specs = (
        P(None, "chan", "brick"),
        P(None, "chan", "brick"),
        P(None, "brick"),
        P("brick"),
        P("brick"),
        P("brick"),
        P("brick"),
        P(None, "chan", None, None),
        P(None, None, "chan", None, None),
        P(None, None, "chan", None, None),
    )
    out_specs = (
        P(None, "chan", "brick"),
        P(None, "chan", None, "brick"),
        P(None, None, "chan", None, "brick"),
        P(None, None, "chan", None, "brick"),
    )
    return jax.shard_map(body, mesh=mesh, in_specs=in_specs, out_specs=out_specs, check_vma=False)
```

```python
import functools

import jax
import jax.numpy as jnp
from jax import lax
from jax.experimental import pallas as pl
from jax.experimental.pallas import tpu as pltpu
from jax.sharding import PartitionSpec as P

BF = jnp.bfloat16
F32 = jnp.float32
EB = 256
LANES = 128
VMEM_LIMIT = 28 * 1024 * 1024
PACK_VMEM = 60 * 1024 * 1024
ZORD = (0, 2, 4, 6, 1, 3, 5)

NN = (((1,), (0,)), ((), ()))
NT = (((1,), (1,)), ((), ()))


def mm(a, b, dims=NN):
    return lax.dot_general(a, b, dims, preferred_element_type=F32)


def kept_row(degree, azimuth):
    if azimuth == 0:
        return degree
    if azimuth == 1:
        return 6 + degree
    if azimuth == -1:
        return 12 + degree
    if azimuth == 2:
        return 17 + degree
    return 22 + degree


def wig_row(degree, azimuth, column):
    start = sum((2 * min(k, 2) + 1) * (2 * k + 1) for k in range(degree))
    return start + (azimuth + min(degree, 2)) * (2 * degree + 1) + column


def orders(degree):
    reach = min(degree, 2)
    return range(-reach, reach + 1)


def eg_place(row):
    return ZORD.index(row) if row < 7 else row


def x_place(row):
    if row < 7:
        return row * 8
    if row < 13:
        return 64 + (row - 7) * 8
    if row < 19:
        return 112 + (row - 13) * 8
    if row < 24:
        return 160 + (row - 19) * 8
    return 208 + (row - 24) * 8


def iota(shape, axis):
    return lax.broadcasted_iota(jnp.int32, shape, axis)


def hot(match):
    return jnp.where(match, 1.0, 0.0).astype(BF)


def source_hots(src):
    width = src.shape[1]
    atom = iota((LANES, width), 0)
    own = hot(atom == src - 32)
    before = [hot(atom == jnp.where(src < 32, src + 32 * q, -1)) for q in range(4)]
    after = [hot(atom == jnp.where(src >= 160, src - 160 + 32 * q, -1)) for q in range(4)]
    return own, before, after


def pack_kernel(node_ref, cot_ref, zero_ref, one_ref, two_ref, node_out, cot_out, rim_out, weight_out):
    blank = jnp.zeros((8, LANES), F32)

    def rows(ref):
        return jnp.concatenate([ref[...].astype(F32).reshape(392, LANES), blank], axis=0).astype(BF)

    cot_out[...] = rows(cot_ref)
    node = rows(node_ref)
    node_out[...] = node
    atom, lane = iota((LANES, LANES), 0), iota((LANES, LANES), 1)
    parts = []
    for q in range(4):
        inside = (lane >= 32 * q) & (lane < 32 * q + 32)
        last = hot(inside & (atom == lane - 32 * q + 96))
        first = hot(inside & (atom == lane - 32 * q))
        parts.append(mm(node, jnp.concatenate([last, first], axis=1)))
    total = []
    for g in range(13):
        members = [parts[q][(4 * g + q) * 8 : (4 * g + q) * 8 + 8] for q in range(4) if 4 * g + q < 49]
        total.append(sum(members[1:], members[0]))
    total.append(jnp.zeros((8, 2 * LANES), F32))
    packed = jnp.concatenate(total, axis=0).astype(BF)
    rim_out[:112] = packed[:, :LANES]
    rim_out[112:] = packed[:, LANES:]
    parts = [ref[...].astype(F32).reshape(-1, LANES) for ref in (zero_ref, one_ref, two_ref)]
    weight_out[...] = jnp.concatenate(parts + [blank], axis=0).astype(BF)


def edge_in_kernel(h_ref, node_ref, near_ref, far_ref, src_ref, wig_ref, x_ref, rot, gathered):
    h = h_ref[0]
    src = src_ref[...]
    own, before, after = source_hots(src)
    gathered[...] = mm(node_ref[...], own)
    rot[...] = wig_ref[...].astype(F32)
    far = far_ref[...]
    from_before = jnp.where(h == 0, far, near_ref[:112])
    from_after = jnp.where(h == 0, near_ref[112:], far)
    for q in range(4):
        part = mm(from_before, before[q]) + mm(from_after, after[q])
        for g in range(13):
            coef = 4 * g + q
            if coef < 49:
                gathered[coef * 8 : coef * 8 + 8, :] += part[g * 8 : g * 8 + 8]
    rows = {}
    for degree in range(7):
        span = 2 * degree + 1
        vals = [gathered[(degree * degree + j) * 8 : (degree * degree + j + 1) * 8, :] for j in range(span)]
        for m in orders(degree):
            total = None
            for j in range(span):
                at = wig_row(degree, m, j)
                term = rot[at : at + 1, :] * vals[j]
                total = term if total is None else total + term
            rows[kept_row(degree, m)] = total
    blank = jnp.zeros((8, EB), F32)
    groups = [
        (0, [rows[r] for r in range(7)] + [blank]),
        (64, [rows[r] for r in range(7, 13)]),
        (112, [rows[r] for r in range(13, 19)]),
        (160, [rows[r] for r in range(19, 24)] + [blank]),
        (208, [rows[r] for r in range(24, 29)] + [blank]),
    ]
    for start, members in groups:
        x_ref[start : start + 8 * len(members), :] = jnp.concatenate(members, axis=0).astype(BF)


def weight_kernel(k_ref, own_ref, sib_ref, zero_ref, one_ref, two_ref):
    k = k_ref[0]
    chan, lane = iota((LANES, LANES), 0), iota((LANES, LANES), 1)

    def pick(offset):
        spot = lane - offset
        block = (spot // 8 % 2) * 4 + spot // 16
        wanted = block * 16 + k * 8 + spot % 8
        return hot((spot >= 0) & (spot < 64) & (chan == wanted))

    low, high = pick(0), pick(64)
    own, sib = own_ref[...], sib_ref[...]
    sides = [(mm(own, low), mm(own, high)), (mm(sib, low), mm(sib, high))]

    def tile(entries, place):
        halves = []
        for side in sides:
            total = None
            for half, entry in enumerate(entries):
                if entry is None:
                    continue
                sign, at = entry
                piece = side[half][at * 8 : at * 8 + 8]
                piece = piece if sign > 0 else -piece
                total = piece if total is None else total + piece
            halves.append(total)
        return jnp.concatenate(halves, axis=0).astype(BF)

    for lp in range(7):
        for p in range(4):
            entries = [
                (1, lp * 7 + ZORD[n]) if n < 7 else None for n in (2 * p, 2 * p + 1)
            ]
            zero_ref[lp * 16 : lp * 16 + 16, p * 128 : p * 128 + 128] = tile(entries, p)
    for ref, count, base in ((one_ref, 6, 49), (two_ref, 5, 121)):
        for out in range(2):
            for lp in range(count):
                for p in range(count):
                    entries = []
                    for n in (2 * p, 2 * p + 1):
                        inp, l = n // count, n % count
                        which = 0 if inp == out else 1
                        sign = -1 if (out == 1 and inp == 0) else 1
                        entries.append((sign, base + which * count * count + lp * count + l))
                    row = (out * count + lp) * 16
                    ref[row : row + 16, p * 128 : p * 128 + 128] = tile(entries, p)


def rotate_pair(z, pair_ref, dest, rot, gathered, store):
    for side in range(2):
        start = pl.multiple_of(400 * (side ^ (z // 4)), 16)
        gathered[side] = mm(pair_ref[pl.ds(start, 400), :], dest)
    for half in range(EB // LANES):
        lanes = slice(half * LANES, half * LANES + LANES)
        for degree in range(7):
            span = 2 * degree + 1
            at0 = degree * degree
            cols = [
                [gathered[side, (at0 + j) * 8 : (at0 + j + 1) * 8, lanes] for j in range(span)]
                for side in range(2)
            ]
            for m in orders(degree):
                totals = [None, None]
                for j in range(span):
                    at = wig_row(degree, m, j)
                    coeff = jnp.broadcast_to(rot[at : at + 1, lanes], (8, LANES))
                    for side in range(2):
                        term = coeff * cols[side][j]
                        totals[side] = term if totals[side] is None else totals[side] + term
                place = eg_place(kept_row(degree, m))
                store(place, lanes, jnp.concatenate(totals, axis=0).astype(BF))


def edge_factor(step, count_ref, scale_ref):
    slot = step * EB + iota((1, EB), 1)
    return jnp.where(slot < count_ref[0], 0.25 * scale_ref[...], 0.0)


def rotate_kernel(z_ref, count_ref, pair_ref, dst_ref, scale_ref, wig_ref, eg_ref, gathered, rot):
    rot[...] = wig_ref[...].astype(F32) * edge_factor(pl.program_id(0), count_ref, scale_ref)
    dest = hot(iota((LANES, EB), 0) == dst_ref[...])

    def store(place, lanes, tile):
        eg_ref[place * 16 : place * 16 + 16, lanes] = tile

    rotate_pair(z_ref[0], pair_ref, dest, rot, gathered, store)


def edge_kernel(
    z_ref, count_ref, eg0, eg2, eg1, pair_ref,
    dst_ref, src_ref, scale_ref, wig_ref, xo_ref, xs_ref, zero_ref, one_ref, two_ref,
    so_ref, go_ref, sib_ref,
    gathered, rot, plain, eg, acc, back, full, atoms, rims,
):
    step = pl.program_id(0)

    @pl.when(step == 0)
    def _():
        acc[...] = jnp.zeros_like(acc)
        atoms[...] = jnp.zeros_like(atoms)
        rims[...] = jnp.zeros_like(rims)

    z = z_ref[0]
    entries = wig_ref[...].astype(F32)
    plain[...] = entries
    rot[...] = entries * edge_factor(step, count_ref, scale_ref)
    dest = hot(iota((LANES, EB), 0) == dst_ref[...])

    def rows_of(place, n):
        return pl.ds(pl.multiple_of(place * 64 + ((z % 4) ^ n) * 16, 16), 16)

    def store(place, lanes, tile):
        eg[rows_of(place, 3), lanes] = tile

    rotate_pair(z, pair_ref, dest, rot, gathered, store)
    for n, ref in ((0, eg0), (2, eg2), (1, eg1)):
        for place in range(29):
            eg[rows_of(place, n), :] = ref[place * 16 : place * 16 + 16]

    def stacked(*pieces):
        return jnp.concatenate(pieces, axis=0)

    def blank(rows):
        return jnp.zeros((rows, EB), BF)

    xo, xs = xo_ref[...], xs_ref[...]
    acc[0:448] += mm(eg[0:448], stacked(xo[:64], blank(64), xs[:64], blank(64)), NT)
    for start, count, plus, minus in ((448, 6, 64, 112), (1216, 5, 160, 208)):
        ahead = stacked(
            xo[plus : plus + 48], -xo[minus : minus + 48], blank(32),
            xs[plus : plus + 48], -xs[minus : minus + 48], blank(32),
        )
        cross = stacked(
            xo[minus : minus + 48], xo[plus : plus + 48], blank(32),
            xs[minus : minus + 48], xs[plus : plus + 48], blank(32),
        )
        size = count * 64
        at = 448 if count == 6 else 832
        acc[at : at + size] += mm(eg[start : start + size], ahead, NT) + mm(
            eg[start + size : start + 2 * size], cross, NT
        )

    back[0:112] = mm(zero_ref[:, 0:448], eg[0:448])
    back[112:304] = mm(one_ref[...], eg[448:1216])
    back[304:464] = mm(two_ref[...], eg[1216:1856])
    quarter_start = (0, 13, 25, 37)
    for half in range(EB // LANES):
        lanes = slice(half * LANES, half * LANES + LANES)
        for degree in range(7):
            vals_m = {
                m: back[kept_row(degree, m) * 16 : kept_row(degree, m) * 16 + 16, lanes]
                for m in orders(degree)
            }
            for j in range(2 * degree + 1):
                total = None
                for m in orders(degree):
                    at = wig_row(degree, m, j)
                    term = plain[at : at + 1, lanes] * vals_m[m]
                    total = term if total is None else total + term
                coef = degree * degree + j
                row = (quarter_start[coef % 4] + coef // 4) * 16
                full[row : row + 16, lanes] = total.astype(BF)
    own, before, after = source_hots(src_ref[...])
    for q in range(4):
        start, size = quarter_start[q] * 16, (13 if q == 0 else 12) * 16
        rows = full[start : start + size]
        atoms[start : start + size] += mm(rows, own, NT)
        rims[0:size] += mm(rows, jnp.concatenate([before[q], after[q]], axis=0), NT)

    @pl.when(step == pl.num_programs(0) - 1)
    def _():
        for zb in range(8):
            tiles = []
            spot = zb % 4 * 16 + zb // 4 * 8
            for t in range(4):
                tile = acc[t * 64 + spot : t * 64 + spot + 8]
                if t < 3:
                    odd = acc[256 + t * 64 + spot : 256 + t * 64 + spot + 8]
                    halves = [pltpu.roll(odd[:, n : n + LANES], 64, 1) for n in (0, LANES)]
                    tile = tile + jnp.concatenate(halves, axis=1)
                tiles.append(tile)
            for n in range(11):
                tiles.append(acc[448 + n * 64 + spot : 448 + n * 64 + spot + 8])
            tiles.append(jnp.zeros((8, 2 * LANES), F32))
            whole_tile = jnp.concatenate(tiles, axis=0).astype(BF)
            so_ref[zb * 128 : zb * 128 + 128] = whole_tile[:, :LANES]
            sib_ref[zb * 128 : zb * 128 + 128] = whole_tile[:, LANES:]
        for side in range(2):
            tiles = []
            for coef in range(49):
                row = (quarter_start[coef % 4] + coef // 4) * 16 + side * 8
                tiles.append(atoms[row : row + 8])
            tiles.append(jnp.zeros((8, LANES), F32))
            for rim in range(2):
                for g in range(13):
                    row = g * 16 + side * 8
                    tiles.append(rims[row : row + 8, rim * LANES : rim * LANES + LANES])
                tiles.append(jnp.zeros((8, LANES), F32))
            if side == 0:
                go_ref[...] = jnp.concatenate(tiles, axis=0)
            else:
                sib_ref[1024:1648] = jnp.concatenate(tiles, axis=0).astype(BF)


def row_spec():
    return pl.BlockSpec((1, EB), lambda i: (0, i))


def wig_spec():
    return pl.BlockSpec((235, EB), lambda i: (0, i))


def rotate_call(z_s, edge_count, pair, dst, scale, wigner):
    slots = dst.shape[1]
    return pl.pallas_call(
        rotate_kernel,
        out_shape=sds((464, slots), BF),
        grid=(slots // EB,),
        in_specs=[smem(), smem(), whole((800, 128)), row_spec(), row_spec(), wig_spec()],
        out_specs=pl.BlockSpec((464, EB), lambda i: (0, i)),
        scratch_shapes=[pltpu.VMEM((2, 400, EB), F32), pltpu.VMEM((235, EB), F32)],
        compiler_params=params(),
        name="rotate",
    )(z_s, edge_count, pair, dst, scale, wigner)


def edge_call(z_s, edge_count, egs, pair, dst, src, scale, wigner, x_own, x_sib, weights):
    slots = dst.shape[1]
    x_spec = pl.BlockSpec((256, EB), lambda i: (0, i))
    return pl.pallas_call(
        edge_kernel,
        out_shape=(sds((1024, 128), BF), sds((624, 128), F32), sds((1648, 128), BF)),
        grid=(slots // EB,),
        in_specs=[smem(), smem()]
        + [pl.BlockSpec((464, EB), lambda i: (0, i))] * 3
        + [whole((800, 128)), row_spec(), row_spec(), row_spec(), wig_spec(), x_spec, x_spec]
        + [whole((112, 512)), whole((192, 768)), whole((160, 640))],
        out_specs=(whole((1024, 128)), whole((624, 128)), whole((1648, 128))),
        scratch_shapes=[
            pltpu.VMEM((2, 400, EB), F32),
            pltpu.VMEM((235, EB), F32),
            pltpu.VMEM((235, EB), F32),
            pltpu.VMEM((1856, EB), BF),
            pltpu.VMEM((1152, 256), F32),
            pltpu.VMEM((464, EB), F32),
            pltpu.VMEM((784, EB), BF),
            pltpu.VMEM((784, LANES), F32),
            pltpu.VMEM((208, 2 * LANES), F32),
        ],
        compiler_params=params(),
        name="edge",
    )(z_s, edge_count, *egs, pair, dst, src, scale, wigner, x_own, x_sib, *weights)


def finish_kernel(mine_ref, got_ref, zero_ref, one_ref, two_ref):
    total = mine_ref[...] + got_ref[...].astype(F32)

    def moved(lane):
        return total if lane == 0 else pltpu.roll(total, LANES - lane, 1)

    for lp in range(7):
        even, odd = moved(lp * 8), moved(64 + lp * 8)
        for n, l in enumerate(ZORD):
            source, row = (even, n * 4) if n < 4 else (odd, (n - 4) * 4)
            zero_ref[lp, l] = source[row : row + 4, 0:8]
    for ref, count, first, stride in ((one_ref, 6, 4, 48), (two_ref, 5, 10, 48)):
        for w in range(2):
            for lp in range(count):
                source = moved(w * stride + lp * 8)
                for l in range(count):
                    row = (first + l) * 4
                    ref[w, lp, l] = source[row : row + 4, 0:8]


def join_kernel(h_ref, own_ref, rim_ref, out_ref):
    h = h_ref[0]
    base_a = jnp.where(h == 0, 96, 0)
    base_b = 96 - base_a
    lane, atom = iota((LANES, LANES), 0), iota((LANES, LANES), 1)
    ra, rb = rim_ref[0:112], rim_ref[112:224]
    for q in range(4):
        inside = (lane >= 32 * q) & (lane < 32 * q + 32)
        put_a = hot(inside & (atom == lane - 32 * q + base_a))
        put_b = hot(inside & (atom == lane - 32 * q + base_b))
        part = mm(ra, put_a) + mm(rb, put_b)
        for g in range(13):
            coef = 4 * g + q
            if coef < 49:
                out_ref[coef] = own_ref[coef * 8 : coef * 8 + 8] + part[g * 8 : g * 8 + 8]


def smem():
    return pl.BlockSpec(memory_space=pltpu.SMEM)


def params():
    return pltpu.CompilerParams(vmem_limit_bytes=VMEM_LIMIT)


def light():
    return pl.CostEstimate(flops=1, bytes_accessed=1, transcendentals=0)


def whole(shape):
    return pl.BlockSpec(shape, lambda *_: (0,) * len(shape))


def sds(shape, dtype):
    return jax.ShapeDtypeStruct(shape, dtype)


def body(
    node_x, cotangent, wigner, src_index, dst_index, edge_scale, edge_count, w_zero, w_one, w_two
):
    chan = lax.axis_index("chan")
    brick = lax.axis_index("brick")
    z, core = chan // 2, chan % 2
    high = brick % 2
    z_s = z.astype(jnp.int32).reshape(1)
    k_s = core.astype(jnp.int32).reshape(1)
    h_s = high.astype(jnp.int32).reshape(1)
    slots = src_index.shape[0]
    steps = slots // EB
    src = src_index.reshape(1, slots)
    dst = dst_index.reshape(1, slots)
    scale = edge_scale.reshape(1, slots)

    def across(x, mask):
        return lax.ppermute(x, "chan", [(i, i ^ mask) for i in range(16)])

    def cross(x):
        return lax.ppermute(x, "brick", [(i, i ^ 1) for i in range(32)])

    def shift(x, away):
        route = [(i, (i + (2 if (i % 2 == 0) == away else -2)) % 32) for i in range(32)]
        return lax.ppermute(x, "brick", route)

    w_tiles = (
        w_zero.transpose(0, 2, 1, 3).reshape(49, 8, 128),
        w_one.transpose(0, 1, 3, 2, 4).reshape(72, 8, 128),
        w_two.transpose(0, 1, 3, 2, 4).reshape(50, 8, 128),
    )
    node, b0, rims, w_own = pl.pallas_call(
        pack_kernel,
        out_shape=(sds((400, 128), BF), sds((400, 128), BF), sds((224, 128), BF), sds((1376, 128), BF)),
        in_specs=[whole((n, 8, 128)) for n in (49, 49, 49, 72, 50)],
        out_specs=(whole((400, 128)), whole((400, 128)), whole((224, 128)), whole((1376, 128))),
        grid=(1,),
        compiler_params=pltpu.CompilerParams(vmem_limit_bytes=PACK_VMEM),
        cost_estimate=light(),
        name="pack",
    )(node_x, cotangent, *w_tiles)
    near = cross(rims)

    w_sib = across(w_own, 1)
    wz, wo, wt = pl.pallas_call(
        weight_kernel,
        out_shape=(sds((112, 512), BF), sds((192, 768), BF), sds((160, 640), BF)),
        grid=(1,),
        in_specs=[smem(), whole((1376, 128)), whole((1376, 128))],
        out_specs=(whole((112, 512)), whole((192, 768)), whole((160, 640))),
        compiler_params=params(),
        cost_estimate=light(),
        name="weights",
    )(k_s, w_own, w_sib)

    b4 = across(b0, 8)
    two = jnp.concatenate([b0, b4], axis=0)
    two, near = lax.optimization_barrier((two, near))
    b26 = across(two, 4)
    far = shift(lax.dynamic_slice_in_dim(near, 112 * high, 112, 0), True)

    def rotated(pair):
        return rotate_call(z_s, edge_count, pair, dst, scale, wigner)

    eg0 = rotated(two)

    x_spec = pl.BlockSpec((256, EB), lambda i: (0, i))
    x_own = pl.pallas_call(
        edge_in_kernel,
        out_shape=sds((256, slots), BF),
        grid=(steps,),
        in_specs=[smem(), whole((400, 128)), whole((224, 128)), whole((112, 128)), row_spec(), wig_spec()],
        out_specs=x_spec,
        scratch_shapes=[pltpu.VMEM((235, EB), F32), pltpu.VMEM((400, EB), F32)],
        compiler_params=params(),
        cost_estimate=light(),
        name="edge_in",
    )(h_s, node, near, far, src, wigner)
    again, b26, x_own, eg0, wz, wo, wt = lax.optimization_barrier((two, b26, x_own, eg0, wz, wo, wt))
    b15 = across(again, 2)
    b37 = across(b26, 2)
    eg2 = rotated(b26)
    eg1 = rotated(b15)
    x_sib = across(x_own, 1)

    s_own, g_own, to_sib = edge_call(
        z_s, edge_count, (eg0, eg2, eg1), b37, dst, src, scale, wigner, x_own, x_sib, (wz, wo, wt)
    )

    got = across(to_sib, 1)
    s_got = got[:1024].reshape(8, 128, 128)
    s_own = s_own.reshape(8, 128, 128)
    is_even = core == 0
    send = jnp.concatenate([jnp.where(is_even, s_own, s_got), jnp.where(is_even, s_got, s_own)], axis=0)
    groups = [[2 * (2 * zb + p) + h for p in range(2) for zb in range(8)] for h in range(2)]
    pieces = lax.all_to_all(send, "brick", 0, 0, axis_index_groups=groups)
    summed = pieces.astype(F32).sum(axis=0).reshape(16, 2, 4, 128)
    mine = jnp.where(high == 0, summed[:, 0], summed[:, 1])
    other = jnp.where(high == 0, summed[:, 1], summed[:, 0])

    g_all = g_own + got[1024:].astype(F32)
    left, right = g_all[400:512].astype(BF), g_all[512:624].astype(BF)
    near_rim = jnp.where(high == 0, right, left)
    far_rim = shift(jnp.where(high == 0, left, right), False)

    crossed = cross(jnp.concatenate([near_rim, far_rim], axis=0))
    crossed, mine = lax.optimization_barrier((crossed, mine))
    got_half = cross(other.astype(BF).reshape(64, 128))
    grad_x = pl.pallas_call(
        join_kernel,
        out_shape=sds((49, 8, 128), F32),
        grid=(1,),
        in_specs=[smem(), whole((400, 128)), whole((224, 128))],
        out_specs=whole((49, 8, 128)),
        compiler_params=params(),
        cost_estimate=light(),
        name="join",
    )(h_s, g_all[:400], crossed)

    zero, one, second = pl.pallas_call(
        finish_kernel,
        out_shape=(sds((7, 7, 4, 8), F32), sds((2, 6, 6, 4, 8), F32), sds((2, 5, 5, 4, 8), F32)),
        grid=(1,),
        in_specs=[whole((64, 128)), whole((64, 128))],
        out_specs=(whole((7, 7, 4, 8)), whole((2, 6, 6, 4, 8)), whole((2, 5, 5, 4, 8))),
        compiler_params=params(),
        cost_estimate=light(),
        name="finish",
    )(mine.reshape(64, 128), got_half)
    grad_zero = zero.transpose(0, 3, 1, 2)
    grad_one = one.transpose(0, 1, 4, 2, 3)
    grad_two = second.transpose(0, 1, 4, 2, 3)
    return grad_x, grad_zero, grad_one, grad_two


def solution(mesh):
    in_specs = (
        P(None, "chan", "brick"),
        P(None, "chan", "brick"),
        P(None, "brick"),
        P("brick"),
        P("brick"),
        P("brick"),
        P("brick"),
        P(None, "chan", None, None),
        P(None, None, "chan", None, None),
        P(None, None, "chan", None, None),
    )
    out_specs = (
        P(None, "chan", "brick"),
        P(None, "chan", None, "brick"),
        P(None, None, "chan", None, "brick"),
        P(None, None, "chan", None, "brick"),
    )
    return jax.shard_map(body, mesh=mesh, in_specs=in_specs, out_specs=out_specs, check_vma=False)
```

```python
import functools

import jax
import jax.numpy as jnp
from jax import lax
from jax.experimental import pallas as pl
from jax.experimental.pallas import tpu as pltpu
from jax.sharding import PartitionSpec as P

BF = jnp.bfloat16
F32 = jnp.float32
EB = 256
LANES = 128
VMEM_LIMIT = 28 * 1024 * 1024
PACK_VMEM = 60 * 1024 * 1024
ZORD = (0, 2, 4, 6, 1, 3, 5)

NN = (((1,), (0,)), ((), ()))
NT = (((1,), (1,)), ((), ()))


def mm(a, b, dims=NN):
    return lax.dot_general(a, b, dims, preferred_element_type=F32)


def kept_row(degree, azimuth):
    if azimuth == 0:
        return degree
    if azimuth == 1:
        return 6 + degree
    if azimuth == -1:
        return 12 + degree
    if azimuth == 2:
        return 17 + degree
    return 22 + degree


def wig_row(degree, azimuth, column):
    start = sum((2 * min(k, 2) + 1) * (2 * k + 1) for k in range(degree))
    return start + (azimuth + min(degree, 2)) * (2 * degree + 1) + column


def orders(degree):
    reach = min(degree, 2)
    return range(-reach, reach + 1)


def eg_place(row):
    return ZORD.index(row) if row < 7 else row


def x_place(row):
    if row < 7:
        return row * 8
    if row < 13:
        return 64 + (row - 7) * 8
    if row < 19:
        return 112 + (row - 13) * 8
    if row < 24:
        return 160 + (row - 19) * 8
    return 208 + (row - 24) * 8


def iota(shape, axis):
    return lax.broadcasted_iota(jnp.int32, shape, axis)


def hot(match):
    return jnp.where(match, 1.0, 0.0).astype(BF)


def source_hots(src):
    width = src.shape[1]
    atom = iota((LANES, width), 0)
    own = hot(atom == src - 32)
    before = [hot(atom == jnp.where(src < 32, src + 32 * q, -1)) for q in range(4)]
    after = [hot(atom == jnp.where(src >= 160, src - 160 + 32 * q, -1)) for q in range(4)]
    return own, before, after


def pack_kernel(node_ref, cot_ref, zero_ref, one_ref, two_ref, node_out, cot_out, rim_out, weight_out):
    blank = jnp.zeros((8, LANES), F32)

    def rows(ref):
        return jnp.concatenate([ref[...].astype(F32).reshape(392, LANES), blank], axis=0).astype(BF)

    cot_out[...] = rows(cot_ref)
    node = rows(node_ref)
    node_out[...] = node
    atom, lane = iota((LANES, LANES), 0), iota((LANES, LANES), 1)
    parts = []
    for q in range(4):
        inside = (lane >= 32 * q) & (lane < 32 * q + 32)
        last = hot(inside & (atom == lane - 32 * q + 96))
        first = hot(inside & (atom == lane - 32 * q))
        parts.append(mm(node, jnp.concatenate([last, first], axis=1)))
    total = []
    for g in range(13):
        members = [parts[q][(4 * g + q) * 8 : (4 * g + q) * 8 + 8] for q in range(4) if 4 * g + q < 49]
        total.append(sum(members[1:], members[0]))
    total.append(jnp.zeros((8, 2 * LANES), F32))
    packed = jnp.concatenate(total, axis=0).astype(BF)
    rim_out[:112] = packed[:, :LANES]
    rim_out[112:] = packed[:, LANES:]
    parts = [ref[...].astype(F32).reshape(-1, LANES) for ref in (zero_ref, one_ref, two_ref)]
    weight_out[...] = jnp.concatenate(parts + [blank], axis=0).astype(BF)


def edge_in_kernel(h_ref, node_ref, near_ref, far_ref, src_ref, wig_ref, x_ref, rot, gathered):
    h = h_ref[0]
    src = src_ref[...]
    own, before, after = source_hots(src)
    gathered[...] = mm(node_ref[...], own)
    rot[...] = wig_ref[...].astype(F32)
    far = far_ref[...]
    from_before = jnp.where(h == 0, far, near_ref[:112])
    from_after = jnp.where(h == 0, near_ref[112:], far)
    for q in range(4):
        part = mm(from_before, before[q]) + mm(from_after, after[q])
        for g in range(13):
            coef = 4 * g + q
            if coef < 49:
                gathered[coef * 8 : coef * 8 + 8, :] += part[g * 8 : g * 8 + 8]
    rows = {}
    for degree in range(7):
        span = 2 * degree + 1
        vals = [gathered[(degree * degree + j) * 8 : (degree * degree + j + 1) * 8, :] for j in range(span)]
        for m in orders(degree):
            total = None
            for j in range(span):
                at = wig_row(degree, m, j)
                term = rot[at : at + 1, :] * vals[j]
                total = term if total is None else total + term
            rows[kept_row(degree, m)] = total
    blank = jnp.zeros((8, EB), F32)
    groups = [
        (0, [rows[r] for r in range(7)] + [blank]),
        (64, [rows[r] for r in range(7, 13)]),
        (112, [rows[r] for r in range(13, 19)]),
        (160, [rows[r] for r in range(19, 24)] + [blank]),
        (208, [rows[r] for r in range(24, 29)] + [blank]),
    ]
    for start, members in groups:
        x_ref[start : start + 8 * len(members), :] = jnp.concatenate(members, axis=0).astype(BF)


def weight_kernel(k_ref, own_ref, sib_ref, zero_ref, one_ref, two_ref):
    k = k_ref[0]
    chan, lane = iota((LANES, LANES), 0), iota((LANES, LANES), 1)

    def pick(offset):
        spot = lane - offset
        block = (spot // 8 % 2) * 4 + spot // 16
        wanted = block * 16 + k * 8 + spot % 8
        return hot((spot >= 0) & (spot < 64) & (chan == wanted))

    low, high = pick(0), pick(64)
    own, sib = own_ref[...], sib_ref[...]
    sides = [(mm(own, low), mm(own, high)), (mm(sib, low), mm(sib, high))]

    def tile(entries, place):
        halves = []
        for side in sides:
            total = None
            for half, entry in enumerate(entries):
                if entry is None:
                    continue
                sign, at = entry
                piece = side[half][at * 8 : at * 8 + 8]
                piece = piece if sign > 0 else -piece
                total = piece if total is None else total + piece
            halves.append(total)
        return jnp.concatenate(halves, axis=0).astype(BF)

    for lp in range(7):
        for p in range(4):
            entries = [
                (1, lp * 7 + ZORD[n]) if n < 7 else None for n in (2 * p, 2 * p + 1)
            ]
            zero_ref[lp * 16 : lp * 16 + 16, p * 128 : p * 128 + 128] = tile(entries, p)
    for ref, count, base in ((one_ref, 6, 49), (two_ref, 5, 121)):
        for out in range(2):
            for lp in range(count):
                for p in range(count):
                    entries = []
                    for n in (2 * p, 2 * p + 1):
                        inp, l = n // count, n % count
                        which = 0 if inp == out else 1
                        sign = -1 if (out == 1 and inp == 0) else 1
                        entries.append((sign, base + which * count * count + lp * count + l))
                    row = (out * count + lp) * 16
                    ref[row : row + 16, p * 128 : p * 128 + 128] = tile(entries, p)


def rotate_pair(z, pair_ref, dest, rot, gathered, store):
    for side in range(2):
        start = pl.multiple_of(400 * (side ^ (z // 4)), 16)
        gathered[side] = mm(pair_ref[pl.ds(start, 400), :], dest)
    for half in range(EB // LANES):
        lanes = slice(half * LANES, half * LANES + LANES)
        for degree in range(7):
            span = 2 * degree + 1
            at0 = degree * degree
            cols = [
                [gathered[side, (at0 + j) * 8 : (at0 + j + 1) * 8, lanes] for j in range(span)]
                for side in range(2)
            ]
            for m in orders(degree):
                totals = [None, None]
                for j in range(span):
                    at = wig_row(degree, m, j)
                    coeff = jnp.broadcast_to(rot[at : at + 1, lanes], (8, LANES))
                    for side in range(2):
                        term = coeff * cols[side][j]
                        totals[side] = term if totals[side] is None else totals[side] + term
                place = eg_place(kept_row(degree, m))
                store(place, lanes, jnp.concatenate(totals, axis=0).astype(BF))


def edge_factor(step, count_ref, scale_ref):
    slot = step * EB + iota((1, EB), 1)
    return jnp.where(slot < count_ref[0], 0.25 * scale_ref[...], 0.0)


def rotate_kernel(z_ref, count_ref, pair_ref, dst_ref, scale_ref, wig_ref, eg_ref, gathered, rot):
    rot[...] = wig_ref[...].astype(F32) * edge_factor(pl.program_id(0), count_ref, scale_ref)
    dest = hot(iota((LANES, EB), 0) == dst_ref[...])

    def store(place, lanes, tile):
        eg_ref[place * 16 : place * 16 + 16, lanes] = tile

    rotate_pair(z_ref[0], pair_ref, dest, rot, gathered, store)


def edge_kernel(
    z_ref, count_ref, eg0, eg2, eg1, pair_ref,
    dst_ref, src_ref, scale_ref, wig_ref, xo_ref, xs_ref, zero_ref, one_ref, two_ref,
    so_ref, go_ref, sib_ref,
    gathered, rot, plain, eg, acc, back, full, atoms, rims,
):
    step = pl.program_id(0)

    @pl.when(step == 0)
    def _():
        acc[...] = jnp.zeros_like(acc)
        atoms[...] = jnp.zeros_like(atoms)
        rims[...] = jnp.zeros_like(rims)

    z = z_ref[0]
    entries = wig_ref[...].astype(F32)
    plain[...] = entries
    rot[...] = entries * edge_factor(step, count_ref, scale_ref)
    dest = hot(iota((LANES, EB), 0) == dst_ref[...])

    def rows_of(place, n):
        return pl.ds(pl.multiple_of(place * 64 + ((z % 4) ^ n) * 16, 16), 16)

    def store(place, lanes, tile):
        eg[rows_of(place, 3), lanes] = tile

    rotate_pair(z, pair_ref, dest, rot, gathered, store)
    for n, ref in ((0, eg0), (2, eg2), (1, eg1)):
        for place in range(29):
            eg[rows_of(place, n), :] = ref[place * 16 : place * 16 + 16]

    def stacked(*pieces):
        return jnp.concatenate(pieces, axis=0)

    def blank(rows):
        return jnp.zeros((rows, EB), BF)

    xo, xs = xo_ref[...], xs_ref[...]
    acc[0:448] += mm(eg[0:448], stacked(xo[:64], blank(64), xs[:64], blank(64)), NT)
    for start, count, plus, minus in ((448, 6, 64, 112), (1216, 5, 160, 208)):
        ahead = stacked(
            xo[plus : plus + 48], -xo[minus : minus + 48], blank(32),
            xs[plus : plus + 48], -xs[minus : minus + 48], blank(32),
        )
        cross = stacked(
            xo[minus : minus + 48], xo[plus : plus + 48], blank(32),
            xs[minus : minus + 48], xs[plus : plus + 48], blank(32),
        )
        size = count * 64
        at = 448 if count == 6 else 832
        acc[at : at + size] += mm(eg[start : start + size], ahead, NT) + mm(
            eg[start + size : start + 2 * size], cross, NT
        )

    back[0:112] = mm(zero_ref[:, 0:448], eg[0:448])
    back[112:304] = mm(one_ref[...], eg[448:1216])
    back[304:464] = mm(two_ref[...], eg[1216:1856])
    quarter_start = (0, 13, 25, 37)
    for half in range(EB // LANES):
        lanes = slice(half * LANES, half * LANES + LANES)
        for degree in range(7):
            vals_m = {
                m: back[kept_row(degree, m) * 16 : kept_row(degree, m) * 16 + 16, lanes]
                for m in orders(degree)
            }
            for j in range(2 * degree + 1):
                total = None
                for m in orders(degree):
                    at = wig_row(degree, m, j)
                    term = plain[at : at + 1, lanes] * vals_m[m]
                    total = term if total is None else total + term
                coef = degree * degree + j
                row = (quarter_start[coef % 4] + coef // 4) * 16
                full[row : row + 16, lanes] = total.astype(BF)
    own, before, after = source_hots(src_ref[...])
    for q in range(4):
        start, size = quarter_start[q] * 16, (13 if q == 0 else 12) * 16
        rows = full[start : start + size]
        atoms[start : start + size] += mm(rows, own, NT)
        rims[0:size] += mm(rows, jnp.concatenate([before[q], after[q]], axis=0), NT)

    @pl.when(step == pl.num_programs(0) - 1)
    def _():
        for zb in range(8):
            tiles = []
            spot = zb % 4 * 16 + zb // 4 * 8
            for t in range(4):
                tile = acc[t * 64 + spot : t * 64 + spot + 8]
                if t < 3:
                    odd = acc[256 + t * 64 + spot : 256 + t * 64 + spot + 8]
                    halves = [pltpu.roll(odd[:, n : n + LANES], 64, 1) for n in (0, LANES)]
                    tile = tile + jnp.concatenate(halves, axis=1)
                tiles.append(tile)
            for n in range(11):
                tiles.append(acc[448 + n * 64 + spot : 448 + n * 64 + spot + 8])
            tiles.append(jnp.zeros((8, 2 * LANES), F32))
            whole_tile = jnp.concatenate(tiles, axis=0).astype(BF)
            so_ref[zb * 128 : zb * 128 + 128] = whole_tile[:, :LANES]
            sib_ref[zb * 128 : zb * 128 + 128] = whole_tile[:, LANES:]
        for side in range(2):
            tiles = []
            for coef in range(49):
                row = (quarter_start[coef % 4] + coef // 4) * 16 + side * 8
                tiles.append(atoms[row : row + 8])
            tiles.append(jnp.zeros((8, LANES), F32))
            for rim in range(2):
                for g in range(13):
                    row = g * 16 + side * 8
                    tiles.append(rims[row : row + 8, rim * LANES : rim * LANES + LANES])
                tiles.append(jnp.zeros((8, LANES), F32))
            if side == 0:
                go_ref[...] = jnp.concatenate(tiles, axis=0)
            else:
                sib_ref[1024:1648] = jnp.concatenate(tiles, axis=0).astype(BF)


def row_spec():
    return pl.BlockSpec((1, EB), lambda i: (0, i))


def wig_spec():
    return pl.BlockSpec((235, EB), lambda i: (0, i))


def rotate_call(z_s, edge_count, pair, dst, scale, wigner):
    slots = dst.shape[1]
    return pl.pallas_call(
        rotate_kernel,
        out_shape=sds((464, slots), BF),
        grid=(slots // EB,),
        in_specs=[smem(), smem(), whole((800, 128)), row_spec(), row_spec(), wig_spec()],
        out_specs=pl.BlockSpec((464, EB), lambda i: (0, i)),
        scratch_shapes=[pltpu.VMEM((2, 400, EB), F32), pltpu.VMEM((235, EB), F32)],
        compiler_params=params(),
        name="rotate",
    )(z_s, edge_count, pair, dst, scale, wigner)


def edge_call(z_s, edge_count, egs, pair, dst, src, scale, wigner, x_own, x_sib, weights):
    slots = dst.shape[1]
    x_spec = pl.BlockSpec((256, EB), lambda i: (0, i))
    return pl.pallas_call(
        edge_kernel,
        out_shape=(sds((1024, 128), BF), sds((624, 128), F32), sds((1648, 128), BF)),
        grid=(slots // EB,),
        in_specs=[smem(), smem()]
        + [pl.BlockSpec((464, EB), lambda i: (0, i))] * 3
        + [whole((800, 128)), row_spec(), row_spec(), row_spec(), wig_spec(), x_spec, x_spec]
        + [whole((112, 512)), whole((192, 768)), whole((160, 640))],
        out_specs=(whole((1024, 128)), whole((624, 128)), whole((1648, 128))),
        scratch_shapes=[
            pltpu.VMEM((2, 400, EB), F32),
            pltpu.VMEM((235, EB), F32),
            pltpu.VMEM((235, EB), F32),
            pltpu.VMEM((1856, EB), BF),
            pltpu.VMEM((1152, 256), F32),
            pltpu.VMEM((464, EB), F32),
            pltpu.VMEM((784, EB), BF),
            pltpu.VMEM((784, LANES), F32),
            pltpu.VMEM((208, 2 * LANES), F32),
        ],
        compiler_params=params(),
        name="edge",
    )(z_s, edge_count, *egs, pair, dst, src, scale, wigner, x_own, x_sib, *weights)


def finish_kernel(mine_ref, got_ref, zero_ref, one_ref, two_ref):
    total = mine_ref[...] + got_ref[224:288].astype(F32)

    def moved(lane):
        return total if lane == 0 else pltpu.roll(total, LANES - lane, 1)

    for lp in range(7):
        even, odd = moved(lp * 8), moved(64 + lp * 8)
        for n, l in enumerate(ZORD):
            source, row = (even, n * 4) if n < 4 else (odd, (n - 4) * 4)
            zero_ref[lp, l] = source[row : row + 4, 0:8]
    for ref, count, first, stride in ((one_ref, 6, 4, 48), (two_ref, 5, 10, 48)):
        for w in range(2):
            for lp in range(count):
                source = moved(w * stride + lp * 8)
                for l in range(count):
                    row = (first + l) * 4
                    ref[w, lp, l] = source[row : row + 4, 0:8]


def join_kernel(h_ref, own_ref, rim_ref, out_ref):
    h = h_ref[0]
    base_a = jnp.where(h == 0, 96, 0)
    base_b = 96 - base_a
    lane, atom = iota((LANES, LANES), 0), iota((LANES, LANES), 1)
    ra, rb = rim_ref[0:112], rim_ref[112:224]
    for q in range(4):
        inside = (lane >= 32 * q) & (lane < 32 * q + 32)
        put_a = hot(inside & (atom == lane - 32 * q + base_a))
        put_b = hot(inside & (atom == lane - 32 * q + base_b))
        part = mm(ra, put_a) + mm(rb, put_b)
        for g in range(13):
            coef = 4 * g + q
            if coef < 49:
                out_ref[coef] = own_ref[coef * 8 : coef * 8 + 8] + part[g * 8 : g * 8 + 8]


def smem():
    return pl.BlockSpec(memory_space=pltpu.SMEM)


def params():
    return pltpu.CompilerParams(vmem_limit_bytes=VMEM_LIMIT)


def light():
    return pl.CostEstimate(flops=1, bytes_accessed=1, transcendentals=0)


def whole(shape):
    return pl.BlockSpec(shape, lambda *_: (0,) * len(shape))


def sds(shape, dtype):
    return jax.ShapeDtypeStruct(shape, dtype)


def body(
    node_x, cotangent, wigner, src_index, dst_index, edge_scale, edge_count, w_zero, w_one, w_two
):
    chan = lax.axis_index("chan")
    brick = lax.axis_index("brick")
    z, core = chan // 2, chan % 2
    high = brick % 2
    z_s = z.astype(jnp.int32).reshape(1)
    k_s = core.astype(jnp.int32).reshape(1)
    h_s = high.astype(jnp.int32).reshape(1)
    slots = src_index.shape[0]
    steps = slots // EB
    src = src_index.reshape(1, slots)
    dst = dst_index.reshape(1, slots)
    scale = edge_scale.reshape(1, slots)

    def across(x, mask):
        return lax.ppermute(x, "chan", [(i, i ^ mask) for i in range(16)])

    def cross(x):
        return lax.ppermute(x, "brick", [(i, i ^ 1) for i in range(32)])

    def shift(x, away):
        route = [(i, (i + (2 if (i % 2 == 0) == away else -2)) % 32) for i in range(32)]
        return lax.ppermute(x, "brick", route)

    w_tiles = (
        w_zero.transpose(0, 2, 1, 3).reshape(49, 8, 128),
        w_one.transpose(0, 1, 3, 2, 4).reshape(72, 8, 128),
        w_two.transpose(0, 1, 3, 2, 4).reshape(50, 8, 128),
    )
    node, b0, rims, w_own = pl.pallas_call(
        pack_kernel,
        out_shape=(sds((400, 128), BF), sds((400, 128), BF), sds((224, 128), BF), sds((1376, 128), BF)),
        in_specs=[whole((n, 8, 128)) for n in (49, 49, 49, 72, 50)],
        out_specs=(whole((400, 128)), whole((400, 128)), whole((224, 128)), whole((1376, 128))),
        grid=(1,),
        compiler_params=pltpu.CompilerParams(vmem_limit_bytes=PACK_VMEM),
        cost_estimate=light(),
        name="pack",
    )(node_x, cotangent, *w_tiles)
    near = cross(rims)

    w_sib = across(w_own, 1)
    wz, wo, wt = pl.pallas_call(
        weight_kernel,
        out_shape=(sds((112, 512), BF), sds((192, 768), BF), sds((160, 640), BF)),
        grid=(1,),
        in_specs=[smem(), whole((1376, 128)), whole((1376, 128))],
        out_specs=(whole((112, 512)), whole((192, 768)), whole((160, 640))),
        compiler_params=params(),
        cost_estimate=light(),
        name="weights",
    )(k_s, w_own, w_sib)

    b4 = across(b0, 8)
    two = jnp.concatenate([b0, b4], axis=0)
    b26 = across(two, 4)

    def rotated(pair):
        return rotate_call(z_s, edge_count, pair, dst, scale, wigner)

    eg0 = rotated(two)
    again, b26, near, eg0 = lax.optimization_barrier((two, b26, near, eg0))
    b15 = across(again, 2)
    b37 = across(b26, 2)
    eg2 = rotated(b26)
    eg1 = rotated(b15)
    far = shift(lax.dynamic_slice_in_dim(near, 112 * high, 112, 0), True)

    x_spec = pl.BlockSpec((256, EB), lambda i: (0, i))
    x_own = pl.pallas_call(
        edge_in_kernel,
        out_shape=sds((256, slots), BF),
        grid=(steps,),
        in_specs=[smem(), whole((400, 128)), whole((224, 128)), whole((112, 128)), row_spec(), wig_spec()],
        out_specs=x_spec,
        scratch_shapes=[pltpu.VMEM((235, EB), F32), pltpu.VMEM((400, EB), F32)],
        compiler_params=params(),
        cost_estimate=light(),
        name="edge_in",
    )(h_s, node, near, far, src, wigner)
    x_own, b37, eg1, eg2, wz, wo, wt = lax.optimization_barrier((x_own, b37, eg1, eg2, wz, wo, wt))
    x_sib = across(x_own, 1)

    s_own, g_own, to_sib = edge_call(
        z_s, edge_count, (eg0, eg2, eg1), b37, dst, src, scale, wigner, x_own, x_sib, (wz, wo, wt)
    )

    got = across(to_sib, 1)
    s_got = got[:1024].reshape(8, 128, 128)
    s_own = s_own.reshape(8, 128, 128)
    is_even = core == 0
    send = jnp.concatenate([jnp.where(is_even, s_own, s_got), jnp.where(is_even, s_got, s_own)], axis=0)
    groups = [[2 * (2 * zb + p) + h for p in range(2) for zb in range(8)] for h in range(2)]
    pieces = lax.all_to_all(send, "brick", 0, 0, axis_index_groups=groups)
    summed = pieces.astype(F32).sum(axis=0).reshape(16, 2, 4, 128)
    mine = jnp.where(high == 0, summed[:, 0], summed[:, 1])
    other = jnp.where(high == 0, summed[:, 1], summed[:, 0])

    g_all = g_own + got[1024:].astype(F32)
    left, right = g_all[400:512].astype(BF), g_all[512:624].astype(BF)
    near_rim = jnp.where(high == 0, right, left)
    far_rim = shift(jnp.where(high == 0, left, right), False)

    crossed = cross(jnp.concatenate([near_rim, far_rim, other.astype(BF).reshape(64, 128)], axis=0))
    grad_x = pl.pallas_call(
        join_kernel,
        out_shape=sds((49, 8, 128), F32),
        grid=(1,),
        in_specs=[smem(), whole((624, 128)), whole((288, 128))],
        out_specs=whole((49, 8, 128)),
        compiler_params=params(),
        cost_estimate=light(),
        name="join",
    )(h_s, g_all, crossed)

    zero, one, second = pl.pallas_call(
        finish_kernel,
        out_shape=(sds((7, 7, 4, 8), F32), sds((2, 6, 6, 4, 8), F32), sds((2, 5, 5, 4, 8), F32)),
        grid=(1,),
        in_specs=[whole((64, 128)), whole((288, 128))],
        out_specs=(whole((7, 7, 4, 8)), whole((2, 6, 6, 4, 8)), whole((2, 5, 5, 4, 8))),
        compiler_params=params(),
        cost_estimate=light(),
        name="finish",
    )(mine.reshape(64, 128), crossed)
    grad_zero = zero.transpose(0, 3, 1, 2)
    grad_one = one.transpose(0, 1, 4, 2, 3)
    grad_two = second.transpose(0, 1, 4, 2, 3)
    return grad_x, grad_zero, grad_one, grad_two


def solution(mesh):
    in_specs = (
        P(None, "chan", "brick"),
        P(None, "chan", "brick"),
        P(None, "brick"),
        P("brick"),
        P("brick"),
        P("brick"),
        P("brick"),
        P(None, "chan", None, None),
        P(None, None, "chan", None, None),
        P(None, None, "chan", None, None),
    )
    out_specs = (
        P(None, "chan", "brick"),
        P(None, "chan", None, "brick"),
        P(None, None, "chan", None, "brick"),
        P(None, None, "chan", None, "brick"),
    )
    return jax.shard_map(body, mesh=mesh, in_specs=in_specs, out_specs=out_specs, check_vma=False)
```

```python
import functools

import jax
import jax.numpy as jnp
from jax import lax
from jax.experimental import pallas as pl
from jax.experimental.pallas import tpu as pltpu
from jax.sharding import PartitionSpec as P

BF = jnp.bfloat16
F32 = jnp.float32
EB = 256
LANES = 128
VMEM_LIMIT = 28 * 1024 * 1024
PACK_VMEM = 60 * 1024 * 1024
ZORD = (0, 2, 4, 6, 1, 3, 5)

NN = (((1,), (0,)), ((), ()))
NT = (((1,), (1,)), ((), ()))


def mm(a, b, dims=NN):
    return lax.dot_general(a, b, dims, preferred_element_type=F32)


def kept_row(degree, azimuth):
    if azimuth == 0:
        return degree
    if azimuth == 1:
        return 6 + degree
    if azimuth == -1:
        return 12 + degree
    if azimuth == 2:
        return 17 + degree
    return 22 + degree


def wig_row(degree, azimuth, column):
    start = sum((2 * min(k, 2) + 1) * (2 * k + 1) for k in range(degree))
    return start + (azimuth + min(degree, 2)) * (2 * degree + 1) + column


def orders(degree):
    reach = min(degree, 2)
    return range(-reach, reach + 1)


def eg_place(row):
    return ZORD.index(row) if row < 7 else row


def x_place(row):
    if row < 7:
        return row * 8
    if row < 13:
        return 64 + (row - 7) * 8
    if row < 19:
        return 112 + (row - 13) * 8
    if row < 24:
        return 160 + (row - 19) * 8
    return 208 + (row - 24) * 8


def iota(shape, axis):
    return lax.broadcasted_iota(jnp.int32, shape, axis)


def hot(match):
    return jnp.where(match, 1.0, 0.0).astype(BF)


def source_hots(src):
    width = src.shape[1]
    atom = iota((LANES, width), 0)
    own = hot(atom == src - 32)
    before = [hot(atom == jnp.where(src < 32, src + 32 * q, -1)) for q in range(4)]
    after = [hot(atom == jnp.where(src >= 160, src - 160 + 32 * q, -1)) for q in range(4)]
    return own, before, after


def pack_kernel(node_ref, cot_ref, zero_ref, one_ref, two_ref, node_out, cot_out, rim_out, weight_out):
    blank = jnp.zeros((8, LANES), F32)

    def rows(ref):
        return jnp.concatenate([ref[...].astype(F32).reshape(392, LANES), blank], axis=0).astype(BF)

    cot_out[...] = rows(cot_ref)
    node = rows(node_ref)
    node_out[...] = node
    atom, lane = iota((LANES, LANES), 0), iota((LANES, LANES), 1)
    parts = []
    for q in range(4):
        inside = (lane >= 32 * q) & (lane < 32 * q + 32)
        last = hot(inside & (atom == lane - 32 * q + 96))
        first = hot(inside & (atom == lane - 32 * q))
        parts.append(mm(node, jnp.concatenate([last, first], axis=1)))
    total = []
    for g in range(13):
        members = [parts[q][(4 * g + q) * 8 : (4 * g + q) * 8 + 8] for q in range(4) if 4 * g + q < 49]
        total.append(sum(members[1:], members[0]))
    total.append(jnp.zeros((8, 2 * LANES), F32))
    packed = jnp.concatenate(total, axis=0).astype(BF)
    rim_out[:112] = packed[:, :LANES]
    rim_out[112:] = packed[:, LANES:]
    parts = [ref[...].astype(F32).reshape(-1, LANES) for ref in (zero_ref, one_ref, two_ref)]
    weight_out[...] = jnp.concatenate(parts + [blank], axis=0).astype(BF)


def edge_in_kernel(h_ref, node_ref, near_ref, far_ref, src_ref, wig_ref, x_ref, rot, gathered):
    h = h_ref[0]
    src = src_ref[...]
    own, before, after = source_hots(src)
    gathered[...] = mm(node_ref[...], own)
    rot[...] = wig_ref[...].astype(F32)
    far = far_ref[...]
    from_before = jnp.where(h == 0, far, near_ref[:112])
    from_after = jnp.where(h == 0, near_ref[112:], far)
    for q in range(4):
        part = mm(from_before, before[q]) + mm(from_after, after[q])
        for g in range(13):
            coef = 4 * g + q
            if coef < 49:
                gathered[coef * 8 : coef * 8 + 8, :] += part[g * 8 : g * 8 + 8]
    rows = {}
    for degree in range(7):
        span = 2 * degree + 1
        vals = [gathered[(degree * degree + j) * 8 : (degree * degree + j + 1) * 8, :] for j in range(span)]
        for m in orders(degree):
            total = None
            for j in range(span):
                at = wig_row(degree, m, j)
                term = rot[at : at + 1, :] * vals[j]
                total = term if total is None else total + term
            rows[kept_row(degree, m)] = total
    blank = jnp.zeros((8, EB), F32)
    groups = [
        (0, [rows[r] for r in range(7)] + [blank]),
        (64, [rows[r] for r in range(7, 13)]),
        (112, [rows[r] for r in range(13, 19)]),
        (160, [rows[r] for r in range(19, 24)] + [blank]),
        (208, [rows[r] for r in range(24, 29)] + [blank]),
    ]
    for start, members in groups:
        x_ref[start : start + 8 * len(members), :] = jnp.concatenate(members, axis=0).astype(BF)


def weight_kernel(k_ref, own_ref, sib_ref, zero_ref, one_ref, two_ref):
    k = k_ref[0]
    chan, lane = iota((LANES, LANES), 0), iota((LANES, LANES), 1)

    def pick(offset):
        spot = lane - offset
        block = (spot // 8 % 2) * 4 + spot // 16
        wanted = block * 16 + k * 8 + spot % 8
        return hot((spot >= 0) & (spot < 64) & (chan == wanted))

    low, high = pick(0), pick(64)
    own, sib = own_ref[...], sib_ref[...]
    sides = [(mm(own, low), mm(own, high)), (mm(sib, low), mm(sib, high))]

    def tile(entries, place):
        halves = []
        for side in sides:
            total = None
            for half, entry in enumerate(entries):
                if entry is None:
                    continue
                sign, at = entry
                piece = side[half][at * 8 : at * 8 + 8]
                piece = piece if sign > 0 else -piece
                total = piece if total is None else total + piece
            halves.append(total)
        return jnp.concatenate(halves, axis=0).astype(BF)

    for lp in range(7):
        for p in range(4):
            entries = [
                (1, lp * 7 + ZORD[n]) if n < 7 else None for n in (2 * p, 2 * p + 1)
            ]
            zero_ref[lp * 16 : lp * 16 + 16, p * 128 : p * 128 + 128] = tile(entries, p)
    for ref, count, base in ((one_ref, 6, 49), (two_ref, 5, 121)):
        for out in range(2):
            for lp in range(count):
                for p in range(count):
                    entries = []
                    for n in (2 * p, 2 * p + 1):
                        inp, l = n // count, n % count
                        which = 0 if inp == out else 1
                        sign = -1 if (out == 1 and inp == 0) else 1
                        entries.append((sign, base + which * count * count + lp * count + l))
                    row = (out * count + lp) * 16
                    ref[row : row + 16, p * 128 : p * 128 + 128] = tile(entries, p)


def rotate_pair(z, pair_ref, dest, rot, gathered, store):
    for side in range(2):
        start = pl.multiple_of(400 * (side ^ (z // 4)), 16)
        gathered[side] = mm(pair_ref[pl.ds(start, 400), :], dest)
    for half in range(EB // LANES):
        lanes = slice(half * LANES, half * LANES + LANES)
        for degree in range(7):
            span = 2 * degree + 1
            at0 = degree * degree
            cols = [
                [gathered[side, (at0 + j) * 8 : (at0 + j + 1) * 8, lanes] for j in range(span)]
                for side in range(2)
            ]
            for m in orders(degree):
                totals = [None, None]
                for j in range(span):
                    at = wig_row(degree, m, j)
                    coeff = jnp.broadcast_to(rot[at : at + 1, lanes], (8, LANES))
                    for side in range(2):
                        term = coeff * cols[side][j]
                        totals[side] = term if totals[side] is None else totals[side] + term
                place = eg_place(kept_row(degree, m))
                store(place, lanes, jnp.concatenate(totals, axis=0).astype(BF))


def edge_factor(step, count_ref, scale_ref):
    slot = step * EB + iota((1, EB), 1)
    return jnp.where(slot < count_ref[0], 0.25 * scale_ref[...], 0.0)


def rotate_kernel(z_ref, count_ref, pair_ref, dst_ref, scale_ref, wig_ref, eg_ref, gathered, rot):
    rot[...] = wig_ref[...].astype(F32) * edge_factor(pl.program_id(0), count_ref, scale_ref)
    dest = hot(iota((LANES, EB), 0) == dst_ref[...])

    def store(place, lanes, tile):
        eg_ref[place * 16 : place * 16 + 16, lanes] = tile

    rotate_pair(z_ref[0], pair_ref, dest, rot, gathered, store)


def edge_kernel(
    z_ref, count_ref, eg0, eg2, eg1, pair_ref,
    dst_ref, src_ref, scale_ref, wig_ref, xo_ref, xs_ref, zero_ref, one_ref, two_ref,
    so_ref, go_ref, sib_ref,
    gathered, rot, plain, eg, acc, back, full, atoms, rims,
):
    step = pl.program_id(0)

    @pl.when(step == 0)
    def _():
        acc[...] = jnp.zeros_like(acc)
        atoms[...] = jnp.zeros_like(atoms)
        rims[...] = jnp.zeros_like(rims)

    z = z_ref[0]
    entries = wig_ref[...].astype(F32)
    plain[...] = entries
    rot[...] = entries * edge_factor(step, count_ref, scale_ref)
    dest = hot(iota((LANES, EB), 0) == dst_ref[...])

    def rows_of(place, n):
        return pl.ds(pl.multiple_of(place * 64 + ((z % 4) ^ n) * 16, 16), 16)

    def store(place, lanes, tile):
        eg[rows_of(place, 3), lanes] = tile

    rotate_pair(z, pair_ref, dest, rot, gathered, store)
    for n, ref in ((0, eg0), (2, eg2), (1, eg1)):
        for place in range(29):
            eg[rows_of(place, n), :] = ref[place * 16 : place * 16 + 16]

    def stacked(*pieces):
        return jnp.concatenate(pieces, axis=0)

    def blank(rows):
        return jnp.zeros((rows, EB), BF)

    xo, xs = xo_ref[...], xs_ref[...]
    acc[0:448] += mm(eg[0:448], stacked(xo[:64], blank(64), xs[:64], blank(64)), NT)
    for start, count, plus, minus in ((448, 6, 64, 112), (1216, 5, 160, 208)):
        ahead = stacked(
            xo[plus : plus + 48], -xo[minus : minus + 48], blank(32),
            xs[plus : plus + 48], -xs[minus : minus + 48], blank(32),
        )
        cross = stacked(
            xo[minus : minus + 48], xo[plus : plus + 48], blank(32),
            xs[minus : minus + 48], xs[plus : plus + 48], blank(32),
        )
        size = count * 64
        at = 448 if count == 6 else 832
        acc[at : at + size] += mm(eg[start : start + size], ahead, NT) + mm(
            eg[start + size : start + 2 * size], cross, NT
        )

    back[0:112] = mm(zero_ref[:, 0:448], eg[0:448])
    back[112:304] = mm(one_ref[...], eg[448:1216])
    back[304:464] = mm(two_ref[...], eg[1216:1856])
    quarter_start = (0, 13, 25, 37)
    for half in range(EB // LANES):
        lanes = slice(half * LANES, half * LANES + LANES)
        for degree in range(7):
            vals_m = {
                m: back[kept_row(degree, m) * 16 : kept_row(degree, m) * 16 + 16, lanes]
                for m in orders(degree)
            }
            for j in range(2 * degree + 1):
                total = None
                for m in orders(degree):
                    at = wig_row(degree, m, j)
                    term = plain[at : at + 1, lanes] * vals_m[m]
                    total = term if total is None else total + term
                coef = degree * degree + j
                row = (quarter_start[coef % 4] + coef // 4) * 16
                full[row : row + 16, lanes] = total.astype(BF)
    own, before, after = source_hots(src_ref[...])
    for q in range(4):
        start, size = quarter_start[q] * 16, (13 if q == 0 else 12) * 16
        rows = full[start : start + size]
        atoms[start : start + size] += mm(rows, own, NT)
        rims[0:size] += mm(rows, jnp.concatenate([before[q], after[q]], axis=0), NT)

    @pl.when(step == pl.num_programs(0) - 1)
    def _():
        for zb in range(8):
            tiles = []
            spot = zb % 4 * 16 + zb // 4 * 8
            for t in range(4):
                tile = acc[t * 64 + spot : t * 64 + spot + 8]
                if t < 3:
                    odd = acc[256 + t * 64 + spot : 256 + t * 64 + spot + 8]
                    halves = [pltpu.roll(odd[:, n : n + LANES], 64, 1) for n in (0, LANES)]
                    tile = tile + jnp.concatenate(halves, axis=1)
                tiles.append(tile)
            for n in range(11):
                tiles.append(acc[448 + n * 64 + spot : 448 + n * 64 + spot + 8])
            tiles.append(jnp.zeros((8, 2 * LANES), F32))
            whole_tile = jnp.concatenate(tiles, axis=0).astype(BF)
            so_ref[zb * 128 : zb * 128 + 128] = whole_tile[:, :LANES]
            sib_ref[zb * 128 : zb * 128 + 128] = whole_tile[:, LANES:]
        for side in range(2):
            tiles = []
            for coef in range(49):
                row = (quarter_start[coef % 4] + coef // 4) * 16 + side * 8
                tiles.append(atoms[row : row + 8])
            tiles.append(jnp.zeros((8, LANES), F32))
            for rim in range(2):
                for g in range(13):
                    row = g * 16 + side * 8
                    tiles.append(rims[row : row + 8, rim * LANES : rim * LANES + LANES])
                tiles.append(jnp.zeros((8, LANES), F32))
            if side == 0:
                go_ref[...] = jnp.concatenate(tiles, axis=0)
            else:
                sib_ref[1024:1648] = jnp.concatenate(tiles, axis=0).astype(BF)


def row_spec():
    return pl.BlockSpec((1, EB), lambda i: (0, i))


def wig_spec():
    return pl.BlockSpec((235, EB), lambda i: (0, i))


def rotate_call(z_s, edge_count, pair, dst, scale, wigner):
    slots = dst.shape[1]
    return pl.pallas_call(
        rotate_kernel,
        out_shape=sds((464, slots), BF),
        grid=(slots // EB,),
        in_specs=[smem(), smem(), whole((800, 128)), row_spec(), row_spec(), wig_spec()],
        out_specs=pl.BlockSpec((464, EB), lambda i: (0, i)),
        scratch_shapes=[pltpu.VMEM((2, 400, EB), F32), pltpu.VMEM((235, EB), F32)],
        compiler_params=params(),
        name="rotate",
    )(z_s, edge_count, pair, dst, scale, wigner)


def edge_call(z_s, edge_count, egs, pair, dst, src, scale, wigner, x_own, x_sib, weights):
    slots = dst.shape[1]
    x_spec = pl.BlockSpec((256, EB), lambda i: (0, i))
    return pl.pallas_call(
        edge_kernel,
        out_shape=(sds((1024, 128), BF), sds((624, 128), F32), sds((1648, 128), BF)),
        grid=(slots // EB,),
        in_specs=[smem(), smem()]
        + [pl.BlockSpec((464, EB), lambda i: (0, i))] * 3
        + [whole((800, 128)), row_spec(), row_spec(), row_spec(), wig_spec(), x_spec, x_spec]
        + [whole((112, 512)), whole((192, 768)), whole((160, 640))],
        out_specs=(whole((1024, 128)), whole((624, 128)), whole((1648, 128))),
        scratch_shapes=[
            pltpu.VMEM((2, 400, EB), F32),
            pltpu.VMEM((235, EB), F32),
            pltpu.VMEM((235, EB), F32),
            pltpu.VMEM((1856, EB), BF),
            pltpu.VMEM((1152, 256), F32),
            pltpu.VMEM((464, EB), F32),
            pltpu.VMEM((784, EB), BF),
            pltpu.VMEM((784, LANES), F32),
            pltpu.VMEM((208, 2 * LANES), F32),
        ],
        compiler_params=params(),
        name="edge",
    )(z_s, edge_count, *egs, pair, dst, src, scale, wigner, x_own, x_sib, *weights)


def finish_kernel(mine_ref, got_ref, zero_ref, one_ref, two_ref):
    total = mine_ref[...] + got_ref[224:288].astype(F32)

    def moved(lane):
        return total if lane == 0 else pltpu.roll(total, LANES - lane, 1)

    for lp in range(7):
        even, odd = moved(lp * 8), moved(64 + lp * 8)
        for n, l in enumerate(ZORD):
            source, row = (even, n * 4) if n < 4 else (odd, (n - 4) * 4)
            zero_ref[lp, l] = source[row : row + 4, 0:8]
    for ref, count, first, stride in ((one_ref, 6, 4, 48), (two_ref, 5, 10, 48)):
        for w in range(2):
            for lp in range(count):
                source = moved(w * stride + lp * 8)
                for l in range(count):
                    row = (first + l) * 4
                    ref[w, lp, l] = source[row : row + 4, 0:8]


def join_kernel(h_ref, own_ref, rim_ref, out_ref):
    h = h_ref[0]
    base_a = jnp.where(h == 0, 96, 0)
    base_b = 96 - base_a
    lane, atom = iota((LANES, LANES), 0), iota((LANES, LANES), 1)
    ra, rb = rim_ref[0:112], rim_ref[112:224]
    for q in range(4):
        inside = (lane >= 32 * q) & (lane < 32 * q + 32)
        put_a = hot(inside & (atom == lane - 32 * q + base_a))
        put_b = hot(inside & (atom == lane - 32 * q + base_b))
        part = mm(ra, put_a) + mm(rb, put_b)
        for g in range(13):
            coef = 4 * g + q
            if coef < 49:
                out_ref[coef] = own_ref[coef * 8 : coef * 8 + 8] + part[g * 8 : g * 8 + 8]


def smem():
    return pl.BlockSpec(memory_space=pltpu.SMEM)


def params():
    return pltpu.CompilerParams(vmem_limit_bytes=VMEM_LIMIT)


def light():
    return pl.CostEstimate(flops=1, bytes_accessed=1, transcendentals=0)


def whole(shape):
    return pl.BlockSpec(shape, lambda *_: (0,) * len(shape))


def sds(shape, dtype):
    return jax.ShapeDtypeStruct(shape, dtype)


def body(
    node_x, cotangent, wigner, src_index, dst_index, edge_scale, edge_count, w_zero, w_one, w_two
):
    chan = lax.axis_index("chan")
    brick = lax.axis_index("brick")
    z, core = chan // 2, chan % 2
    high = brick % 2
    z_s = z.astype(jnp.int32).reshape(1)
    k_s = core.astype(jnp.int32).reshape(1)
    h_s = high.astype(jnp.int32).reshape(1)
    slots = src_index.shape[0]
    steps = slots // EB
    src = src_index.reshape(1, slots)
    dst = dst_index.reshape(1, slots)
    scale = edge_scale.reshape(1, slots)

    def across(x, mask):
        return lax.ppermute(x, "chan", [(i, i ^ mask) for i in range(16)])

    def cross(x):
        return lax.ppermute(x, "brick", [(i, i ^ 1) for i in range(32)])

    def shift(x, away):
        route = [(i, (i + (2 if (i % 2 == 0) == away else -2)) % 32) for i in range(32)]
        return lax.ppermute(x, "brick", route)

    w_tiles = (
        w_zero.transpose(0, 2, 1, 3).reshape(49, 8, 128),
        w_one.transpose(0, 1, 3, 2, 4).reshape(72, 8, 128),
        w_two.transpose(0, 1, 3, 2, 4).reshape(50, 8, 128),
    )
    node, b0, rims, w_own = pl.pallas_call(
        pack_kernel,
        out_shape=(sds((400, 128), BF), sds((400, 128), BF), sds((224, 128), BF), sds((1376, 128), BF)),
        in_specs=[whole((n, 8, 128)) for n in (49, 49, 49, 72, 50)],
        out_specs=(whole((400, 128)), whole((400, 128)), whole((224, 128)), whole((1376, 128))),
        grid=(1,),
        compiler_params=pltpu.CompilerParams(vmem_limit_bytes=PACK_VMEM),
        cost_estimate=light(),
        name="pack",
    )(node_x, cotangent, *w_tiles)
    near = cross(rims)

    far = shift(lax.dynamic_slice_in_dim(near, 112 * high, 112, 0), True)
    b4 = across(b0, 8)
    b4, far = lax.optimization_barrier((b4, far))
    two = jnp.concatenate([b0, b4], axis=0)
    two, far, w_own = lax.optimization_barrier((two, far, w_own))
    b26 = across(two, 4)

    def rotated(pair):
        return rotate_call(z_s, edge_count, pair, dst, scale, wigner)

    eg0 = rotated(two)
    far, eg0 = lax.optimization_barrier((far, eg0))

    w_sib = across(w_own, 1)
    wz, wo, wt = pl.pallas_call(
        weight_kernel,
        out_shape=(sds((112, 512), BF), sds((192, 768), BF), sds((160, 640), BF)),
        grid=(1,),
        in_specs=[smem(), whole((1376, 128)), whole((1376, 128))],
        out_specs=(whole((112, 512)), whole((192, 768)), whole((160, 640))),
        compiler_params=params(),
        cost_estimate=light(),
        name="weights",
    )(k_s, w_own, w_sib)

    x_spec = pl.BlockSpec((256, EB), lambda i: (0, i))
    x_own = pl.pallas_call(
        edge_in_kernel,
        out_shape=sds((256, slots), BF),
        grid=(steps,),
        in_specs=[smem(), whole((400, 128)), whole((224, 128)), whole((112, 128)), row_spec(), wig_spec()],
        out_specs=x_spec,
        scratch_shapes=[pltpu.VMEM((235, EB), F32), pltpu.VMEM((400, EB), F32)],
        compiler_params=params(),
        cost_estimate=light(),
        name="edge_in",
    )(h_s, node, near, far, src, wigner)
    two, b26, x_own, eg0, wz, wo, wt = lax.optimization_barrier(
        (two, b26, x_own, eg0, wz, wo, wt)
    )
    b15 = across(two, 2)
    b37 = across(b26, 2)
    eg2 = rotated(b26)
    eg1 = rotated(b15)
    x_sib = across(x_own, 1)

    s_own, g_own, to_sib = edge_call(
        z_s, edge_count, (eg0, eg2, eg1), b37, dst, src, scale, wigner, x_own, x_sib, (wz, wo, wt)
    )

    got = across(to_sib, 1)
    s_got = got[:1024].reshape(8, 128, 128)
    s_own = s_own.reshape(8, 128, 128)
    is_even = core == 0
    send = jnp.concatenate([jnp.where(is_even, s_own, s_got), jnp.where(is_even, s_got, s_own)], axis=0)
    groups = [[2 * (2 * zb + p) + h for p in range(2) for zb in range(8)] for h in range(2)]
    pieces = lax.all_to_all(send, "brick", 0, 0, axis_index_groups=groups)
    summed = pieces.astype(F32).sum(axis=0).reshape(16, 2, 4, 128)
    mine = jnp.where(high == 0, summed[:, 0], summed[:, 1])
    other = jnp.where(high == 0, summed[:, 1], summed[:, 0])

    g_all = g_own + got[1024:].astype(F32)
    left, right = g_all[400:512].astype(BF), g_all[512:624].astype(BF)
    near_rim = jnp.where(high == 0, right, left)
    far_rim = shift(jnp.where(high == 0, left, right), False)

    crossed = cross(jnp.concatenate([near_rim, far_rim, other.astype(BF).reshape(64, 128)], axis=0))
    grad_x = pl.pallas_call(
        join_kernel,
        out_shape=sds((49, 8, 128), F32),
        grid=(1,),
        in_specs=[smem(), whole((624, 128)), whole((288, 128))],
        out_specs=whole((49, 8, 128)),
        compiler_params=params(),
        cost_estimate=light(),
        name="join",
    )(h_s, g_all, crossed)

    zero, one, second = pl.pallas_call(
        finish_kernel,
        out_shape=(sds((7, 7, 4, 8), F32), sds((2, 6, 6, 4, 8), F32), sds((2, 5, 5, 4, 8), F32)),
        grid=(1,),
        in_specs=[whole((64, 128)), whole((288, 128))],
        out_specs=(whole((7, 7, 4, 8)), whole((2, 6, 6, 4, 8)), whole((2, 5, 5, 4, 8))),
        compiler_params=params(),
        cost_estimate=light(),
        name="finish",
    )(mine.reshape(64, 128), crossed)
    grad_zero = zero.transpose(0, 3, 1, 2)
    grad_one = one.transpose(0, 1, 4, 2, 3)
    grad_two = second.transpose(0, 1, 4, 2, 3)
    return grad_x, grad_zero, grad_one, grad_two


def solution(mesh):
    in_specs = (
        P(None, "chan", "brick"),
        P(None, "chan", "brick"),
        P(None, "brick"),
        P("brick"),
        P("brick"),
        P("brick"),
        P("brick"),
        P(None, "chan", None, None),
        P(None, None, "chan", None, None),
        P(None, None, "chan", None, None),
    )
    out_specs = (
        P(None, "chan", "brick"),
        P(None, "chan", None, "brick"),
        P(None, None, "chan", None, "brick"),
        P(None, None, "chan", None, "brick"),
    )
    return jax.shard_map(body, mesh=mesh, in_specs=in_specs, out_specs=out_specs, check_vma=False)
```

```python
import functools

import jax
import jax.numpy as jnp
from jax import lax
from jax.experimental import pallas as pl
from jax.experimental.pallas import tpu as pltpu
from jax.sharding import PartitionSpec as P

BF = jnp.bfloat16
F32 = jnp.float32
EB = 256
LANES = 128
VMEM_LIMIT = 28 * 1024 * 1024
PACK_VMEM = 60 * 1024 * 1024
ZORD = (0, 2, 4, 6, 1, 3, 5)

NN = (((1,), (0,)), ((), ()))
NT = (((1,), (1,)), ((), ()))


def mm(a, b, dims=NN):
    return lax.dot_general(a, b, dims, preferred_element_type=F32)


def kept_row(degree, azimuth):
    if azimuth == 0:
        return degree
    if azimuth == 1:
        return 6 + degree
    if azimuth == -1:
        return 12 + degree
    if azimuth == 2:
        return 17 + degree
    return 22 + degree


def wig_row(degree, azimuth, column):
    start = sum((2 * min(k, 2) + 1) * (2 * k + 1) for k in range(degree))
    return start + (azimuth + min(degree, 2)) * (2 * degree + 1) + column


def orders(degree):
    reach = min(degree, 2)
    return range(-reach, reach + 1)


def eg_place(row):
    return ZORD.index(row) if row < 7 else row


def x_place(row):
    if row < 7:
        return row * 8
    if row < 13:
        return 64 + (row - 7) * 8
    if row < 19:
        return 112 + (row - 13) * 8
    if row < 24:
        return 160 + (row - 19) * 8
    return 208 + (row - 24) * 8


def iota(shape, axis):
    return lax.broadcasted_iota(jnp.int32, shape, axis)


def hot(match):
    return jnp.where(match, 1.0, 0.0).astype(BF)


def source_hots(src):
    width = src.shape[1]
    atom = iota((LANES, width), 0)
    own = hot(atom == src - 32)
    before = [hot(atom == jnp.where(src < 32, src + 32 * q, -1)) for q in range(4)]
    after = [hot(atom == jnp.where(src >= 160, src - 160 + 32 * q, -1)) for q in range(4)]
    return own, before, after


def pack_kernel(node_ref, cot_ref, zero_ref, one_ref, two_ref, node_out, cot_out, rim_out, weight_out):
    blank = jnp.zeros((8, LANES), F32)

    def rows(ref):
        return jnp.concatenate([ref[...].astype(F32).reshape(392, LANES), blank], axis=0).astype(BF)

    cot_out[...] = rows(cot_ref)
    node = rows(node_ref)
    node_out[...] = node
    atom, lane = iota((LANES, LANES), 0), iota((LANES, LANES), 1)
    parts = []
    for q in range(4):
        inside = (lane >= 32 * q) & (lane < 32 * q + 32)
        last = hot(inside & (atom == lane - 32 * q + 96))
        first = hot(inside & (atom == lane - 32 * q))
        parts.append(mm(node, jnp.concatenate([last, first], axis=1)))
    total = []
    for g in range(13):
        members = [parts[q][(4 * g + q) * 8 : (4 * g + q) * 8 + 8] for q in range(4) if 4 * g + q < 49]
        total.append(sum(members[1:], members[0]))
    total.append(jnp.zeros((8, 2 * LANES), F32))
    packed = jnp.concatenate(total, axis=0).astype(BF)
    rim_out[:112] = packed[:, :LANES]
    rim_out[112:] = packed[:, LANES:]
    parts = [ref[...].astype(F32).reshape(-1, LANES) for ref in (zero_ref, one_ref, two_ref)]
    weight_out[...] = jnp.concatenate(parts + [blank], axis=0).astype(BF)


def edge_in_kernel(h_ref, node_ref, near_ref, far_ref, src_ref, wig_ref, x_ref, rot, gathered):
    h = h_ref[0]
    src = src_ref[...]
    own, before, after = source_hots(src)
    gathered[...] = mm(node_ref[...], own)
    rot[...] = wig_ref[...].astype(F32)
    far = far_ref[...]
    from_before = jnp.where(h == 0, far, near_ref[:112])
    from_after = jnp.where(h == 0, near_ref[112:], far)
    for q in range(4):
        part = mm(from_before, before[q]) + mm(from_after, after[q])
        for g in range(13):
            coef = 4 * g + q
            if coef < 49:
                gathered[coef * 8 : coef * 8 + 8, :] += part[g * 8 : g * 8 + 8]
    rows = {}
    for degree in range(7):
        span = 2 * degree + 1
        vals = [gathered[(degree * degree + j) * 8 : (degree * degree + j + 1) * 8, :] for j in range(span)]
        for m in orders(degree):
            total = None
            for j in range(span):
                at = wig_row(degree, m, j)
                term = rot[at : at + 1, :] * vals[j]
                total = term if total is None else total + term
            rows[kept_row(degree, m)] = total
    blank = jnp.zeros((8, EB), F32)
    groups = [
        (0, [rows[r] for r in range(7)] + [blank]),
        (64, [rows[r] for r in range(7, 13)]),
        (112, [rows[r] for r in range(13, 19)]),
        (160, [rows[r] for r in range(19, 24)] + [blank]),
        (208, [rows[r] for r in range(24, 29)] + [blank]),
    ]
    for start, members in groups:
        x_ref[start : start + 8 * len(members), :] = jnp.concatenate(members, axis=0).astype(BF)


def weight_kernel(k_ref, own_ref, sib_ref, zero_ref, one_ref, two_ref):
    k = k_ref[0]
    chan, lane = iota((LANES, LANES), 0), iota((LANES, LANES), 1)

    def pick(offset):
        spot = lane - offset
        block = (spot // 8 % 2) * 4 + spot // 16
        wanted = block * 16 + k * 8 + spot % 8
        return hot((spot >= 0) & (spot < 64) & (chan == wanted))

    low, high = pick(0), pick(64)
    own, sib = own_ref[...], sib_ref[...]
    sides = [(mm(own, low), mm(own, high)), (mm(sib, low), mm(sib, high))]

    def tile(entries, place):
        halves = []
        for side in sides:
            total = None
            for half, entry in enumerate(entries):
                if entry is None:
                    continue
                sign, at = entry
                piece = side[half][at * 8 : at * 8 + 8]
                piece = piece if sign > 0 else -piece
                total = piece if total is None else total + piece
            halves.append(total)
        return jnp.concatenate(halves, axis=0).astype(BF)

    for lp in range(7):
        for p in range(4):
            entries = [
                (1, lp * 7 + ZORD[n]) if n < 7 else None for n in (2 * p, 2 * p + 1)
            ]
            zero_ref[lp * 16 : lp * 16 + 16, p * 128 : p * 128 + 128] = tile(entries, p)
    for ref, count, base in ((one_ref, 6, 49), (two_ref, 5, 121)):
        for out in range(2):
            for lp in range(count):
                for p in range(count):
                    entries = []
                    for n in (2 * p, 2 * p + 1):
                        inp, l = n // count, n % count
                        which = 0 if inp == out else 1
                        sign = -1 if (out == 1 and inp == 0) else 1
                        entries.append((sign, base + which * count * count + lp * count + l))
                    row = (out * count + lp) * 16
                    ref[row : row + 16, p * 128 : p * 128 + 128] = tile(entries, p)


def rotate_pair(z, near_ref, far_ref, dest, rot, gathered, store):
    gathered[z // 4] = mm(near_ref[...], dest)
    gathered[1 - z // 4] = mm(far_ref[...], dest)
    for half in range(EB // LANES):
        lanes = slice(half * LANES, half * LANES + LANES)
        for degree in range(7):
            span = 2 * degree + 1
            at0 = degree * degree
            cols = [
                [gathered[side, (at0 + j) * 8 : (at0 + j + 1) * 8, lanes] for j in range(span)]
                for side in range(2)
            ]
            for m in orders(degree):
                totals = [None, None]
                for j in range(span):
                    at = wig_row(degree, m, j)
                    coeff = jnp.broadcast_to(rot[at : at + 1, lanes], (8, LANES))
                    for side in range(2):
                        term = coeff * cols[side][j]
                        totals[side] = term if totals[side] is None else totals[side] + term
                place = eg_place(kept_row(degree, m))
                store(place, lanes, jnp.concatenate(totals, axis=0).astype(BF))


def edge_factor(step, count_ref, scale_ref):
    slot = step * EB + iota((1, EB), 1)
    return jnp.where(slot < count_ref[0], 0.25 * scale_ref[...], 0.0)


def rotate_kernel(z_ref, count_ref, near_ref, far_ref, dst_ref, scale_ref, wig_ref, eg_ref, gathered, rot):
    rot[...] = wig_ref[...].astype(F32) * edge_factor(pl.program_id(0), count_ref, scale_ref)
    dest = hot(iota((LANES, EB), 0) == dst_ref[...])

    def store(place, lanes, tile):
        eg_ref[place * 16 : place * 16 + 16, lanes] = tile

    rotate_pair(z_ref[0], near_ref, far_ref, dest, rot, gathered, store)


def edge_kernel(
    z_ref, count_ref, eg0, eg2, eg1, near_ref, far_ref,
    dst_ref, src_ref, scale_ref, wig_ref, xo_ref, xs_ref, zero_ref, one_ref, two_ref,
    so_ref, go_ref, sib_ref,
    gathered, rot, plain, eg, acc, back, full, atoms, rims,
):
    step = pl.program_id(0)

    @pl.when(step == 0)
    def _():
        acc[...] = jnp.zeros_like(acc)
        atoms[...] = jnp.zeros_like(atoms)
        rims[...] = jnp.zeros_like(rims)

    z = z_ref[0]
    entries = wig_ref[...].astype(F32)
    plain[...] = entries
    rot[...] = entries * edge_factor(step, count_ref, scale_ref)
    dest = hot(iota((LANES, EB), 0) == dst_ref[...])

    def rows_of(place, n):
        return pl.ds(pl.multiple_of(place * 64 + ((z % 4) ^ n) * 16, 16), 16)

    def store(place, lanes, tile):
        eg[rows_of(place, 3), lanes] = tile

    rotate_pair(z, near_ref, far_ref, dest, rot, gathered, store)
    for n, ref in ((0, eg0), (2, eg2), (1, eg1)):
        for place in range(29):
            eg[rows_of(place, n), :] = ref[place * 16 : place * 16 + 16]

    def stacked(*pieces):
        return jnp.concatenate(pieces, axis=0)

    def blank(rows):
        return jnp.zeros((rows, EB), BF)

    xo, xs = xo_ref[...], xs_ref[...]
    acc[0:448] += mm(eg[0:448], stacked(xo[:64], blank(64), xs[:64], blank(64)), NT)
    for start, count, plus, minus in ((448, 6, 64, 112), (1216, 5, 160, 208)):
        ahead = stacked(
            xo[plus : plus + 48], -xo[minus : minus + 48], blank(32),
            xs[plus : plus + 48], -xs[minus : minus + 48], blank(32),
        )
        cross = stacked(
            xo[minus : minus + 48], xo[plus : plus + 48], blank(32),
            xs[minus : minus + 48], xs[plus : plus + 48], blank(32),
        )
        size = count * 64
        at = 448 if count == 6 else 832
        acc[at : at + size] += mm(eg[start : start + size], ahead, NT) + mm(
            eg[start + size : start + 2 * size], cross, NT
        )

    back[0:112] = mm(zero_ref[:, 0:448], eg[0:448])
    back[112:304] = mm(one_ref[...], eg[448:1216])
    back[304:464] = mm(two_ref[...], eg[1216:1856])
    quarter_start = (0, 13, 25, 37)
    for half in range(EB // LANES):
        lanes = slice(half * LANES, half * LANES + LANES)
        for degree in range(7):
            vals_m = {
                m: back[kept_row(degree, m) * 16 : kept_row(degree, m) * 16 + 16, lanes]
                for m in orders(degree)
            }
            for j in range(2 * degree + 1):
                total = None
                for m in orders(degree):
                    at = wig_row(degree, m, j)
                    term = plain[at : at + 1, lanes] * vals_m[m]
                    total = term if total is None else total + term
                coef = degree * degree + j
                row = (quarter_start[coef % 4] + coef // 4) * 16
                full[row : row + 16, lanes] = total.astype(BF)
    own, before, after = source_hots(src_ref[...])
    for q in range(4):
        start, size = quarter_start[q] * 16, (13 if q == 0 else 12) * 16
        rows = full[start : start + size]
        atoms[start : start + size] += mm(rows, own, NT)
        rims[0:size] += mm(rows, jnp.concatenate([before[q], after[q]], axis=0), NT)

    @pl.when(step == pl.num_programs(0) - 1)
    def _():
        for zb in range(8):
            tiles = []
            spot = zb % 4 * 16 + zb // 4 * 8
            for t in range(4):
                tile = acc[t * 64 + spot : t * 64 + spot + 8]
                if t < 3:
                    odd = acc[256 + t * 64 + spot : 256 + t * 64 + spot + 8]
                    halves = [pltpu.roll(odd[:, n : n + LANES], 64, 1) for n in (0, LANES)]
                    tile = tile + jnp.concatenate(halves, axis=1)
                tiles.append(tile)
            for n in range(11):
                tiles.append(acc[448 + n * 64 + spot : 448 + n * 64 + spot + 8])
            tiles.append(jnp.zeros((8, 2 * LANES), F32))
            whole_tile = jnp.concatenate(tiles, axis=0).astype(BF)
            so_ref[zb * 128 : zb * 128 + 128] = whole_tile[:, :LANES]
            sib_ref[zb * 128 : zb * 128 + 128] = whole_tile[:, LANES:]
        for side in range(2):
            tiles = []
            for coef in range(49):
                row = (quarter_start[coef % 4] + coef // 4) * 16 + side * 8
                tiles.append(atoms[row : row + 8])
            tiles.append(jnp.zeros((8, LANES), F32))
            for rim in range(2):
                for g in range(13):
                    row = g * 16 + side * 8
                    tiles.append(rims[row : row + 8, rim * LANES : rim * LANES + LANES])
                tiles.append(jnp.zeros((8, LANES), F32))
            if side == 0:
                go_ref[...] = jnp.concatenate(tiles, axis=0)
            else:
                sib_ref[1024:1648] = jnp.concatenate(tiles, axis=0).astype(BF)


def row_spec():
    return pl.BlockSpec((1, EB), lambda i: (0, i))


def wig_spec():
    return pl.BlockSpec((235, EB), lambda i: (0, i))


def rotate_call(z_s, edge_count, pair, dst, scale, wigner):
    slots = dst.shape[1]
    return pl.pallas_call(
        rotate_kernel,
        out_shape=sds((464, slots), BF),
        grid=(slots // EB,),
        in_specs=[smem(), smem(), whole((400, 128)), whole((400, 128)), row_spec(), row_spec(), wig_spec()],
        out_specs=pl.BlockSpec((464, EB), lambda i: (0, i)),
        scratch_shapes=[pltpu.VMEM((2, 400, EB), F32), pltpu.VMEM((235, EB), F32)],
        compiler_params=params(),
        name="rotate",
    )(z_s, edge_count, *pair, dst, scale, wigner)


def edge_call(z_s, edge_count, egs, pair, dst, src, scale, wigner, x_own, x_sib, weights):
    slots = dst.shape[1]
    x_spec = pl.BlockSpec((256, EB), lambda i: (0, i))
    return pl.pallas_call(
        edge_kernel,
        out_shape=(sds((1024, 128), BF), sds((624, 128), F32), sds((1648, 128), BF)),
        grid=(slots // EB,),
        in_specs=[smem(), smem()]
        + [pl.BlockSpec((464, EB), lambda i: (0, i))] * 3
        + [whole((400, 128)), whole((400, 128)), row_spec(), row_spec(), row_spec(), wig_spec(), x_spec, x_spec]
        + [whole((112, 512)), whole((192, 768)), whole((160, 640))],
        out_specs=(whole((1024, 128)), whole((624, 128)), whole((1648, 128))),
        scratch_shapes=[
            pltpu.VMEM((2, 400, EB), F32),
            pltpu.VMEM((235, EB), F32),
            pltpu.VMEM((235, EB), F32),
            pltpu.VMEM((1856, EB), BF),
            pltpu.VMEM((1152, 256), F32),
            pltpu.VMEM((464, EB), F32),
            pltpu.VMEM((784, EB), BF),
            pltpu.VMEM((784, LANES), F32),
            pltpu.VMEM((208, 2 * LANES), F32),
        ],
        compiler_params=params(),
        name="edge",
    )(z_s, edge_count, *egs, *pair, dst, src, scale, wigner, x_own, x_sib, *weights)


def finish_kernel(mine_ref, got_ref, zero_ref, one_ref, two_ref):
    total = mine_ref[...] + got_ref[224:288].astype(F32)

    def moved(lane):
        return total if lane == 0 else pltpu.roll(total, LANES - lane, 1)

    for lp in range(7):
        even, odd = moved(lp * 8), moved(64 + lp * 8)
        for n, l in enumerate(ZORD):
            source, row = (even, n * 4) if n < 4 else (odd, (n - 4) * 4)
            zero_ref[lp, l] = source[row : row + 4, 0:8]
    for ref, count, first, stride in ((one_ref, 6, 4, 48), (two_ref, 5, 10, 48)):
        for w in range(2):
            for lp in range(count):
                source = moved(w * stride + lp * 8)
                for l in range(count):
                    row = (first + l) * 4
                    ref[w, lp, l] = source[row : row + 4, 0:8]


def join_kernel(h_ref, own_ref, rim_ref, out_ref):
    h = h_ref[0]
    base_a = jnp.where(h == 0, 96, 0)
    base_b = 96 - base_a
    lane, atom = iota((LANES, LANES), 0), iota((LANES, LANES), 1)
    ra, rb = rim_ref[0:112], rim_ref[112:224]
    for q in range(4):
        inside = (lane >= 32 * q) & (lane < 32 * q + 32)
        put_a = hot(inside & (atom == lane - 32 * q + base_a))
        put_b = hot(inside & (atom == lane - 32 * q + base_b))
        part = mm(ra, put_a) + mm(rb, put_b)
        for g in range(13):
            coef = 4 * g + q
            if coef < 49:
                out_ref[coef] = own_ref[coef * 8 : coef * 8 + 8] + part[g * 8 : g * 8 + 8]


def smem():
    return pl.BlockSpec(memory_space=pltpu.SMEM)


def params():
    return pltpu.CompilerParams(vmem_limit_bytes=VMEM_LIMIT)


def light():
    return pl.CostEstimate(flops=1, bytes_accessed=1, transcendentals=0)


def whole(shape):
    return pl.BlockSpec(shape, lambda *_: (0,) * len(shape))


def sds(shape, dtype):
    return jax.ShapeDtypeStruct(shape, dtype)


def body(
    node_x, cotangent, wigner, src_index, dst_index, edge_scale, edge_count, w_zero, w_one, w_two
):
    chan = lax.axis_index("chan")
    brick = lax.axis_index("brick")
    z, core = chan // 2, chan % 2
    high = brick % 2
    z_s = z.astype(jnp.int32).reshape(1)
    k_s = core.astype(jnp.int32).reshape(1)
    h_s = high.astype(jnp.int32).reshape(1)
    slots = src_index.shape[0]
    steps = slots // EB
    src = src_index.reshape(1, slots)
    dst = dst_index.reshape(1, slots)
    scale = edge_scale.reshape(1, slots)

    def across(x, mask):
        return lax.ppermute(x, "chan", [(i, i ^ mask) for i in range(16)])

    def cross(x):
        return lax.ppermute(x, "brick", [(i, i ^ 1) for i in range(32)])

    def shift(x, away):
        route = [(i, (i + (2 if (i % 2 == 0) == away else -2)) % 32) for i in range(32)]
        return lax.ppermute(x, "brick", route)

    w_tiles = (
        w_zero.transpose(0, 2, 1, 3).reshape(49, 8, 128),
        w_one.transpose(0, 1, 3, 2, 4).reshape(72, 8, 128),
        w_two.transpose(0, 1, 3, 2, 4).reshape(50, 8, 128),
    )
    node, b0, rims, w_own = pl.pallas_call(
        pack_kernel,
        out_shape=(sds((400, 128), BF), sds((400, 128), BF), sds((224, 128), BF), sds((1376, 128), BF)),
        in_specs=[whole((n, 8, 128)) for n in (49, 49, 49, 72, 50)],
        out_specs=(whole((400, 128)), whole((400, 128)), whole((224, 128)), whole((1376, 128))),
        grid=(1,),
        compiler_params=pltpu.CompilerParams(vmem_limit_bytes=PACK_VMEM),
        cost_estimate=light(),
        name="pack",
    )(node_x, cotangent, *w_tiles)
    near = cross(rims)

    def rotated(*pair):
        return rotate_call(z_s, edge_count, pair, dst, scale, wigner)

    b4 = across(b0, 8)
    b2 = across(b0, 4)
    b1 = across(b0, 2)
    b4, b2, b1, near, w_own = lax.optimization_barrier((b4, b2, b1, near, w_own))
    b6 = across(b4, 4)
    b5 = across(b4, 2)
    b3 = across(b2, 2)
    far = shift(lax.dynamic_slice_in_dim(near, 112 * high, 112, 0), True)
    eg0 = rotated(b0, b4)
    far, eg0 = lax.optimization_barrier((far, eg0))

    w_sib = across(w_own, 1)
    wz, wo, wt = pl.pallas_call(
        weight_kernel,
        out_shape=(sds((112, 512), BF), sds((192, 768), BF), sds((160, 640), BF)),
        grid=(1,),
        in_specs=[smem(), whole((1376, 128)), whole((1376, 128))],
        out_specs=(whole((112, 512)), whole((192, 768)), whole((160, 640))),
        compiler_params=params(),
        cost_estimate=light(),
        name="weights",
    )(k_s, w_own, w_sib)

    x_spec = pl.BlockSpec((256, EB), lambda i: (0, i))
    x_own = pl.pallas_call(
        edge_in_kernel,
        out_shape=sds((256, slots), BF),
        grid=(steps,),
        in_specs=[smem(), whole((400, 128)), whole((224, 128)), whole((112, 128)), row_spec(), wig_spec()],
        out_specs=x_spec,
        scratch_shapes=[pltpu.VMEM((235, EB), F32), pltpu.VMEM((400, EB), F32)],
        compiler_params=params(),
        cost_estimate=light(),
        name="edge_in",
    )(h_s, node, near, far, src, wigner)
    b6, b5, b3, x_own, eg0, wz, wo, wt = lax.optimization_barrier(
        (b6, b5, b3, x_own, eg0, wz, wo, wt)
    )
    b7 = across(b6, 2)
    eg2 = rotated(b2, b6)
    eg1 = rotated(b1, b5)
    x_sib = across(x_own, 1)

    s_own, g_own, to_sib = edge_call(
        z_s, edge_count, (eg0, eg2, eg1), (b3, b7), dst, src, scale, wigner, x_own, x_sib, (wz, wo, wt)
    )

    got = across(to_sib, 1)
    s_got = got[:1024].reshape(8, 128, 128)
    s_own = s_own.reshape(8, 128, 128)
    is_even = core == 0
    send = jnp.concatenate([jnp.where(is_even, s_own, s_got), jnp.where(is_even, s_got, s_own)], axis=0)
    groups = [[2 * (2 * zb + p) + h for p in range(2) for zb in range(8)] for h in range(2)]
    pieces = lax.all_to_all(send, "brick", 0, 0, axis_index_groups=groups)
    summed = pieces.astype(F32).sum(axis=0).reshape(16, 2, 4, 128)
    mine = jnp.where(high == 0, summed[:, 0], summed[:, 1])
    other = jnp.where(high == 0, summed[:, 1], summed[:, 0])

    g_all = g_own + got[1024:].astype(F32)
    left, right = g_all[400:512].astype(BF), g_all[512:624].astype(BF)
    near_rim = jnp.where(high == 0, right, left)
    far_rim = shift(jnp.where(high == 0, left, right), False)

    crossed = cross(jnp.concatenate([near_rim, far_rim, other.astype(BF).reshape(64, 128)], axis=0))
    grad_x = pl.pallas_call(
        join_kernel,
        out_shape=sds((49, 8, 128), F32),
        grid=(1,),
        in_specs=[smem(), whole((624, 128)), whole((288, 128))],
        out_specs=whole((49, 8, 128)),
        compiler_params=params(),
        cost_estimate=light(),
        name="join",
    )(h_s, g_all, crossed)

    zero, one, second = pl.pallas_call(
        finish_kernel,
        out_shape=(sds((7, 7, 4, 8), F32), sds((2, 6, 6, 4, 8), F32), sds((2, 5, 5, 4, 8), F32)),
        grid=(1,),
        in_specs=[whole((64, 128)), whole((288, 128))],
        out_specs=(whole((7, 7, 4, 8)), whole((2, 6, 6, 4, 8)), whole((2, 5, 5, 4, 8))),
        compiler_params=params(),
        cost_estimate=light(),
        name="finish",
    )(mine.reshape(64, 128), crossed)
    grad_zero = zero.transpose(0, 3, 1, 2)
    grad_one = one.transpose(0, 1, 4, 2, 3)
    grad_two = second.transpose(0, 1, 4, 2, 3)
    return grad_x, grad_zero, grad_one, grad_two


def solution(mesh):
    in_specs = (
        P(None, "chan", "brick"),
        P(None, "chan", "brick"),
        P(None, "brick"),
        P("brick"),
        P("brick"),
        P("brick"),
        P("brick"),
        P(None, "chan", None, None),
        P(None, None, "chan", None, None),
        P(None, None, "chan", None, None),
    )
    out_specs = (
        P(None, "chan", "brick"),
        P(None, "chan", None, "brick"),
        P(None, None, "chan", None, "brick"),
        P(None, None, "chan", None, "brick"),
    )
    return jax.shard_map(body, mesh=mesh, in_specs=in_specs, out_specs=out_specs, check_vma=False)
```

```python
import functools

import jax
import jax.numpy as jnp
from jax import lax
from jax.experimental import pallas as pl
from jax.experimental.pallas import tpu as pltpu
from jax.sharding import PartitionSpec as P

BF = jnp.bfloat16
F32 = jnp.float32
EB = 256
LANES = 128
VMEM_LIMIT = 28 * 1024 * 1024
PACK_VMEM = 60 * 1024 * 1024
ZORD = (0, 2, 4, 6, 1, 3, 5)

NN = (((1,), (0,)), ((), ()))
NT = (((1,), (1,)), ((), ()))


def mm(a, b, dims=NN):
    return lax.dot_general(a, b, dims, preferred_element_type=F32)


def kept_row(degree, azimuth):
    if azimuth == 0:
        return degree
    if azimuth == 1:
        return 6 + degree
    if azimuth == -1:
        return 12 + degree
    if azimuth == 2:
        return 17 + degree
    return 22 + degree


def wig_row(degree, azimuth, column):
    start = sum((2 * min(k, 2) + 1) * (2 * k + 1) for k in range(degree))
    return start + (azimuth + min(degree, 2)) * (2 * degree + 1) + column


def orders(degree):
    reach = min(degree, 2)
    return range(-reach, reach + 1)


def eg_place(row):
    return ZORD.index(row) if row < 7 else row


def x_place(row):
    if row < 7:
        return row * 8
    if row < 13:
        return 64 + (row - 7) * 8
    if row < 19:
        return 112 + (row - 13) * 8
    if row < 24:
        return 160 + (row - 19) * 8
    return 208 + (row - 24) * 8


def iota(shape, axis):
    return lax.broadcasted_iota(jnp.int32, shape, axis)


def hot(match):
    return jnp.where(match, 1.0, 0.0).astype(BF)


def source_hots(src):
    width = src.shape[1]
    atom = iota((LANES, width), 0)
    own = hot(atom == src - 32)
    before = [hot(atom == jnp.where(src < 32, src + 32 * q, -1)) for q in range(4)]
    after = [hot(atom == jnp.where(src >= 160, src - 160 + 32 * q, -1)) for q in range(4)]
    return own, before, after


def pack_kernel(node_ref, cot_ref, zero_ref, one_ref, two_ref, node_out, cot_out, rim_out, weight_out):
    blank = jnp.zeros((8, LANES), F32)

    def rows(ref):
        return jnp.concatenate([ref[...].astype(F32).reshape(392, LANES), blank], axis=0).astype(BF)

    cot_out[...] = rows(cot_ref)
    node = rows(node_ref)
    node_out[...] = node
    atom, lane = iota((LANES, LANES), 0), iota((LANES, LANES), 1)
    parts = []
    for q in range(4):
        inside = (lane >= 32 * q) & (lane < 32 * q + 32)
        last = hot(inside & (atom == lane - 32 * q + 96))
        first = hot(inside & (atom == lane - 32 * q))
        parts.append(mm(node, jnp.concatenate([last, first], axis=1)))
    total = []
    for g in range(13):
        members = [parts[q][(4 * g + q) * 8 : (4 * g + q) * 8 + 8] for q in range(4) if 4 * g + q < 49]
        total.append(sum(members[1:], members[0]))
    total.append(jnp.zeros((8, 2 * LANES), F32))
    packed = jnp.concatenate(total, axis=0).astype(BF)
    rim_out[:112] = packed[:, :LANES]
    rim_out[112:] = packed[:, LANES:]
    parts = [ref[...].astype(F32).reshape(-1, LANES) for ref in (zero_ref, one_ref, two_ref)]
    weight_out[...] = jnp.concatenate(parts + [blank], axis=0).astype(BF)


def edge_in_kernel(h_ref, node_ref, near_ref, far_ref, src_ref, wig_ref, x_ref, rot, gathered):
    h = h_ref[0]
    src = src_ref[...]
    own, before, after = source_hots(src)
    gathered[...] = mm(node_ref[...], own)
    rot[...] = wig_ref[...].astype(F32)
    far = far_ref[...]
    from_before = jnp.where(h == 0, far, near_ref[:112])
    from_after = jnp.where(h == 0, near_ref[112:], far)
    for q in range(4):
        part = mm(from_before, before[q]) + mm(from_after, after[q])
        for g in range(13):
            coef = 4 * g + q
            if coef < 49:
                gathered[coef * 8 : coef * 8 + 8, :] += part[g * 8 : g * 8 + 8]
    rows = {}
    for degree in range(7):
        span = 2 * degree + 1
        vals = [gathered[(degree * degree + j) * 8 : (degree * degree + j + 1) * 8, :] for j in range(span)]
        for m in orders(degree):
            total = None
            for j in range(span):
                at = wig_row(degree, m, j)
                term = rot[at : at + 1, :] * vals[j]
                total = term if total is None else total + term
            rows[kept_row(degree, m)] = total
    blank = jnp.zeros((8, EB), F32)
    groups = [
        (0, [rows[r] for r in range(7)] + [blank]),
        (64, [rows[r] for r in range(7, 13)]),
        (112, [rows[r] for r in range(13, 19)]),
        (160, [rows[r] for r in range(19, 24)] + [blank]),
        (208, [rows[r] for r in range(24, 29)] + [blank]),
    ]
    for start, members in groups:
        x_ref[start : start + 8 * len(members), :] = jnp.concatenate(members, axis=0).astype(BF)


def weight_kernel(k_ref, own_ref, sib_ref, zero_ref, one_ref, two_ref):
    k = k_ref[0]
    chan, lane = iota((LANES, LANES), 0), iota((LANES, LANES), 1)

    def pick(offset):
        spot = lane - offset
        block = (spot // 8 % 2) * 4 + spot // 16
        wanted = block * 16 + k * 8 + spot % 8
        return hot((spot >= 0) & (spot < 64) & (chan == wanted))

    low, high = pick(0), pick(64)
    own, sib = own_ref[...], sib_ref[...]
    sides = [(mm(own, low), mm(own, high)), (mm(sib, low), mm(sib, high))]

    def tile(entries, place):
        halves = []
        for side in sides:
            total = None
            for half, entry in enumerate(entries):
                if entry is None:
                    continue
                sign, at = entry
                piece = side[half][at * 8 : at * 8 + 8]
                piece = piece if sign > 0 else -piece
                total = piece if total is None else total + piece
            halves.append(total)
        return jnp.concatenate(halves, axis=0).astype(BF)

    for lp in range(7):
        for p in range(4):
            entries = [
                (1, lp * 7 + ZORD[n]) if n < 7 else None for n in (2 * p, 2 * p + 1)
            ]
            zero_ref[lp * 16 : lp * 16 + 16, p * 128 : p * 128 + 128] = tile(entries, p)
    for ref, count, base in ((one_ref, 6, 49), (two_ref, 5, 121)):
        for out in range(2):
            for lp in range(count):
                for p in range(count):
                    entries = []
                    for n in (2 * p, 2 * p + 1):
                        inp, l = n // count, n % count
                        which = 0 if inp == out else 1
                        sign = -1 if (out == 1 and inp == 0) else 1
                        entries.append((sign, base + which * count * count + lp * count + l))
                    row = (out * count + lp) * 16
                    ref[row : row + 16, p * 128 : p * 128 + 128] = tile(entries, p)


def rotate_pair(z, near_ref, far_ref, dest, rot, gathered, store):
    gathered[z // 4] = mm(near_ref[...], dest)
    gathered[1 - z // 4] = mm(far_ref[...], dest)
    for half in range(EB // LANES):
        lanes = slice(half * LANES, half * LANES + LANES)
        for degree in range(7):
            span = 2 * degree + 1
            at0 = degree * degree
            cols = [
                [gathered[side, (at0 + j) * 8 : (at0 + j + 1) * 8, lanes] for j in range(span)]
                for side in range(2)
            ]
            for m in orders(degree):
                totals = [None, None]
                for j in range(span):
                    at = wig_row(degree, m, j)
                    coeff = jnp.broadcast_to(rot[at : at + 1, lanes], (8, LANES))
                    for side in range(2):
                        term = coeff * cols[side][j]
                        totals[side] = term if totals[side] is None else totals[side] + term
                place = eg_place(kept_row(degree, m))
                store(place, lanes, jnp.concatenate(totals, axis=0).astype(BF))


def edge_factor(step, count_ref, scale_ref):
    slot = step * EB + iota((1, EB), 1)
    return jnp.where(slot < count_ref[0], 0.25 * scale_ref[...], 0.0)


def rotate_kernel(z_ref, count_ref, near_ref, far_ref, dst_ref, scale_ref, wig_ref, eg_ref, gathered, rot):
    rot[...] = wig_ref[...].astype(F32) * edge_factor(pl.program_id(0), count_ref, scale_ref)
    dest = hot(iota((LANES, EB), 0) == dst_ref[...])

    def store(place, lanes, tile):
        eg_ref[place * 16 : place * 16 + 16, lanes] = tile

    rotate_pair(z_ref[0], near_ref, far_ref, dest, rot, gathered, store)


def edge_kernel(
    z_ref, count_ref, eg0, eg2, eg1, near_ref, far_ref,
    dst_ref, src_ref, scale_ref, wig_ref, xo_ref, xs_ref, zero_ref, one_ref, two_ref,
    so_ref, go_ref, sib_ref,
    gathered, rot, plain, eg, acc, back, full, atoms, rims,
):
    step = pl.program_id(0)

    @pl.when(step == 0)
    def _():
        acc[...] = jnp.zeros_like(acc)
        atoms[...] = jnp.zeros_like(atoms)
        rims[...] = jnp.zeros_like(rims)

    z = z_ref[0]
    entries = wig_ref[...].astype(F32)
    plain[...] = entries
    rot[...] = entries * edge_factor(step, count_ref, scale_ref)
    dest = hot(iota((LANES, EB), 0) == dst_ref[...])

    def rows_of(place, n):
        return pl.ds(pl.multiple_of(place * 64 + ((z % 4) ^ n) * 16, 16), 16)

    def store(place, lanes, tile):
        eg[rows_of(place, 3), lanes] = tile

    rotate_pair(z, near_ref, far_ref, dest, rot, gathered, store)
    for n, ref in ((0, eg0), (2, eg2), (1, eg1)):
        for place in range(29):
            eg[rows_of(place, n), :] = ref[place * 16 : place * 16 + 16]

    def stacked(*pieces):
        return jnp.concatenate(pieces, axis=0)

    def blank(rows):
        return jnp.zeros((rows, EB), BF)

    xo, xs = xo_ref[...], xs_ref[...]
    acc[0:448] += mm(eg[0:448], stacked(xo[:64], blank(64), xs[:64], blank(64)), NT)
    for start, count, plus, minus in ((448, 6, 64, 112), (1216, 5, 160, 208)):
        ahead = stacked(
            xo[plus : plus + 48], -xo[minus : minus + 48], blank(32),
            xs[plus : plus + 48], -xs[minus : minus + 48], blank(32),
        )
        cross = stacked(
            xo[minus : minus + 48], xo[plus : plus + 48], blank(32),
            xs[minus : minus + 48], xs[plus : plus + 48], blank(32),
        )
        size = count * 64
        at = 448 if count == 6 else 832
        acc[at : at + size] += mm(eg[start : start + size], ahead, NT) + mm(
            eg[start + size : start + 2 * size], cross, NT
        )

    back[0:112] = mm(zero_ref[:, 0:448], eg[0:448])
    back[112:304] = mm(one_ref[...], eg[448:1216])
    back[304:464] = mm(two_ref[...], eg[1216:1856])
    quarter_start = (0, 13, 25, 37)
    for half in range(EB // LANES):
        lanes = slice(half * LANES, half * LANES + LANES)
        for degree in range(7):
            vals_m = {
                m: back[kept_row(degree, m) * 16 : kept_row(degree, m) * 16 + 16, lanes]
                for m in orders(degree)
            }
            for j in range(2 * degree + 1):
                total = None
                for m in orders(degree):
                    at = wig_row(degree, m, j)
                    term = plain[at : at + 1, lanes] * vals_m[m]
                    total = term if total is None else total + term
                coef = degree * degree + j
                row = (quarter_start[coef % 4] + coef // 4) * 16
                full[row : row + 16, lanes] = total.astype(BF)
    own, before, after = source_hots(src_ref[...])
    for q in range(4):
        start, size = quarter_start[q] * 16, (13 if q == 0 else 12) * 16
        rows = full[start : start + size]
        atoms[start : start + size] += mm(rows, own, NT)
        rims[0:size] += mm(rows, jnp.concatenate([before[q], after[q]], axis=0), NT)

    @pl.when(step == pl.num_programs(0) - 1)
    def _():
        for zb in range(8):
            tiles = []
            spot = zb % 4 * 16 + zb // 4 * 8
            for t in range(4):
                tile = acc[t * 64 + spot : t * 64 + spot + 8]
                if t < 3:
                    odd = acc[256 + t * 64 + spot : 256 + t * 64 + spot + 8]
                    halves = [pltpu.roll(odd[:, n : n + LANES], 64, 1) for n in (0, LANES)]
                    tile = tile + jnp.concatenate(halves, axis=1)
                tiles.append(tile)
            for n in range(11):
                tiles.append(acc[448 + n * 64 + spot : 448 + n * 64 + spot + 8])
            tiles.append(jnp.zeros((8, 2 * LANES), F32))
            whole_tile = jnp.concatenate(tiles, axis=0).astype(BF)
            so_ref[zb * 128 : zb * 128 + 128] = whole_tile[:, :LANES]
            sib_ref[zb * 128 : zb * 128 + 128] = whole_tile[:, LANES:]
        for side in range(2):
            tiles = []
            for coef in range(49):
                row = (quarter_start[coef % 4] + coef // 4) * 16 + side * 8
                tiles.append(atoms[row : row + 8])
            tiles.append(jnp.zeros((8, LANES), F32))
            for rim in range(2):
                for g in range(13):
                    row = g * 16 + side * 8
                    tiles.append(rims[row : row + 8, rim * LANES : rim * LANES + LANES])
                tiles.append(jnp.zeros((8, LANES), F32))
            if side == 0:
                go_ref[...] = jnp.concatenate(tiles, axis=0)
            else:
                sib_ref[1024:1648] = jnp.concatenate(tiles, axis=0).astype(BF)


def row_spec():
    return pl.BlockSpec((1, EB), lambda i: (0, i))


def wig_spec():
    return pl.BlockSpec((235, EB), lambda i: (0, i))


def rotate_call(z_s, edge_count, pair, dst, scale, wigner):
    slots = dst.shape[1]
    return pl.pallas_call(
        rotate_kernel,
        out_shape=sds((464, slots), BF),
        grid=(slots // EB,),
        in_specs=[smem(), smem(), whole((400, 128)), whole((400, 128)), row_spec(), row_spec(), wig_spec()],
        out_specs=pl.BlockSpec((464, EB), lambda i: (0, i)),
        scratch_shapes=[pltpu.VMEM((2, 400, EB), F32), pltpu.VMEM((235, EB), F32)],
        compiler_params=params(),
        name="rotate",
    )(z_s, edge_count, *pair, dst, scale, wigner)


def edge_call(z_s, edge_count, egs, pair, dst, src, scale, wigner, x_own, x_sib, weights):
    slots = dst.shape[1]
    x_spec = pl.BlockSpec((256, EB), lambda i: (0, i))
    return pl.pallas_call(
        edge_kernel,
        out_shape=(sds((1024, 128), BF), sds((624, 128), F32), sds((1648, 128), BF)),
        grid=(slots // EB,),
        in_specs=[smem(), smem()]
        + [pl.BlockSpec((464, EB), lambda i: (0, i))] * 3
        + [whole((400, 128)), whole((400, 128)), row_spec(), row_spec(), row_spec(), wig_spec(), x_spec, x_spec]
        + [whole((112, 512)), whole((192, 768)), whole((160, 640))],
        out_specs=(whole((1024, 128)), whole((624, 128)), whole((1648, 128))),
        scratch_shapes=[
            pltpu.VMEM((2, 400, EB), F32),
            pltpu.VMEM((235, EB), F32),
            pltpu.VMEM((235, EB), F32),
            pltpu.VMEM((1856, EB), BF),
            pltpu.VMEM((1152, 256), F32),
            pltpu.VMEM((464, EB), F32),
            pltpu.VMEM((784, EB), BF),
            pltpu.VMEM((784, LANES), F32),
            pltpu.VMEM((208, 2 * LANES), F32),
        ],
        compiler_params=params(),
        name="edge",
    )(z_s, edge_count, *egs, *pair, dst, src, scale, wigner, x_own, x_sib, *weights)


def finish_kernel(mine_ref, got_ref, zero_ref, one_ref, two_ref):
    total = mine_ref[...] + got_ref[224:288].astype(F32)

    def moved(lane):
        return total if lane == 0 else pltpu.roll(total, LANES - lane, 1)

    for lp in range(7):
        even, odd = moved(lp * 8), moved(64 + lp * 8)
        for n, l in enumerate(ZORD):
            source, row = (even, n * 4) if n < 4 else (odd, (n - 4) * 4)
            zero_ref[lp, l] = source[row : row + 4, 0:8]
    for ref, count, first, stride in ((one_ref, 6, 4, 48), (two_ref, 5, 10, 48)):
        for w in range(2):
            for lp in range(count):
                source = moved(w * stride + lp * 8)
                for l in range(count):
                    row = (first + l) * 4
                    ref[w, lp, l] = source[row : row + 4, 0:8]


def join_kernel(h_ref, own_ref, rim_ref, out_ref):
    h = h_ref[0]
    base_a = jnp.where(h == 0, 96, 0)
    base_b = 96 - base_a
    lane, atom = iota((LANES, LANES), 0), iota((LANES, LANES), 1)
    ra, rb = rim_ref[0:112], rim_ref[112:224]
    for q in range(4):
        inside = (lane >= 32 * q) & (lane < 32 * q + 32)
        put_a = hot(inside & (atom == lane - 32 * q + base_a))
        put_b = hot(inside & (atom == lane - 32 * q + base_b))
        part = mm(ra, put_a) + mm(rb, put_b)
        for g in range(13):
            coef = 4 * g + q
            if coef < 49:
                out_ref[coef] = own_ref[coef * 8 : coef * 8 + 8] + part[g * 8 : g * 8 + 8]


def smem():
    return pl.BlockSpec(memory_space=pltpu.SMEM)


def params():
    return pltpu.CompilerParams(vmem_limit_bytes=VMEM_LIMIT)


def light():
    return pl.CostEstimate(flops=1, bytes_accessed=1, transcendentals=0)


def whole(shape):
    return pl.BlockSpec(shape, lambda *_: (0,) * len(shape))


def sds(shape, dtype):
    return jax.ShapeDtypeStruct(shape, dtype)


def body(
    node_x, cotangent, wigner, src_index, dst_index, edge_scale, edge_count, w_zero, w_one, w_two
):
    chan = lax.axis_index("chan")
    brick = lax.axis_index("brick")
    z, core = chan // 2, chan % 2
    high = brick % 2
    z_s = z.astype(jnp.int32).reshape(1)
    k_s = core.astype(jnp.int32).reshape(1)
    h_s = high.astype(jnp.int32).reshape(1)
    slots = src_index.shape[0]
    steps = slots // EB
    src = src_index.reshape(1, slots)
    dst = dst_index.reshape(1, slots)
    scale = edge_scale.reshape(1, slots)

    def across(x, mask):
        return lax.ppermute(x, "chan", [(i, i ^ mask) for i in range(16)])

    def cross(x):
        return lax.ppermute(x, "brick", [(i, i ^ 1) for i in range(32)])

    def shift(x, away):
        route = [(i, (i + (2 if (i % 2 == 0) == away else -2)) % 32) for i in range(32)]
        return lax.ppermute(x, "brick", route)

    w_tiles = (
        w_zero.transpose(0, 2, 1, 3).reshape(49, 8, 128),
        w_one.transpose(0, 1, 3, 2, 4).reshape(72, 8, 128),
        w_two.transpose(0, 1, 3, 2, 4).reshape(50, 8, 128),
    )
    node, b0, rims, w_own = pl.pallas_call(
        pack_kernel,
        out_shape=(sds((400, 128), BF), sds((400, 128), BF), sds((224, 128), BF), sds((1376, 128), BF)),
        in_specs=[whole((n, 8, 128)) for n in (49, 49, 49, 72, 50)],
        out_specs=(whole((400, 128)), whole((400, 128)), whole((224, 128)), whole((1376, 128))),
        grid=(1,),
        compiler_params=pltpu.CompilerParams(vmem_limit_bytes=PACK_VMEM),
        cost_estimate=light(),
        name="pack",
    )(node_x, cotangent, *w_tiles)
    near = cross(rims)

    def rotated(*pair):
        return rotate_call(z_s, edge_count, pair, dst, scale, wigner)

    b4 = across(b0, 8)
    b2 = across(b0, 4)
    b1 = across(b0, 2)
    far = shift(lax.dynamic_slice_in_dim(near, 112 * high, 112, 0), True)
    b4, b2, b1, far, w_own = lax.optimization_barrier((b4, b2, b1, far, w_own))
    b6 = across(b4, 4)
    b5 = across(b4, 2)
    b3 = across(b2, 2)
    eg0 = rotated(b0, b4)
    far, eg0 = lax.optimization_barrier((far, eg0))

    w_sib = across(w_own, 1)
    wz, wo, wt = pl.pallas_call(
        weight_kernel,
        out_shape=(sds((112, 512), BF), sds((192, 768), BF), sds((160, 640), BF)),
        grid=(1,),
        in_specs=[smem(), whole((1376, 128)), whole((1376, 128))],
        out_specs=(whole((112, 512)), whole((192, 768)), whole((160, 640))),
        compiler_params=params(),
        cost_estimate=light(),
        name="weights",
    )(k_s, w_own, w_sib)

    x_spec = pl.BlockSpec((256, EB), lambda i: (0, i))
    x_own = pl.pallas_call(
        edge_in_kernel,
        out_shape=sds((256, slots), BF),
        grid=(steps,),
        in_specs=[smem(), whole((400, 128)), whole((224, 128)), whole((112, 128)), row_spec(), wig_spec()],
        out_specs=x_spec,
        scratch_shapes=[pltpu.VMEM((235, EB), F32), pltpu.VMEM((400, EB), F32)],
        compiler_params=params(),
        cost_estimate=light(),
        name="edge_in",
    )(h_s, node, near, far, src, wigner)
    b6, b5, b3, x_own, eg0, wz, wo, wt = lax.optimization_barrier(
        (b6, b5, b3, x_own, eg0, wz, wo, wt)
    )
    b7 = across(b6, 2)
    eg2 = rotated(b2, b6)
    eg1 = rotated(b1, b5)
    x_sib = across(x_own, 1)

    s_own, g_own, to_sib = edge_call(
        z_s, edge_count, (eg0, eg2, eg1), (b3, b7), dst, src, scale, wigner, x_own, x_sib, (wz, wo, wt)
    )

    got = across(to_sib, 1)
    s_got = got[:1024].reshape(8, 128, 128)
    s_own = s_own.reshape(8, 128, 128)
    is_even = core == 0
    send = jnp.concatenate([jnp.where(is_even, s_own, s_got), jnp.where(is_even, s_got, s_own)], axis=0)
    groups = [[2 * (2 * zb + p) + h for p in range(2) for zb in range(8)] for h in range(2)]
    pieces = lax.all_to_all(send, "brick", 0, 0, axis_index_groups=groups)
    summed = pieces.astype(F32).sum(axis=0).reshape(16, 2, 4, 128)
    mine = jnp.where(high == 0, summed[:, 0], summed[:, 1])
    other = jnp.where(high == 0, summed[:, 1], summed[:, 0])

    g_all = g_own + got[1024:].astype(F32)
    left, right = g_all[400:512].astype(BF), g_all[512:624].astype(BF)
    near_rim = jnp.where(high == 0, right, left)
    far_rim = shift(jnp.where(high == 0, left, right), False)

    crossed = cross(jnp.concatenate([near_rim, far_rim, other.astype(BF).reshape(64, 128)], axis=0))
    grad_x = pl.pallas_call(
        join_kernel,
        out_shape=sds((49, 8, 128), F32),
        grid=(1,),
        in_specs=[smem(), whole((624, 128)), whole((288, 128))],
        out_specs=whole((49, 8, 128)),
        compiler_params=params(),
        cost_estimate=light(),
        name="join",
    )(h_s, g_all, crossed)

    zero, one, second = pl.pallas_call(
        finish_kernel,
        out_shape=(sds((7, 7, 4, 8), F32), sds((2, 6, 6, 4, 8), F32), sds((2, 5, 5, 4, 8), F32)),
        grid=(1,),
        in_specs=[whole((64, 128)), whole((288, 128))],
        out_specs=(whole((7, 7, 4, 8)), whole((2, 6, 6, 4, 8)), whole((2, 5, 5, 4, 8))),
        compiler_params=params(),
        cost_estimate=light(),
        name="finish",
    )(mine.reshape(64, 128), crossed)
    grad_zero = zero.transpose(0, 3, 1, 2)
    grad_one = one.transpose(0, 1, 4, 2, 3)
    grad_two = second.transpose(0, 1, 4, 2, 3)
    return grad_x, grad_zero, grad_one, grad_two


def solution(mesh):
    in_specs = (
        P(None, "chan", "brick"),
        P(None, "chan", "brick"),
        P(None, "brick"),
        P("brick"),
        P("brick"),
        P("brick"),
        P("brick"),
        P(None, "chan", None, None),
        P(None, None, "chan", None, None),
        P(None, None, "chan", None, None),
    )
    out_specs = (
        P(None, "chan", "brick"),
        P(None, "chan", None, "brick"),
        P(None, None, "chan", None, "brick"),
        P(None, None, "chan", None, "brick"),
    )
    return jax.shard_map(body, mesh=mesh, in_specs=in_specs, out_specs=out_specs, check_vma=False)
```

```python
import functools

import jax
import jax.numpy as jnp
from jax import lax
from jax.experimental import pallas as pl
from jax.experimental.pallas import tpu as pltpu
from jax.sharding import PartitionSpec as P

BF = jnp.bfloat16
F32 = jnp.float32
EB = 256
LANES = 128
VMEM_LIMIT = 28 * 1024 * 1024
PACK_VMEM = 60 * 1024 * 1024
ZORD = (0, 2, 4, 6, 1, 3, 5)

NN = (((1,), (0,)), ((), ()))
NT = (((1,), (1,)), ((), ()))


def mm(a, b, dims=NN):
    return lax.dot_general(a, b, dims, preferred_element_type=F32)


def kept_row(degree, azimuth):
    if azimuth == 0:
        return degree
    if azimuth == 1:
        return 6 + degree
    if azimuth == -1:
        return 12 + degree
    if azimuth == 2:
        return 17 + degree
    return 22 + degree


def wig_row(degree, azimuth, column):
    start = sum((2 * min(k, 2) + 1) * (2 * k + 1) for k in range(degree))
    return start + (azimuth + min(degree, 2)) * (2 * degree + 1) + column


def orders(degree):
    reach = min(degree, 2)
    return range(-reach, reach + 1)


def eg_place(row):
    return ZORD.index(row) if row < 7 else row


def x_place(row):
    if row < 7:
        return row * 8
    if row < 13:
        return 64 + (row - 7) * 8
    if row < 19:
        return 112 + (row - 13) * 8
    if row < 24:
        return 160 + (row - 19) * 8
    return 208 + (row - 24) * 8


def iota(shape, axis):
    return lax.broadcasted_iota(jnp.int32, shape, axis)


def hot(match):
    return jnp.where(match, 1.0, 0.0).astype(BF)


def source_hots(src):
    width = src.shape[1]
    atom = iota((LANES, width), 0)
    own = hot(atom == src - 32)
    before = [hot(atom == jnp.where(src < 32, src + 32 * q, -1)) for q in range(4)]
    after = [hot(atom == jnp.where(src >= 160, src - 160 + 32 * q, -1)) for q in range(4)]
    return own, before, after


def pack_kernel(node_ref, cot_ref, zero_ref, one_ref, two_ref, node_out, cot_out, rim_out, weight_out):
    blank = jnp.zeros((8, LANES), F32)

    def rows(ref):
        return jnp.concatenate([ref[...].astype(F32).reshape(392, LANES), blank], axis=0).astype(BF)

    cot_out[...] = rows(cot_ref)
    node = rows(node_ref)
    node_out[...] = node
    atom, lane = iota((LANES, LANES), 0), iota((LANES, LANES), 1)
    parts = []
    for q in range(4):
        inside = (lane >= 32 * q) & (lane < 32 * q + 32)
        last = hot(inside & (atom == lane - 32 * q + 96))
        first = hot(inside & (atom == lane - 32 * q))
        parts.append(mm(node, jnp.concatenate([last, first], axis=1)))
    total = []
    for g in range(13):
        members = [parts[q][(4 * g + q) * 8 : (4 * g + q) * 8 + 8] for q in range(4) if 4 * g + q < 49]
        total.append(sum(members[1:], members[0]))
    total.append(jnp.zeros((8, 2 * LANES), F32))
    packed = jnp.concatenate(total, axis=0).astype(BF)
    rim_out[:112] = packed[:, :LANES]
    rim_out[112:] = packed[:, LANES:]
    parts = [ref[...].astype(F32).reshape(-1, LANES) for ref in (zero_ref, one_ref, two_ref)]
    weight_out[...] = jnp.concatenate(parts + [blank], axis=0).astype(BF)


def edge_in_kernel(h_ref, node_ref, near_ref, far_ref, src_ref, wig_ref, x_ref, rot, gathered):
    h = h_ref[0]
    src = src_ref[...]
    own, before, after = source_hots(src)
    gathered[...] = mm(node_ref[...], own)
    rot[...] = wig_ref[...].astype(F32)
    far = far_ref[...]
    from_before = jnp.where(h == 0, far, near_ref[:112])
    from_after = jnp.where(h == 0, near_ref[112:], far)
    for q in range(4):
        part = mm(from_before, before[q]) + mm(from_after, after[q])
        for g in range(13):
            coef = 4 * g + q
            if coef < 49:
                gathered[coef * 8 : coef * 8 + 8, :] += part[g * 8 : g * 8 + 8]
    rows = {}
    for degree in range(7):
        span = 2 * degree + 1
        vals = [gathered[(degree * degree + j) * 8 : (degree * degree + j + 1) * 8, :] for j in range(span)]
        for m in orders(degree):
            total = None
            for j in range(span):
                at = wig_row(degree, m, j)
                term = rot[at : at + 1, :] * vals[j]
                total = term if total is None else total + term
            rows[kept_row(degree, m)] = total
    blank = jnp.zeros((8, EB), F32)
    groups = [
        (0, [rows[r] for r in range(7)] + [blank]),
        (64, [rows[r] for r in range(7, 13)]),
        (112, [rows[r] for r in range(13, 19)]),
        (160, [rows[r] for r in range(19, 24)] + [blank]),
        (208, [rows[r] for r in range(24, 29)] + [blank]),
    ]
    for start, members in groups:
        x_ref[start : start + 8 * len(members), :] = jnp.concatenate(members, axis=0).astype(BF)


def weight_kernel(k_ref, own_ref, sib_ref, zero_ref, one_ref, two_ref):
    k = k_ref[0]
    chan, lane = iota((LANES, LANES), 0), iota((LANES, LANES), 1)

    def pick(offset):
        spot = lane - offset
        wanted = (spot // 8) * 16 + k * 8 + spot % 8
        return hot((spot >= 0) & (spot < 64) & (chan == wanted))

    low, high = pick(0), pick(64)
    own, sib = own_ref[...], sib_ref[...]
    sides = [(mm(own, low), mm(own, high)), (mm(sib, low), mm(sib, high))]

    def tile(entries, place):
        halves = []
        for side in sides:
            total = None
            for half, entry in enumerate(entries):
                if entry is None:
                    continue
                sign, at = entry
                piece = side[half][at * 8 : at * 8 + 8]
                piece = piece if sign > 0 else -piece
                total = piece if total is None else total + piece
            halves.append(total)
        return jnp.concatenate(halves, axis=0).astype(BF)

    for lp in range(7):
        for p in range(4):
            entries = [
                (1, lp * 7 + ZORD[n]) if n < 7 else None for n in (2 * p, 2 * p + 1)
            ]
            zero_ref[lp * 16 : lp * 16 + 16, p * 128 : p * 128 + 128] = tile(entries, p)
    for ref, count, base in ((one_ref, 6, 49), (two_ref, 5, 121)):
        for out in range(2):
            for lp in range(count):
                for p in range(count):
                    entries = []
                    for n in (2 * p, 2 * p + 1):
                        inp, l = n // count, n % count
                        which = 0 if inp == out else 1
                        sign = -1 if (out == 1 and inp == 0) else 1
                        entries.append((sign, base + which * count * count + lp * count + l))
                    row = (out * count + lp) * 16
                    ref[row : row + 16, p * 128 : p * 128 + 128] = tile(entries, p)


def rotate_pair(z, near_ref, far_ref, dest, rot, gathered, store):
    gathered[z % 2] = mm(near_ref[...], dest)
    gathered[1 - z % 2] = mm(far_ref[...], dest)
    for half in range(EB // LANES):
        lanes = slice(half * LANES, half * LANES + LANES)
        for degree in range(7):
            span = 2 * degree + 1
            at0 = degree * degree
            cols = [
                [gathered[side, (at0 + j) * 8 : (at0 + j + 1) * 8, lanes] for j in range(span)]
                for side in range(2)
            ]
            for m in orders(degree):
                totals = [None, None]
                for j in range(span):
                    at = wig_row(degree, m, j)
                    coeff = jnp.broadcast_to(rot[at : at + 1, lanes], (8, LANES))
                    for side in range(2):
                        term = coeff * cols[side][j]
                        totals[side] = term if totals[side] is None else totals[side] + term
                place = eg_place(kept_row(degree, m))
                store(place, lanes, jnp.concatenate(totals, axis=0).astype(BF))


def edge_factor(step, count_ref, scale_ref):
    slot = step * EB + iota((1, EB), 1)
    return jnp.where(slot < count_ref[0], 0.25 * scale_ref[...], 0.0)


def rotate_kernel(pairs, z_ref, count_ref, *refs):
    blocks, (dst_ref, scale_ref, wig_ref), outs = refs[: 2 * pairs], refs[2 * pairs : 2 * pairs + 3], refs[2 * pairs + 3 : -2]
    gathered, rot = refs[-2:]
    rot[...] = wig_ref[...].astype(F32) * edge_factor(pl.program_id(0), count_ref, scale_ref)
    dest = hot(iota((LANES, EB), 0) == dst_ref[...])
    for pair, eg_ref in enumerate(outs):

        def store(place, lanes, tile, eg_ref=eg_ref):
            eg_ref[place * 16 : place * 16 + 16, lanes] = tile

        near_ref, far_ref = blocks[2 * pair : 2 * pair + 2]
        rotate_pair(z_ref[0], near_ref, far_ref, dest, rot, gathered.at[pair], store)


def edge_kernel(
    z_ref, count_ref, eg0, eg1, eg2, near_ref, far_ref,
    dst_ref, src_ref, scale_ref, wig_ref, xo_ref, xs_ref, zero_ref, one_ref, two_ref,
    so_ref, go_ref, sib_ref,
    gathered, rot, plain, eg, acc, back, full, atoms, rims,
):
    step = pl.program_id(0)

    @pl.when(step == 0)
    def _():
        acc[...] = jnp.zeros_like(acc)
        atoms[...] = jnp.zeros_like(atoms)
        rims[...] = jnp.zeros_like(rims)

    z = z_ref[0]
    entries = wig_ref[...].astype(F32)
    plain[...] = entries
    rot[...] = entries * edge_factor(step, count_ref, scale_ref)
    dest = hot(iota((LANES, EB), 0) == dst_ref[...])

    def rows_of(place, n):
        return pl.ds(pl.multiple_of(place * 64 + ((z // 2) ^ n) * 16, 16), 16)

    def store(place, lanes, tile):
        eg[rows_of(place, 3), lanes] = tile

    rotate_pair(z, near_ref, far_ref, dest, rot, gathered, store)
    for n, ref in ((0, eg0), (1, eg1), (2, eg2)):
        for place in range(29):
            eg[rows_of(place, n), :] = ref[place * 16 : place * 16 + 16]

    def stacked(*pieces):
        return jnp.concatenate(pieces, axis=0)

    def blank(rows):
        return jnp.zeros((rows, EB), BF)

    xo, xs = xo_ref[...], xs_ref[...]
    acc[0:448] += mm(eg[0:448], stacked(xo[:64], blank(64), xs[:64], blank(64)), NT)
    for start, count, plus, minus in ((448, 6, 64, 112), (1216, 5, 160, 208)):
        ahead = stacked(
            xo[plus : plus + 48], -xo[minus : minus + 48], blank(32),
            xs[plus : plus + 48], -xs[minus : minus + 48], blank(32),
        )
        cross = stacked(
            xo[minus : minus + 48], xo[plus : plus + 48], blank(32),
            xs[minus : minus + 48], xs[plus : plus + 48], blank(32),
        )
        size = count * 64
        at = 448 if count == 6 else 832
        acc[at : at + size] += mm(eg[start : start + size], ahead, NT) + mm(
            eg[start + size : start + 2 * size], cross, NT
        )

    back[0:112] = mm(zero_ref[:, 0:448], eg[0:448])
    back[112:304] = mm(one_ref[...], eg[448:1216])
    back[304:464] = mm(two_ref[...], eg[1216:1856])
    quarter_start = (0, 13, 25, 37)
    for half in range(EB // LANES):
        lanes = slice(half * LANES, half * LANES + LANES)
        for degree in range(7):
            vals_m = {
                m: back[kept_row(degree, m) * 16 : kept_row(degree, m) * 16 + 16, lanes]
                for m in orders(degree)
            }
            for j in range(2 * degree + 1):
                total = None
                for m in orders(degree):
                    at = wig_row(degree, m, j)
                    term = plain[at : at + 1, lanes] * vals_m[m]
                    total = term if total is None else total + term
                coef = degree * degree + j
                row = (quarter_start[coef % 4] + coef // 4) * 16
                full[row : row + 16, lanes] = total.astype(BF)
    own, before, after = source_hots(src_ref[...])
    for q in range(4):
        start, size = quarter_start[q] * 16, (13 if q == 0 else 12) * 16
        rows = full[start : start + size]
        atoms[start : start + size] += mm(rows, own, NT)
        rims[0:size] += mm(rows, jnp.concatenate([before[q], after[q]], axis=0), NT)

    @pl.when(step == pl.num_programs(0) - 1)
    def _():
        for zb in range(8):
            tiles = []
            spot = zb * 8
            for t in range(4):
                tile = acc[t * 64 + spot : t * 64 + spot + 8]
                if t < 3:
                    odd = acc[256 + t * 64 + spot : 256 + t * 64 + spot + 8]
                    halves = [pltpu.roll(odd[:, n : n + LANES], 64, 1) for n in (0, LANES)]
                    tile = tile + jnp.concatenate(halves, axis=1)
                tiles.append(tile)
            for n in range(11):
                tiles.append(acc[448 + n * 64 + spot : 448 + n * 64 + spot + 8])
            tiles.append(jnp.zeros((8, 2 * LANES), F32))
            whole_tile = jnp.concatenate(tiles, axis=0).astype(BF)
            so_ref[zb * 128 : zb * 128 + 128] = whole_tile[:, :LANES]
            sib_ref[zb * 128 : zb * 128 + 128] = whole_tile[:, LANES:]
        for side in range(2):
            tiles = []
            for coef in range(49):
                row = (quarter_start[coef % 4] + coef // 4) * 16 + side * 8
                tiles.append(atoms[row : row + 8])
            tiles.append(jnp.zeros((8, LANES), F32))
            for rim in range(2):
                for g in range(13):
                    row = g * 16 + side * 8
                    tiles.append(rims[row : row + 8, rim * LANES : rim * LANES + LANES])
                tiles.append(jnp.zeros((8, LANES), F32))
            if side == 0:
                go_ref[...] = jnp.concatenate(tiles, axis=0)
            else:
                sib_ref[1024:1648] = jnp.concatenate(tiles, axis=0).astype(BF)


def row_spec():
    return pl.BlockSpec((1, EB), lambda i: (0, i))


def wig_spec():
    return pl.BlockSpec((235, EB), lambda i: (0, i))


def rotate_call(z_s, edge_count, blocks, dst, scale, wigner):
    slots = dst.shape[1]
    pairs = len(blocks) // 2
    return pl.pallas_call(
        functools.partial(rotate_kernel, pairs),
        out_shape=[sds((464, slots), BF)] * pairs,
        grid=(slots // EB,),
        in_specs=[smem(), smem()] + [whole((400, 128))] * len(blocks) + [row_spec(), row_spec(), wig_spec()],
        out_specs=[pl.BlockSpec((464, EB), lambda i: (0, i))] * pairs,
        scratch_shapes=[pltpu.VMEM((pairs, 2, 400, EB), F32), pltpu.VMEM((235, EB), F32)],
        compiler_params=params(),
        name="rotate",
    )(z_s, edge_count, *blocks, dst, scale, wigner)


def edge_call(z_s, edge_count, egs, pair, dst, src, scale, wigner, x_own, x_sib, weights):
    slots = dst.shape[1]
    x_spec = pl.BlockSpec((256, EB), lambda i: (0, i))
    return pl.pallas_call(
        edge_kernel,
        out_shape=(sds((1024, 128), BF), sds((624, 128), F32), sds((1648, 128), BF)),
        grid=(slots // EB,),
        in_specs=[smem(), smem()]
        + [pl.BlockSpec((464, EB), lambda i: (0, i))] * 3
        + [whole((400, 128)), whole((400, 128)), row_spec(), row_spec(), row_spec(), wig_spec(), x_spec, x_spec]
        + [whole((112, 512)), whole((192, 768)), whole((160, 640))],
        out_specs=(whole((1024, 128)), whole((624, 128)), whole((1648, 128))),
        scratch_shapes=[
            pltpu.VMEM((2, 400, EB), F32),
            pltpu.VMEM((235, EB), F32),
            pltpu.VMEM((235, EB), F32),
            pltpu.VMEM((1856, EB), BF),
            pltpu.VMEM((1152, 256), F32),
            pltpu.VMEM((464, EB), F32),
            pltpu.VMEM((784, EB), BF),
            pltpu.VMEM((784, LANES), F32),
            pltpu.VMEM((208, 2 * LANES), F32),
        ],
        compiler_params=params(),
        name="edge",
    )(z_s, edge_count, *egs, *pair, dst, src, scale, wigner, x_own, x_sib, *weights)


def finish_kernel(mine_ref, got_ref, zero_ref, one_ref, two_ref):
    total = mine_ref[...] + got_ref[224:288].astype(F32)

    def moved(lane):
        return total if lane == 0 else pltpu.roll(total, LANES - lane, 1)

    for lp in range(7):
        even, odd = moved(lp * 8), moved(64 + lp * 8)
        for n, l in enumerate(ZORD):
            source, row = (even, n * 4) if n < 4 else (odd, (n - 4) * 4)
            zero_ref[lp, l] = source[row : row + 4, 0:8]
    for ref, count, first, stride in ((one_ref, 6, 4, 48), (two_ref, 5, 10, 48)):
        for w in range(2):
            for lp in range(count):
                source = moved(w * stride + lp * 8)
                for l in range(count):
                    row = (first + l) * 4
                    ref[w, lp, l] = source[row : row + 4, 0:8]


def join_kernel(h_ref, own_ref, rim_ref, out_ref):
    h = h_ref[0]
    base_a = jnp.where(h == 0, 96, 0)
    base_b = 96 - base_a
    lane, atom = iota((LANES, LANES), 0), iota((LANES, LANES), 1)
    ra, rb = rim_ref[0:112], rim_ref[112:224]
    for q in range(4):
        inside = (lane >= 32 * q) & (lane < 32 * q + 32)
        put_a = hot(inside & (atom == lane - 32 * q + base_a))
        put_b = hot(inside & (atom == lane - 32 * q + base_b))
        part = mm(ra, put_a) + mm(rb, put_b)
        for g in range(13):
            coef = 4 * g + q
            if coef < 49:
                out_ref[coef] = own_ref[coef * 8 : coef * 8 + 8] + part[g * 8 : g * 8 + 8]


def smem():
    return pl.BlockSpec(memory_space=pltpu.SMEM)


def params():
    return pltpu.CompilerParams(vmem_limit_bytes=VMEM_LIMIT)


def light():
    return pl.CostEstimate(flops=1, bytes_accessed=1, transcendentals=0)


def whole(shape):
    return pl.BlockSpec(shape, lambda *_: (0,) * len(shape))


def sds(shape, dtype):
    return jax.ShapeDtypeStruct(shape, dtype)


def body(
    node_x, cotangent, wigner, src_index, dst_index, edge_scale, edge_count, w_zero, w_one, w_two
):
    chan = lax.axis_index("chan")
    brick = lax.axis_index("brick")
    z, core = chan // 2, chan % 2
    high = brick % 2
    z_s = z.astype(jnp.int32).reshape(1)
    k_s = core.astype(jnp.int32).reshape(1)
    h_s = high.astype(jnp.int32).reshape(1)
    slots = src_index.shape[0]
    steps = slots // EB
    src = src_index.reshape(1, slots)
    dst = dst_index.reshape(1, slots)
    scale = edge_scale.reshape(1, slots)

    def across(x, mask):
        return lax.ppermute(x, "chan", [(i, i ^ mask) for i in range(16)])

    def cross(x):
        return lax.ppermute(x, "brick", [(i, i ^ 1) for i in range(32)])

    def shift(x, away):
        route = [(i, (i + (2 if (i % 2 == 0) == away else -2)) % 32) for i in range(32)]
        return lax.ppermute(x, "brick", route)

    w_tiles = (
        w_zero.transpose(0, 2, 1, 3).reshape(49, 8, 128),
        w_one.transpose(0, 1, 3, 2, 4).reshape(72, 8, 128),
        w_two.transpose(0, 1, 3, 2, 4).reshape(50, 8, 128),
    )
    node, b0, rims, w_own = pl.pallas_call(
        pack_kernel,
        out_shape=(sds((400, 128), BF), sds((400, 128), BF), sds((224, 128), BF), sds((1376, 128), BF)),
        in_specs=[whole((n, 8, 128)) for n in (49, 49, 49, 72, 50)],
        out_specs=(whole((400, 128)), whole((400, 128)), whole((224, 128)), whole((1376, 128))),
        grid=(1,),
        compiler_params=pltpu.CompilerParams(vmem_limit_bytes=PACK_VMEM),
        cost_estimate=light(),
        name="pack",
    )(node_x, cotangent, *w_tiles)
    near = cross(rims)

    def rotated(*blocks):
        return rotate_call(z_s, edge_count, blocks, dst, scale, wigner)

    b4 = across(b0, 8)
    b2 = across(b0, 4)
    b1 = across(b0, 2)
    far = shift(lax.dynamic_slice_in_dim(near, 112 * high, 112, 0), True)
    (eg0,) = rotated(b0, b1)

    x_spec = pl.BlockSpec((256, EB), lambda i: (0, i))
    x_own = pl.pallas_call(
        edge_in_kernel,
        out_shape=sds((256, slots), BF),
        grid=(steps,),
        in_specs=[smem(), whole((400, 128)), whole((224, 128)), whole((112, 128)), row_spec(), wig_spec()],
        out_specs=x_spec,
        scratch_shapes=[pltpu.VMEM((235, EB), F32), pltpu.VMEM((400, EB), F32)],
        compiler_params=params(),
        cost_estimate=light(),
        name="edge_in",
    )(h_s, node, near, far, src, wigner)
    b4, b2, w_own, x_own, eg0 = lax.optimization_barrier((b4, b2, w_own, x_own, eg0))
    b6 = across(b4, 4)
    b5 = across(b4, 2)
    b3 = across(b2, 2)

    w_sib = across(w_own, 1)
    wz, wo, wt = pl.pallas_call(
        weight_kernel,
        out_shape=(sds((112, 512), BF), sds((192, 768), BF), sds((160, 640), BF)),
        grid=(1,),
        in_specs=[smem(), whole((1376, 128)), whole((1376, 128))],
        out_specs=(whole((112, 512)), whole((192, 768)), whole((160, 640))),
        compiler_params=params(),
        cost_estimate=light(),
        name="weights",
    )(k_s, w_own, w_sib)

    b6, b5, b3, x_own, wz, wo, wt = lax.optimization_barrier((b6, b5, b3, x_own, wz, wo, wt))
    b7 = across(b6, 2)
    eg1, eg2 = rotated(b2, b3, b4, b5)
    x_sib = across(x_own, 1)

    s_own, g_own, to_sib = edge_call(
        z_s, edge_count, (eg0, eg1, eg2), (b6, b7), dst, src, scale, wigner, x_own, x_sib, (wz, wo, wt)
    )

    got = across(to_sib, 1)
    s_got = got[:1024].reshape(8, 128, 128)
    s_own = s_own.reshape(8, 128, 128)
    send = jnp.concatenate([s_own, s_got], axis=0)
    groups = [
        [
            (2 * (2 * zb + (k ^ p)) + h) * 16 + 2 * zl + k
            for p in range(2)
            for zb in range(8)
        ]
        for h in range(2)
        for zl in range(8)
        for k in range(2)
    ]
    pieces = lax.all_to_all(send, ("brick", "chan"), 0, 0, axis_index_groups=groups)
    summed = pieces.astype(F32).sum(axis=0).reshape(16, 2, 4, 128)
    mine = jnp.where(high == 0, summed[:, 0], summed[:, 1])
    other = jnp.where(high == 0, summed[:, 1], summed[:, 0])

    g_all = g_own + got[1024:].astype(F32)
    left, right = g_all[400:512].astype(BF), g_all[512:624].astype(BF)
    near_rim = jnp.where(high == 0, right, left)
    far_rim = shift(jnp.where(high == 0, left, right), False)

    crossed = cross(jnp.concatenate([near_rim, far_rim, other.astype(BF).reshape(64, 128)], axis=0))
    grad_x = pl.pallas_call(
        join_kernel,
        out_shape=sds((49, 8, 128), F32),
        grid=(1,),
        in_specs=[smem(), whole((624, 128)), whole((288, 128))],
        out_specs=whole((49, 8, 128)),
        compiler_params=params(),
        cost_estimate=light(),
        name="join",
    )(h_s, g_all, crossed)

    zero, one, second = pl.pallas_call(
        finish_kernel,
        out_shape=(sds((7, 7, 4, 8), F32), sds((2, 6, 6, 4, 8), F32), sds((2, 5, 5, 4, 8), F32)),
        grid=(1,),
        in_specs=[whole((64, 128)), whole((288, 128))],
        out_specs=(whole((7, 7, 4, 8)), whole((2, 6, 6, 4, 8)), whole((2, 5, 5, 4, 8))),
        compiler_params=params(),
        cost_estimate=light(),
        name="finish",
    )(mine.reshape(64, 128), crossed)
    grad_zero = zero.transpose(0, 3, 1, 2)
    grad_one = one.transpose(0, 1, 4, 2, 3)
    grad_two = second.transpose(0, 1, 4, 2, 3)
    return grad_x, grad_zero, grad_one, grad_two


def solution(mesh):
    in_specs = (
        P(None, "chan", "brick"),
        P(None, "chan", "brick"),
        P(None, "brick"),
        P("brick"),
        P("brick"),
        P("brick"),
        P("brick"),
        P(None, "chan", None, None),
        P(None, None, "chan", None, None),
        P(None, None, "chan", None, None),
    )
    out_specs = (
        P(None, "chan", "brick"),
        P(None, "chan", None, "brick"),
        P(None, None, "chan", None, "brick"),
        P(None, None, "chan", None, "brick"),
    )
    return jax.shard_map(body, mesh=mesh, in_specs=in_specs, out_specs=out_specs, check_vma=False)
```

```python
import functools

import jax
import jax.numpy as jnp
from jax import lax
from jax.experimental import pallas as pl
from jax.experimental.pallas import tpu as pltpu
from jax.sharding import PartitionSpec as P

BF = jnp.bfloat16
F32 = jnp.float32
EB = 256
LANES = 128
VMEM_LIMIT = 28 * 1024 * 1024
PACK_VMEM = 60 * 1024 * 1024
X_ROWS = 2048
ZORD = (0, 2, 4, 6, 1, 3, 5)

NN = (((1,), (0,)), ((), ()))
NT = (((1,), (1,)), ((), ()))


def mm(a, b, dims=NN):
    return lax.dot_general(a, b, dims, preferred_element_type=F32)


def kept_row(degree, azimuth):
    if azimuth == 0:
        return degree
    if azimuth == 1:
        return 6 + degree
    if azimuth == -1:
        return 12 + degree
    if azimuth == 2:
        return 17 + degree
    return 22 + degree


def wig_row(degree, azimuth, column):
    start = sum((2 * min(k, 2) + 1) * (2 * k + 1) for k in range(degree))
    return start + (azimuth + min(degree, 2)) * (2 * degree + 1) + column


def orders(degree):
    reach = min(degree, 2)
    return range(-reach, reach + 1)


def eg_place(row):
    return ZORD.index(row) if row < 7 else row


def x_place(row):
    if row < 7:
        return row * 8
    if row < 13:
        return 64 + (row - 7) * 8
    if row < 19:
        return 112 + (row - 13) * 8
    if row < 24:
        return 160 + (row - 19) * 8
    return 208 + (row - 24) * 8


def iota(shape, axis):
    return lax.broadcasted_iota(jnp.int32, shape, axis)


def hot(match):
    return jnp.where(match, 1.0, 0.0).astype(BF)


def source_hots(src):
    width = src.shape[1]
    atom = iota((LANES, width), 0)
    own = hot(atom == src - 32)
    before = [hot(atom == jnp.where(src < 32, src + 32 * q, -1)) for q in range(4)]
    after = [hot(atom == jnp.where(src >= 160, src - 160 + 32 * q, -1)) for q in range(4)]
    return own, before, after


def pack_kernel(node_ref, cot_ref, zero_ref, one_ref, two_ref, node_out, cot_out, rim_out, weight_out):
    blank = jnp.zeros((8, LANES), F32)

    def rows(ref):
        return jnp.concatenate([ref[...].astype(F32).reshape(392, LANES), blank], axis=0).astype(BF)

    cot_out[...] = rows(cot_ref)
    node = rows(node_ref)
    node_out[...] = node
    atom, lane = iota((LANES, LANES), 0), iota((LANES, LANES), 1)
    parts = []
    for q in range(4):
        inside = (lane >= 32 * q) & (lane < 32 * q + 32)
        last = hot(inside & (atom == lane - 32 * q + 96))
        first = hot(inside & (atom == lane - 32 * q))
        parts.append(mm(node, jnp.concatenate([last, first], axis=1)))
    total = []
    for g in range(13):
        members = [parts[q][(4 * g + q) * 8 : (4 * g + q) * 8 + 8] for q in range(4) if 4 * g + q < 49]
        total.append(sum(members[1:], members[0]))
    total.append(jnp.zeros((8, 2 * LANES), F32))
    packed = jnp.concatenate(total, axis=0).astype(BF)
    rim_out[:112] = packed[:, :LANES]
    rim_out[112:] = packed[:, LANES:]
    parts = [ref[...].astype(F32).reshape(-1, LANES) for ref in (zero_ref, one_ref, two_ref)]
    weight_out[...] = jnp.concatenate(parts + [blank], axis=0).astype(BF)


def edge_in_kernel(h_ref, node_ref, near_ref, far_ref, weight_ref, src_ref, wig_ref, x_ref, rot, gathered):
    step = pl.program_id(0)

    @pl.when(step == 0)
    def _():
        x_ref[X_ROWS:] = weight_ref[...]

    h = h_ref[0]
    src = src_ref[...]
    own, before, after = source_hots(src)
    gathered[...] = mm(node_ref[...], own)
    rot[...] = wig_ref[...].astype(F32)
    far = far_ref[...]
    from_before = jnp.where(h == 0, far, near_ref[:112])
    from_after = jnp.where(h == 0, near_ref[112:], far)
    for q in range(4):
        part = mm(from_before, before[q]) + mm(from_after, after[q])
        for g in range(13):
            coef = 4 * g + q
            if coef < 49:
                gathered[coef * 8 : coef * 8 + 8, :] += part[g * 8 : g * 8 + 8]
    rows = {}
    for degree in range(7):
        span = 2 * degree + 1
        vals = [gathered[(degree * degree + j) * 8 : (degree * degree + j + 1) * 8, :] for j in range(span)]
        for m in orders(degree):
            total = None
            for j in range(span):
                at = wig_row(degree, m, j)
                term = rot[at : at + 1, :] * vals[j]
                total = term if total is None else total + term
            rows[kept_row(degree, m)] = total
    blank = jnp.zeros((8, EB), F32)
    groups = [
        (0, [rows[r] for r in range(7)] + [blank]),
        (64, [rows[r] for r in range(7, 13)]),
        (112, [rows[r] for r in range(13, 19)]),
        (160, [rows[r] for r in range(19, 24)] + [blank]),
        (208, [rows[r] for r in range(24, 29)] + [blank]),
    ]
    for start, members in groups:
        block = jnp.concatenate(members, axis=0).astype(BF)
        for half in range(EB // LANES):
            row = pl.multiple_of(step * (256 * EB // LANES) + 256 * half + start, 16)
            x_ref[pl.ds(row, 8 * len(members)), :] = block[:, half * LANES : half * LANES + LANES]


def weight_kernel(k_ref, own_ref, sib_ref, zero_ref, one_ref, two_ref):
    k = k_ref[0]
    chan, lane = iota((LANES, LANES), 0), iota((LANES, LANES), 1)

    def pick(offset):
        spot = lane - offset
        wanted = (spot // 8) * 16 + k * 8 + spot % 8
        return hot((spot >= 0) & (spot < 64) & (chan == wanted))

    low, high = pick(0), pick(64)
    own, sib = own_ref[X_ROWS:], sib_ref[X_ROWS:]
    sides = [(mm(own, low), mm(own, high)), (mm(sib, low), mm(sib, high))]

    def tile(entries, place):
        halves = []
        for side in sides:
            total = None
            for half, entry in enumerate(entries):
                if entry is None:
                    continue
                sign, at = entry
                piece = side[half][at * 8 : at * 8 + 8]
                piece = piece if sign > 0 else -piece
                total = piece if total is None else total + piece
            halves.append(total)
        return jnp.concatenate(halves, axis=0).astype(BF)

    for lp in range(7):
        for p in range(4):
            entries = [
                (1, lp * 7 + ZORD[n]) if n < 7 else None for n in (2 * p, 2 * p + 1)
            ]
            zero_ref[lp * 16 : lp * 16 + 16, p * 128 : p * 128 + 128] = tile(entries, p)
    for ref, count, base in ((one_ref, 6, 49), (two_ref, 5, 121)):
        for out in range(2):
            for lp in range(count):
                for p in range(count):
                    entries = []
                    for n in (2 * p, 2 * p + 1):
                        inp, l = n // count, n % count
                        which = 0 if inp == out else 1
                        sign = -1 if (out == 1 and inp == 0) else 1
                        entries.append((sign, base + which * count * count + lp * count + l))
                    row = (out * count + lp) * 16
                    ref[row : row + 16, p * 128 : p * 128 + 128] = tile(entries, p)


def rotate_pair(z, near_ref, far_ref, dest, rot, gathered, store):
    gathered[z % 2] = mm(near_ref[...], dest)
    gathered[1 - z % 2] = mm(far_ref[...], dest)
    for half in range(EB // LANES):
        lanes = slice(half * LANES, half * LANES + LANES)
        for degree in range(7):
            span = 2 * degree + 1
            at0 = degree * degree
            cols = [
                [gathered[side, (at0 + j) * 8 : (at0 + j + 1) * 8, lanes] for j in range(span)]
                for side in range(2)
            ]
            for m in orders(degree):
                totals = [None, None]
                for j in range(span):
                    at = wig_row(degree, m, j)
                    coeff = jnp.broadcast_to(rot[at : at + 1, lanes], (8, LANES))
                    for side in range(2):
                        term = coeff * cols[side][j]
                        totals[side] = term if totals[side] is None else totals[side] + term
                place = eg_place(kept_row(degree, m))
                store(place, lanes, jnp.concatenate(totals, axis=0).astype(BF))


def edge_factor(step, count_ref, scale_ref):
    slot = step * EB + iota((1, EB), 1)
    return jnp.where(slot < count_ref[0], 0.25 * scale_ref[...], 0.0)


def rotate_kernel(pairs, z_ref, count_ref, *refs):
    blocks, (dst_ref, scale_ref, wig_ref), outs = refs[: 2 * pairs], refs[2 * pairs : 2 * pairs + 3], refs[2 * pairs + 3 : -2]
    gathered, rot = refs[-2:]
    rot[...] = wig_ref[...].astype(F32) * edge_factor(pl.program_id(0), count_ref, scale_ref)
    dest = hot(iota((LANES, EB), 0) == dst_ref[...])
    for pair, eg_ref in enumerate(outs):

        def store(place, lanes, tile, eg_ref=eg_ref):
            eg_ref[place * 16 : place * 16 + 16, lanes] = tile

        near_ref, far_ref = blocks[2 * pair : 2 * pair + 2]
        rotate_pair(z_ref[0], near_ref, far_ref, dest, rot, gathered.at[pair], store)


def edge_kernel(
    z_ref, count_ref, eg0, eg1, eg2, near_ref, far_ref,
    dst_ref, src_ref, scale_ref, wig_ref, xo_ref, xs_ref, zero_ref, one_ref, two_ref,
    so_ref, go_ref, sib_ref,
    gathered, rot, plain, eg, acc, back, full, atoms, rims,
):
    step = pl.program_id(0)

    @pl.when(step == 0)
    def _():
        acc[...] = jnp.zeros_like(acc)
        atoms[...] = jnp.zeros_like(atoms)
        rims[...] = jnp.zeros_like(rims)

    z = z_ref[0]
    entries = wig_ref[...].astype(F32)
    plain[...] = entries
    rot[...] = entries * edge_factor(step, count_ref, scale_ref)
    dest = hot(iota((LANES, EB), 0) == dst_ref[...])

    def rows_of(place, n):
        return pl.ds(pl.multiple_of(place * 64 + ((z // 2) ^ n) * 16, 16), 16)

    def store(place, lanes, tile):
        eg[rows_of(place, 3), lanes] = tile

    rotate_pair(z, near_ref, far_ref, dest, rot, gathered, store)
    for n, ref in ((0, eg0), (1, eg1), (2, eg2)):
        for place in range(29):
            eg[rows_of(place, n), :] = ref[place * 16 : place * 16 + 16]

    def stacked(*pieces):
        return jnp.concatenate(pieces, axis=0)

    def blank(rows):
        return jnp.zeros((rows, EB), BF)

    def tiles_of(ref):
        return jnp.concatenate([ref[256 * n : 256 * n + 256] for n in range(EB // LANES)], axis=1)

    xo, xs = tiles_of(xo_ref), tiles_of(xs_ref)
    acc[0:448] += mm(eg[0:448], stacked(xo[:64], blank(64), xs[:64], blank(64)), NT)
    for start, count, plus, minus in ((448, 6, 64, 112), (1216, 5, 160, 208)):
        ahead = stacked(
            xo[plus : plus + 48], -xo[minus : minus + 48], blank(32),
            xs[plus : plus + 48], -xs[minus : minus + 48], blank(32),
        )
        cross = stacked(
            xo[minus : minus + 48], xo[plus : plus + 48], blank(32),
            xs[minus : minus + 48], xs[plus : plus + 48], blank(32),
        )
        size = count * 64
        at = 448 if count == 6 else 832
        acc[at : at + size] += mm(eg[start : start + size], ahead, NT) + mm(
            eg[start + size : start + 2 * size], cross, NT
        )

    back[0:112] = mm(zero_ref[:, 0:448], eg[0:448])
    back[112:304] = mm(one_ref[...], eg[448:1216])
    back[304:464] = mm(two_ref[...], eg[1216:1856])
    quarter_start = (0, 13, 25, 37)
    for half in range(EB // LANES):
        lanes = slice(half * LANES, half * LANES + LANES)
        for degree in range(7):
            vals_m = {
                m: back[kept_row(degree, m) * 16 : kept_row(degree, m) * 16 + 16, lanes]
                for m in orders(degree)
            }
            for j in range(2 * degree + 1):
                total = None
                for m in orders(degree):
                    at = wig_row(degree, m, j)
                    term = plain[at : at + 1, lanes] * vals_m[m]
                    total = term if total is None else total + term
                coef = degree * degree + j
                row = (quarter_start[coef % 4] + coef // 4) * 16
                full[row : row + 16, lanes] = total.astype(BF)
    own, before, after = source_hots(src_ref[...])
    for q in range(4):
        start, size = quarter_start[q] * 16, (13 if q == 0 else 12) * 16
        rows = full[start : start + size]
        atoms[start : start + size] += mm(rows, own, NT)
        rims[0:size] += mm(rows, jnp.concatenate([before[q], after[q]], axis=0), NT)

    @pl.when(step == pl.num_programs(0) - 1)
    def _():
        for zb in range(8):
            tiles = []
            spot = zb * 8
            for t in range(4):
                tile = acc[t * 64 + spot : t * 64 + spot + 8]
                if t < 3:
                    odd = acc[256 + t * 64 + spot : 256 + t * 64 + spot + 8]
                    halves = [pltpu.roll(odd[:, n : n + LANES], 64, 1) for n in (0, LANES)]
                    tile = tile + jnp.concatenate(halves, axis=1)
                tiles.append(tile)
            for n in range(11):
                tiles.append(acc[448 + n * 64 + spot : 448 + n * 64 + spot + 8])
            tiles.append(jnp.zeros((8, 2 * LANES), F32))
            whole_tile = jnp.concatenate(tiles, axis=0).astype(BF)
            so_ref[zb * 128 : zb * 128 + 128] = whole_tile[:, :LANES]
            sib_ref[zb * 128 : zb * 128 + 128] = whole_tile[:, LANES:]
        for side in range(2):
            tiles = []
            for coef in range(49):
                row = (quarter_start[coef % 4] + coef // 4) * 16 + side * 8
                tiles.append(atoms[row : row + 8])
            tiles.append(jnp.zeros((8, LANES), F32))
            for rim in range(2):
                for g in range(13):
                    row = g * 16 + side * 8
                    tiles.append(rims[row : row + 8, rim * LANES : rim * LANES + LANES])
                tiles.append(jnp.zeros((8, LANES), F32))
            if side == 0:
                go_ref[...] = jnp.concatenate(tiles, axis=0)
            else:
                sib_ref[1024:1648] = jnp.concatenate(tiles, axis=0).astype(BF)


def row_spec():
    return pl.BlockSpec((1, EB), lambda i: (0, i))


def wig_spec():
    return pl.BlockSpec((235, EB), lambda i: (0, i))


def rotate_call(z_s, edge_count, blocks, dst, scale, wigner):
    slots = dst.shape[1]
    pairs = len(blocks) // 2
    return pl.pallas_call(
        functools.partial(rotate_kernel, pairs),
        out_shape=[sds((464, slots), BF)] * pairs,
        grid=(slots // EB,),
        in_specs=[smem(), smem()] + [whole((400, 128))] * len(blocks) + [row_spec(), row_spec(), wig_spec()],
        out_specs=[pl.BlockSpec((464, EB), lambda i: (0, i))] * pairs,
        scratch_shapes=[pltpu.VMEM((pairs, 2, 400, EB), F32), pltpu.VMEM((235, EB), F32)],
        compiler_params=params(),
        name="rotate",
    )(z_s, edge_count, *blocks, dst, scale, wigner)


def edge_call(z_s, edge_count, egs, pair, dst, src, scale, wigner, x_own, x_sib, weights):
    slots = dst.shape[1]
    x_spec = pl.BlockSpec((256 * EB // LANES, LANES), lambda i: (i, 0))
    return pl.pallas_call(
        edge_kernel,
        out_shape=(sds((1024, 128), BF), sds((624, 128), F32), sds((1648, 128), BF)),
        grid=(slots // EB,),
        in_specs=[smem(), smem()]
        + [pl.BlockSpec((464, EB), lambda i: (0, i))] * 3
        + [whole((400, 128)), whole((400, 128)), row_spec(), row_spec(), row_spec(), wig_spec(), x_spec, x_spec]
        + [whole((112, 512)), whole((192, 768)), whole((160, 640))],
        out_specs=(whole((1024, 128)), whole((624, 128)), whole((1648, 128))),
        scratch_shapes=[
            pltpu.VMEM((2, 400, EB), F32),
            pltpu.VMEM((235, EB), F32),
            pltpu.VMEM((235, EB), F32),
            pltpu.VMEM((1856, EB), BF),
            pltpu.VMEM((1152, 256), F32),
            pltpu.VMEM((464, EB), F32),
            pltpu.VMEM((784, EB), BF),
            pltpu.VMEM((784, LANES), F32),
            pltpu.VMEM((208, 2 * LANES), F32),
        ],
        compiler_params=params(),
        name="edge",
    )(z_s, edge_count, *egs, *pair, dst, src, scale, wigner, x_own, x_sib, *weights)


def finish_kernel(mine_ref, got_ref, zero_ref, one_ref, two_ref):
    total = mine_ref[...] + got_ref[224:288].astype(F32)

    def moved(lane):
        return total if lane == 0 else pltpu.roll(total, LANES - lane, 1)

    for lp in range(7):
        even, odd = moved(lp * 8), moved(64 + lp * 8)
        for n, l in enumerate(ZORD):
            source, row = (even, n * 4) if n < 4 else (odd, (n - 4) * 4)
            zero_ref[lp, l] = source[row : row + 4, 0:8]
    for ref, count, first, stride in ((one_ref, 6, 4, 48), (two_ref, 5, 10, 48)):
        for w in range(2):
            for lp in range(count):
                source = moved(w * stride + lp * 8)
                for l in range(count):
                    row = (first + l) * 4
                    ref[w, lp, l] = source[row : row + 4, 0:8]


def join_kernel(h_ref, own_ref, rim_ref, out_ref):
    h = h_ref[0]
    base_a = jnp.where(h == 0, 96, 0)
    base_b = 96 - base_a
    lane, atom = iota((LANES, LANES), 0), iota((LANES, LANES), 1)
    ra, rb = rim_ref[0:112], rim_ref[112:224]
    for q in range(4):
        inside = (lane >= 32 * q) & (lane < 32 * q + 32)
        put_a = hot(inside & (atom == lane - 32 * q + base_a))
        put_b = hot(inside & (atom == lane - 32 * q + base_b))
        part = mm(ra, put_a) + mm(rb, put_b)
        for g in range(13):
            coef = 4 * g + q
            if coef < 49:
                out_ref[coef] = own_ref[coef * 8 : coef * 8 + 8] + part[g * 8 : g * 8 + 8]


def smem():
    return pl.BlockSpec(memory_space=pltpu.SMEM)


def params():
    return pltpu.CompilerParams(vmem_limit_bytes=VMEM_LIMIT)


def light():
    return pl.CostEstimate(flops=1, bytes_accessed=1, transcendentals=0)


def whole(shape):
    return pl.BlockSpec(shape, lambda *_: (0,) * len(shape))


def sds(shape, dtype):
    return jax.ShapeDtypeStruct(shape, dtype)


def body(
    node_x, cotangent, wigner, src_index, dst_index, edge_scale, edge_count, w_zero, w_one, w_two
):
    chan = lax.axis_index("chan")
    brick = lax.axis_index("brick")
    z, core = chan // 2, chan % 2
    high = brick % 2
    z_s = z.astype(jnp.int32).reshape(1)
    k_s = core.astype(jnp.int32).reshape(1)
    h_s = high.astype(jnp.int32).reshape(1)
    slots = src_index.shape[0]
    steps = slots // EB
    src = src_index.reshape(1, slots)
    dst = dst_index.reshape(1, slots)
    scale = edge_scale.reshape(1, slots)

    def across(x, mask):
        return lax.ppermute(x, "chan", [(i, i ^ mask) for i in range(16)])

    def cross(x):
        return lax.ppermute(x, "brick", [(i, i ^ 1) for i in range(32)])

    def shift(x, away):
        route = [(i, (i + (2 if (i % 2 == 0) == away else -2)) % 32) for i in range(32)]
        return lax.ppermute(x, "brick", route)

    w_tiles = (
        w_zero.transpose(0, 2, 1, 3).reshape(49, 8, 128),
        w_one.transpose(0, 1, 3, 2, 4).reshape(72, 8, 128),
        w_two.transpose(0, 1, 3, 2, 4).reshape(50, 8, 128),
    )
    node, b0, rims, w_own = pl.pallas_call(
        pack_kernel,
        out_shape=(sds((400, 128), BF), sds((400, 128), BF), sds((224, 128), BF), sds((1376, 128), BF)),
        in_specs=[whole((n, 8, 128)) for n in (49, 49, 49, 72, 50)],
        out_specs=(whole((400, 128)), whole((400, 128)), whole((224, 128)), whole((1376, 128))),
        grid=(1,),
        compiler_params=pltpu.CompilerParams(vmem_limit_bytes=PACK_VMEM),
        cost_estimate=light(),
        name="pack",
    )(node_x, cotangent, *w_tiles)
    near = cross(rims)

    def rotated(*blocks):
        return rotate_call(z_s, edge_count, blocks, dst, scale, wigner)

    b4 = across(b0, 8)
    b2 = across(b0, 4)
    b1 = across(b0, 2)
    far = shift(lax.dynamic_slice_in_dim(near, 112 * high, 112, 0), True)

    x_own = pl.pallas_call(
        edge_in_kernel,
        out_shape=sds((X_ROWS + 1376, 128), BF),
        grid=(steps,),
        in_specs=[smem(), whole((400, 128)), whole((224, 128)), whole((112, 128)), whole((1376, 128))]
        + [row_spec(), wig_spec()],
        out_specs=whole((X_ROWS + 1376, 128)),
        scratch_shapes=[pltpu.VMEM((235, EB), F32), pltpu.VMEM((400, EB), F32)],
        compiler_params=params(),
        cost_estimate=light(),
        name="edge_in",
    )(h_s, node, near, far, w_own, src, wigner)
    b4, b2, b1, x_own = lax.optimization_barrier((b4, b2, b1, x_own))
    b6 = across(b4, 4)
    b5 = across(b4, 2)
    b3 = across(b2, 2)
    (eg0,) = rotated(b0, b1)

    b6, b5, b3, x_own, eg0 = lax.optimization_barrier((b6, b5, b3, x_own, eg0))
    b7 = across(b6, 2)
    eg1, eg2 = rotated(b2, b3, b4, b5)
    x_sib = across(x_own, 1)

    wz, wo, wt = pl.pallas_call(
        weight_kernel,
        out_shape=(sds((112, 512), BF), sds((192, 768), BF), sds((160, 640), BF)),
        grid=(1,),
        in_specs=[smem(), whole((X_ROWS + 1376, 128)), whole((X_ROWS + 1376, 128))],
        out_specs=(whole((112, 512)), whole((192, 768)), whole((160, 640))),
        compiler_params=params(),
        cost_estimate=light(),
        name="weights",
    )(k_s, x_own, x_sib)

    s_own, g_own, to_sib = edge_call(
        z_s, edge_count, (eg0, eg1, eg2), (b6, b7), dst, src, scale, wigner, x_own, x_sib, (wz, wo, wt)
    )

    got = across(to_sib, 1)
    s_got = got[:1024].reshape(8, 128, 128)
    s_own = s_own.reshape(8, 128, 128)
    send = jnp.concatenate([s_own, s_got], axis=0)
    groups = [
        [
            (2 * (2 * zb + (k ^ p)) + h) * 16 + 2 * zl + k
            for p in range(2)
            for zb in range(8)
        ]
        for h in range(2)
        for zl in range(8)
        for k in range(2)
    ]
    pieces = lax.all_to_all(send, ("brick", "chan"), 0, 0, axis_index_groups=groups)
    summed = pieces.astype(F32).sum(axis=0).reshape(16, 2, 4, 128)
    mine = jnp.where(high == 0, summed[:, 0], summed[:, 1])
    other = jnp.where(high == 0, summed[:, 1], summed[:, 0])

    g_all = g_own + got[1024:].astype(F32)
    left, right = g_all[400:512].astype(BF), g_all[512:624].astype(BF)
    near_rim = jnp.where(high == 0, right, left)
    far_rim = shift(jnp.where(high == 0, left, right), False)

    crossed = cross(jnp.concatenate([near_rim, far_rim, other.astype(BF).reshape(64, 128)], axis=0))
    grad_x = pl.pallas_call(
        join_kernel,
        out_shape=sds((49, 8, 128), F32),
        grid=(1,),
        in_specs=[smem(), whole((624, 128)), whole((288, 128))],
        out_specs=whole((49, 8, 128)),
        compiler_params=params(),
        cost_estimate=light(),
        name="join",
    )(h_s, g_all, crossed)

    zero, one, second = pl.pallas_call(
        finish_kernel,
        out_shape=(sds((7, 7, 4, 8), F32), sds((2, 6, 6, 4, 8), F32), sds((2, 5, 5, 4, 8), F32)),
        grid=(1,),
        in_specs=[whole((64, 128)), whole((288, 128))],
        out_specs=(whole((7, 7, 4, 8)), whole((2, 6, 6, 4, 8)), whole((2, 5, 5, 4, 8))),
        compiler_params=params(),
        cost_estimate=light(),
        name="finish",
    )(mine.reshape(64, 128), crossed)
    grad_zero = zero.transpose(0, 3, 1, 2)
    grad_one = one.transpose(0, 1, 4, 2, 3)
    grad_two = second.transpose(0, 1, 4, 2, 3)
    return grad_x, grad_zero, grad_one, grad_two


def solution(mesh):
    in_specs = (
        P(None, "chan", "brick"),
        P(None, "chan", "brick"),
        P(None, "brick"),
        P("brick"),
        P("brick"),
        P("brick"),
        P("brick"),
        P(None, "chan", None, None),
        P(None, None, "chan", None, None),
        P(None, None, "chan", None, None),
    )
    out_specs = (
        P(None, "chan", "brick"),
        P(None, "chan", None, "brick"),
        P(None, None, "chan", None, "brick"),
        P(None, None, "chan", None, "brick"),
    )
    return jax.shard_map(body, mesh=mesh, in_specs=in_specs, out_specs=out_specs, check_vma=False)
```

```python
import functools

import jax
import jax.numpy as jnp
from jax import lax
from jax.experimental import pallas as pl
from jax.experimental.pallas import tpu as pltpu
from jax.sharding import PartitionSpec as P

BF = jnp.bfloat16
F32 = jnp.float32
EB = 256
LANES = 128
VMEM_LIMIT = 28 * 1024 * 1024
PACK_VMEM = 60 * 1024 * 1024
X_ROWS = 2048
ZORD = (0, 2, 4, 6, 1, 3, 5)

NN = (((1,), (0,)), ((), ()))
NT = (((1,), (1,)), ((), ()))


def mm(a, b, dims=NN):
    return lax.dot_general(a, b, dims, preferred_element_type=F32)


def kept_row(degree, azimuth):
    if azimuth == 0:
        return degree
    if azimuth == 1:
        return 6 + degree
    if azimuth == -1:
        return 12 + degree
    if azimuth == 2:
        return 17 + degree
    return 22 + degree


def wig_row(degree, azimuth, column):
    start = sum((2 * min(k, 2) + 1) * (2 * k + 1) for k in range(degree))
    return start + (azimuth + min(degree, 2)) * (2 * degree + 1) + column


def orders(degree):
    reach = min(degree, 2)
    return range(-reach, reach + 1)


def eg_place(row):
    return ZORD.index(row) if row < 7 else row


def x_place(row):
    if row < 7:
        return row * 8
    if row < 13:
        return 64 + (row - 7) * 8
    if row < 19:
        return 112 + (row - 13) * 8
    if row < 24:
        return 160 + (row - 19) * 8
    return 208 + (row - 24) * 8


def iota(shape, axis):
    return lax.broadcasted_iota(jnp.int32, shape, axis)


def hot(match):
    return jnp.where(match, 1.0, 0.0).astype(BF)


def source_hots(src):
    width = src.shape[1]
    atom = iota((LANES, width), 0)
    own = hot(atom == src - 32)
    before = [hot(atom == jnp.where(src < 32, src + 32 * q, -1)) for q in range(4)]
    after = [hot(atom == jnp.where(src >= 160, src - 160 + 32 * q, -1)) for q in range(4)]
    return own, before, after


def pack_kernel(node_ref, cot_ref, zero_ref, one_ref, two_ref, node_out, cot_out, rim_out, weight_out):
    blank = jnp.zeros((8, LANES), F32)

    def rows(ref):
        return jnp.concatenate([ref[...].astype(F32).reshape(392, LANES), blank], axis=0).astype(BF)

    cot_out[...] = rows(cot_ref)
    node = rows(node_ref)
    node_out[...] = node
    atom, lane = iota((LANES, LANES), 0), iota((LANES, LANES), 1)
    parts = []
    for q in range(4):
        inside = (lane >= 32 * q) & (lane < 32 * q + 32)
        last = hot(inside & (atom == lane - 32 * q + 96))
        first = hot(inside & (atom == lane - 32 * q))
        parts.append(mm(node, jnp.concatenate([last, first], axis=1)))
    total = []
    for g in range(13):
        members = [parts[q][(4 * g + q) * 8 : (4 * g + q) * 8 + 8] for q in range(4) if 4 * g + q < 49]
        total.append(sum(members[1:], members[0]))
    total.append(jnp.zeros((8, 2 * LANES), F32))
    packed = jnp.concatenate(total, axis=0).astype(BF)
    rim_out[:112] = packed[:, :LANES]
    rim_out[112:] = packed[:, LANES:]
    parts = [ref[...].astype(F32).reshape(-1, LANES) for ref in (zero_ref, one_ref, two_ref)]
    weight_out[...] = jnp.concatenate(parts + [blank], axis=0).astype(BF)


def edge_in_kernel(
    h_ref, count_ref, node_ref, near_ref, far_ref, weight_ref, src_ref, dst_ref, scale_ref, wig_ref,
    x_ref, factor_ref, dest_ref, rot, gathered, sem,
):
    step = pl.program_id(0)
    copy = pltpu.make_async_copy(weight_ref, x_ref.at[pl.ds(X_ROWS, 1376)], sem)

    @pl.when(step == 0)
    def _():
        copy.start()

    factor_ref[...] = edge_factor(step, count_ref, scale_ref)
    dest_ref[...] = dst_ref[...]
    h = h_ref[0]
    src = src_ref[...]
    own, before, after = source_hots(src)
    gathered[...] = mm(node_ref[...], own)
    rot[...] = wig_ref[...].astype(F32)
    far = far_ref[...]
    from_before = jnp.where(h == 0, far, near_ref[:112])
    from_after = jnp.where(h == 0, near_ref[112:], far)
    for q in range(4):
        part = mm(from_before, before[q]) + mm(from_after, after[q])
        for g in range(13):
            coef = 4 * g + q
            if coef < 49:
                gathered[coef * 8 : coef * 8 + 8, :] += part[g * 8 : g * 8 + 8]
    rows = {}
    for degree in range(7):
        span = 2 * degree + 1
        vals = [gathered[(degree * degree + j) * 8 : (degree * degree + j + 1) * 8, :] for j in range(span)]
        for m in orders(degree):
            total = None
            for j in range(span):
                at = wig_row(degree, m, j)
                term = rot[at : at + 1, :] * vals[j]
                total = term if total is None else total + term
            rows[kept_row(degree, m)] = total
    blank = jnp.zeros((8, EB), F32)
    groups = [
        (0, [rows[r] for r in range(7)] + [blank]),
        (64, [rows[r] for r in range(7, 13)]),
        (112, [rows[r] for r in range(13, 19)]),
        (160, [rows[r] for r in range(19, 24)] + [blank]),
        (208, [rows[r] for r in range(24, 29)] + [blank]),
    ]
    for start, members in groups:
        block = jnp.concatenate(members, axis=0).astype(BF)
        for half in range(EB // LANES):
            row = pl.multiple_of(step * (256 * EB // LANES) + 256 * half + start, 16)
            x_ref[pl.ds(row, 8 * len(members)), :] = block[:, half * LANES : half * LANES + LANES]

    @pl.when(step == pl.num_programs(0) - 1)
    def _():
        copy.wait()


def weight_kernel(k_ref, own_ref, sib_ref, zero_ref, one_ref, two_ref):
    k = k_ref[0]
    chan, lane = iota((LANES, LANES), 0), iota((LANES, LANES), 1)

    def pick(offset):
        spot = lane - offset
        wanted = (spot // 8) * 16 + k * 8 + spot % 8
        return hot((spot >= 0) & (spot < 64) & (chan == wanted))

    low, high = pick(0), pick(64)
    own, sib = own_ref[X_ROWS:], sib_ref[X_ROWS:]
    sides = [(mm(own, low), mm(own, high)), (mm(sib, low), mm(sib, high))]

    def tile(entries, place):
        halves = []
        for side in sides:
            total = None
            for half, entry in enumerate(entries):
                if entry is None:
                    continue
                sign, at = entry
                piece = side[half][at * 8 : at * 8 + 8]
                piece = piece if sign > 0 else -piece
                total = piece if total is None else total + piece
            halves.append(total)
        return jnp.concatenate(halves, axis=0).astype(BF)

    for lp in range(7):
        for p in range(4):
            entries = [
                (1, lp * 7 + ZORD[n]) if n < 7 else None for n in (2 * p, 2 * p + 1)
            ]
            zero_ref[lp * 16 : lp * 16 + 16, p * 128 : p * 128 + 128] = tile(entries, p)
    for ref, count, base in ((one_ref, 6, 49), (two_ref, 5, 121)):
        for out in range(2):
            for lp in range(count):
                for p in range(count):
                    entries = []
                    for n in (2 * p, 2 * p + 1):
                        inp, l = n // count, n % count
                        which = 0 if inp == out else 1
                        sign = -1 if (out == 1 and inp == 0) else 1
                        entries.append((sign, base + which * count * count + lp * count + l))
                    row = (out * count + lp) * 16
                    ref[row : row + 16, p * 128 : p * 128 + 128] = tile(entries, p)


def rotate_pair(z, near_ref, far_ref, dest, rot, gathered, store):
    gathered[z % 2] = mm(near_ref[...], dest)
    gathered[1 - z % 2] = mm(far_ref[...], dest)
    for half in range(EB // LANES):
        lanes = slice(half * LANES, half * LANES + LANES)
        for degree in range(7):
            span = 2 * degree + 1
            at0 = degree * degree
            cols = [
                [gathered[side, (at0 + j) * 8 : (at0 + j + 1) * 8, lanes] for j in range(span)]
                for side in range(2)
            ]
            for m in orders(degree):
                totals = [None, None]
                for j in range(span):
                    at = wig_row(degree, m, j)
                    coeff = jnp.broadcast_to(rot[at : at + 1, lanes], (8, LANES))
                    for side in range(2):
                        term = coeff * cols[side][j]
                        totals[side] = term if totals[side] is None else totals[side] + term
                place = eg_place(kept_row(degree, m))
                store(place, lanes, jnp.concatenate(totals, axis=0).astype(BF))


def edge_factor(step, count_ref, scale_ref):
    slot = step * EB + iota((1, EB), 1)
    return jnp.where(slot < count_ref[0], 0.25 * scale_ref[...], 0.0)


def rotate_kernel(pairs, z_ref, *refs):
    blocks, (dst_ref, factor_ref, wig_ref), outs = refs[: 2 * pairs], refs[2 * pairs : 2 * pairs + 3], refs[2 * pairs + 3 : -2]
    gathered, rot = refs[-2:]
    rot[...] = wig_ref[...].astype(F32) * factor_ref[...]
    dest = hot(iota((LANES, EB), 0) == dst_ref[...])
    for pair, eg_ref in enumerate(outs):

        def store(place, lanes, tile, eg_ref=eg_ref):
            eg_ref[place * 16 : place * 16 + 16, lanes] = tile

        near_ref, far_ref = blocks[2 * pair : 2 * pair + 2]
        rotate_pair(z_ref[0], near_ref, far_ref, dest, rot, gathered.at[pair], store)


def edge_kernel(
    z_ref, eg0, eg1, eg2, near_ref, far_ref,
    dst_ref, src_ref, factor_ref, wig_ref, xo_ref, xs_ref, zero_ref, one_ref, two_ref,
    so_ref, go_ref, sib_ref,
    gathered, rot, plain, eg, acc, back, full, atoms, rims,
):
    step = pl.program_id(0)

    @pl.when(step == 0)
    def _():
        acc[...] = jnp.zeros_like(acc)
        atoms[...] = jnp.zeros_like(atoms)
        rims[...] = jnp.zeros_like(rims)

    z = z_ref[0]
    entries = wig_ref[...].astype(F32)
    plain[...] = entries
    rot[...] = entries * factor_ref[...]
    dest = hot(iota((LANES, EB), 0) == dst_ref[...])

    def rows_of(place, n):
        return pl.ds(pl.multiple_of(place * 64 + ((z // 2) ^ n) * 16, 16), 16)

    def store(place, lanes, tile):
        eg[rows_of(place, 3), lanes] = tile

    rotate_pair(z, near_ref, far_ref, dest, rot, gathered, store)
    for n, ref in ((0, eg0), (1, eg1), (2, eg2)):
        for place in range(29):
            eg[rows_of(place, n), :] = ref[place * 16 : place * 16 + 16]

    def stacked(*pieces):
        return jnp.concatenate(pieces, axis=0)

    def blank(rows):
        return jnp.zeros((rows, EB), BF)

    def tiles_of(ref):
        return jnp.concatenate([ref[256 * n : 256 * n + 256] for n in range(EB // LANES)], axis=1)

    xo, xs = tiles_of(xo_ref), tiles_of(xs_ref)
    acc[0:448] += mm(eg[0:448], stacked(xo[:64], blank(64), xs[:64], blank(64)), NT)
    for start, count, plus, minus in ((448, 6, 64, 112), (1216, 5, 160, 208)):
        ahead = stacked(
            xo[plus : plus + 48], -xo[minus : minus + 48], blank(32),
            xs[plus : plus + 48], -xs[minus : minus + 48], blank(32),
        )
        cross = stacked(
            xo[minus : minus + 48], xo[plus : plus + 48], blank(32),
            xs[minus : minus + 48], xs[plus : plus + 48], blank(32),
        )
        size = count * 64
        at = 448 if count == 6 else 832
        acc[at : at + size] += mm(eg[start : start + size], ahead, NT) + mm(
            eg[start + size : start + 2 * size], cross, NT
        )

    back[0:112] = mm(zero_ref[:, 0:448], eg[0:448])
    back[112:304] = mm(one_ref[...], eg[448:1216])
    back[304:464] = mm(two_ref[...], eg[1216:1856])
    quarter_start = (0, 13, 25, 37)
    for half in range(EB // LANES):
        lanes = slice(half * LANES, half * LANES + LANES)
        for degree in range(7):
            vals_m = {
                m: back[kept_row(degree, m) * 16 : kept_row(degree, m) * 16 + 16, lanes]
                for m in orders(degree)
            }
            for j in range(2 * degree + 1):
                total = None
                for m in orders(degree):
                    at = wig_row(degree, m, j)
                    term = plain[at : at + 1, lanes] * vals_m[m]
                    total = term if total is None else total + term
                coef = degree * degree + j
                row = (quarter_start[coef % 4] + coef // 4) * 16
                full[row : row + 16, lanes] = total.astype(BF)
    own, before, after = source_hots(src_ref[...])
    for q in range(4):
        start, size = quarter_start[q] * 16, (13 if q == 0 else 12) * 16
        rows = full[start : start + size]
        atoms[start : start + size] += mm(rows, own, NT)
        rims[0:size] += mm(rows, jnp.concatenate([before[q], after[q]], axis=0), NT)

    @pl.when(step == pl.num_programs(0) - 1)
    def _():
        for zb in range(8):
            tiles = []
            spot = zb * 8
            for t in range(4):
                tile = acc[t * 64 + spot : t * 64 + spot + 8]
                if t < 3:
                    odd = acc[256 + t * 64 + spot : 256 + t * 64 + spot + 8]
                    halves = [pltpu.roll(odd[:, n : n + LANES], 64, 1) for n in (0, LANES)]
                    tile = tile + jnp.concatenate(halves, axis=1)
                tiles.append(tile)
            for n in range(11):
                tiles.append(acc[448 + n * 64 + spot : 448 + n * 64 + spot + 8])
            tiles.append(jnp.zeros((8, 2 * LANES), F32))
            whole_tile = jnp.concatenate(tiles, axis=0).astype(BF)
            so_ref[zb * 128 : zb * 128 + 128] = whole_tile[:, :LANES]
            sib_ref[zb * 128 : zb * 128 + 128] = whole_tile[:, LANES:]
        for side in range(2):
            tiles = []
            for coef in range(49):
                row = (quarter_start[coef % 4] + coef // 4) * 16 + side * 8
                tiles.append(atoms[row : row + 8])
            tiles.append(jnp.zeros((8, LANES), F32))
            for rim in range(2):
                for g in range(13):
                    row = g * 16 + side * 8
                    tiles.append(rims[row : row + 8, rim * LANES : rim * LANES + LANES])
                tiles.append(jnp.zeros((8, LANES), F32))
            if side == 0:
                go_ref[...] = jnp.concatenate(tiles, axis=0)
            else:
                sib_ref[1024:1648] = jnp.concatenate(tiles, axis=0).astype(BF)


def row_spec():
    return pl.BlockSpec((1, EB), lambda i: (0, i))


def wig_spec():
    return pl.BlockSpec((235, EB), lambda i: (0, i))


def rotate_call(z_s, blocks, dst, factor, wigner):
    slots = dst.shape[1]
    pairs = len(blocks) // 2
    return pl.pallas_call(
        functools.partial(rotate_kernel, pairs),
        out_shape=[sds((464, slots), BF)] * pairs,
        grid=(slots // EB,),
        in_specs=[smem()] + [whole((400, 128))] * len(blocks) + [row_spec(), row_spec(), wig_spec()],
        out_specs=[pl.BlockSpec((464, EB), lambda i: (0, i))] * pairs,
        scratch_shapes=[pltpu.VMEM((pairs, 2, 400, EB), F32), pltpu.VMEM((235, EB), F32)],
        compiler_params=params(),
        name="rotate",
    )(z_s, *blocks, dst, factor, wigner)


def edge_call(z_s, egs, pair, dst, src, factor, wigner, x_own, x_sib, weights):
    slots = dst.shape[1]
    x_spec = pl.BlockSpec((256 * EB // LANES, LANES), lambda i: (i, 0))
    return pl.pallas_call(
        edge_kernel,
        out_shape=(sds((1024, 128), BF), sds((624, 128), F32), sds((1648, 128), BF)),
        grid=(slots // EB,),
        in_specs=[smem()]
        + [pl.BlockSpec((464, EB), lambda i: (0, i))] * 3
        + [whole((400, 128)), whole((400, 128)), row_spec(), row_spec(), row_spec(), wig_spec(), x_spec, x_spec]
        + [whole((112, 512)), whole((192, 768)), whole((160, 640))],
        out_specs=(whole((1024, 128)), whole((624, 128)), whole((1648, 128))),
        scratch_shapes=[
            pltpu.VMEM((2, 400, EB), F32),
            pltpu.VMEM((235, EB), F32),
            pltpu.VMEM((235, EB), F32),
            pltpu.VMEM((1856, EB), BF),
            pltpu.VMEM((1152, 256), F32),
            pltpu.VMEM((464, EB), F32),
            pltpu.VMEM((784, EB), BF),
            pltpu.VMEM((784, LANES), F32),
            pltpu.VMEM((208, 2 * LANES), F32),
        ],
        compiler_params=params(),
        name="edge",
    )(z_s, *egs, *pair, dst, src, factor, wigner, x_own, x_sib, *weights)


def finish(mine_ref, got_ref, zero_ref, one_ref, two_ref):
    total = mine_ref[...] + got_ref[224:288].astype(F32)

    def moved(lane):
        return total if lane == 0 else pltpu.roll(total, LANES - lane, 1)

    for lp in range(7):
        even, odd = moved(lp * 8), moved(64 + lp * 8)
        for n, l in enumerate(ZORD):
            source, row = (even, n * 4) if n < 4 else (odd, (n - 4) * 4)
            zero_ref[lp, l] = source[row : row + 4, 0:8]
    for ref, count, first, stride in ((one_ref, 6, 4, 48), (two_ref, 5, 10, 48)):
        for w in range(2):
            for lp in range(count):
                source = moved(w * stride + lp * 8)
                for l in range(count):
                    row = (first + l) * 4
                    ref[w, lp, l] = source[row : row + 4, 0:8]


def end_kernel(h_ref, own_ref, mine_ref, rim_ref, out_ref, zero_ref, one_ref, two_ref):
    finish(mine_ref, rim_ref, zero_ref, one_ref, two_ref)
    h = h_ref[0]
    base_a = jnp.where(h == 0, 96, 0)
    base_b = 96 - base_a
    lane, atom = iota((LANES, LANES), 0), iota((LANES, LANES), 1)
    ra, rb = rim_ref[0:112], rim_ref[112:224]
    for q in range(4):
        inside = (lane >= 32 * q) & (lane < 32 * q + 32)
        put_a = hot(inside & (atom == lane - 32 * q + base_a))
        put_b = hot(inside & (atom == lane - 32 * q + base_b))
        part = mm(ra, put_a) + mm(rb, put_b)
        for g in range(13):
            coef = 4 * g + q
            if coef < 49:
                out_ref[coef] = own_ref[coef * 8 : coef * 8 + 8] + part[g * 8 : g * 8 + 8]


def smem():
    return pl.BlockSpec(memory_space=pltpu.SMEM)


def params():
    return pltpu.CompilerParams(vmem_limit_bytes=VMEM_LIMIT)


def light():
    return pl.CostEstimate(flops=1, bytes_accessed=1, transcendentals=0)


def whole(shape):
    return pl.BlockSpec(shape, lambda *_: (0,) * len(shape))


def sds(shape, dtype):
    return jax.ShapeDtypeStruct(shape, dtype)


def body(
    node_x, cotangent, wigner, src_index, dst_index, edge_scale, edge_count, w_zero, w_one, w_two
):
    chan = lax.axis_index("chan")
    brick = lax.axis_index("brick")
    z, core = chan // 2, chan % 2
    high = brick % 2
    z_s = z.astype(jnp.int32).reshape(1)
    k_s = core.astype(jnp.int32).reshape(1)
    h_s = high.astype(jnp.int32).reshape(1)
    slots = src_index.shape[0]
    steps = slots // EB
    src = src_index.reshape(1, slots)
    dst = dst_index.reshape(1, slots)
    scale = edge_scale.reshape(1, slots)

    def across(x, mask):
        return lax.ppermute(x, "chan", [(i, i ^ mask) for i in range(16)])

    def cross(x):
        return lax.ppermute(x, "brick", [(i, i ^ 1) for i in range(32)])

    def shift(x, away):
        route = [(i, (i + (2 if (i % 2 == 0) == away else -2)) % 32) for i in range(32)]
        return lax.ppermute(x, "brick", route)

    w_tiles = (
        w_zero.transpose(0, 2, 1, 3).reshape(49, 8, 128),
        w_one.transpose(0, 1, 3, 2, 4).reshape(72, 8, 128),
        w_two.transpose(0, 1, 3, 2, 4).reshape(50, 8, 128),
    )
    node, b0, rims, w_own = pl.pallas_call(
        pack_kernel,
        out_shape=(sds((400, 128), BF), sds((400, 128), BF), sds((224, 128), BF), sds((1376, 128), BF)),
        in_specs=[whole((n, 8, 128)) for n in (49, 49, 49, 72, 50)],
        out_specs=(whole((400, 128)), whole((400, 128)), whole((224, 128)), whole((1376, 128))),
        grid=(1,),
        compiler_params=pltpu.CompilerParams(vmem_limit_bytes=PACK_VMEM),
        cost_estimate=light(),
        name="pack",
    )(node_x, cotangent, *w_tiles)
    near = cross(rims)

    def rotated(*blocks):
        return rotate_call(z_s, blocks, dest, factor, wigner)

    b4 = across(b0, 8)
    b2 = across(b0, 4)
    b1 = across(b0, 2)
    far = shift(lax.dynamic_slice_in_dim(near, 112 * high, 112, 0), True)

    x_own, factor, dest = pl.pallas_call(
        edge_in_kernel,
        out_shape=(sds((X_ROWS + 1376, 128), BF), sds((1, slots), F32), sds((1, slots), jnp.int32)),
        grid=(steps,),
        in_specs=[smem(), smem(), whole((400, 128)), whole((224, 128)), whole((112, 128))]
        + [pl.BlockSpec(memory_space=pltpu.HBM), row_spec(), row_spec(), row_spec(), wig_spec()],
        out_specs=(whole((X_ROWS + 1376, 128)), row_spec(), row_spec()),
        scratch_shapes=[pltpu.VMEM((235, EB), F32), pltpu.VMEM((400, EB), F32), pltpu.SemaphoreType.DMA],
        compiler_params=params(),
        cost_estimate=light(),
        name="edge_in",
    )(h_s, edge_count, node, near, far, w_own, src, dst, scale, wigner)
    b4, b2, b1, x_own = lax.optimization_barrier((b4, b2, b1, x_own))
    b6 = across(b4, 4)
    b5 = across(b4, 2)
    b3 = across(b2, 2)
    (eg0,) = rotated(b0, b1)

    b6, b5, b3, x_own, eg0 = lax.optimization_barrier((b6, b5, b3, x_own, eg0))
    b7 = across(b6, 2)
    eg1, eg2 = rotated(b2, b3, b4, b5)
    x_sib = across(x_own, 1)

    wz, wo, wt = pl.pallas_call(
        weight_kernel,
        out_shape=(sds((112, 512), BF), sds((192, 768), BF), sds((160, 640), BF)),
        grid=(1,),
        in_specs=[smem(), whole((X_ROWS + 1376, 128)), whole((X_ROWS + 1376, 128))],
        out_specs=(whole((112, 512)), whole((192, 768)), whole((160, 640))),
        compiler_params=params(),
        cost_estimate=light(),
        name="weights",
    )(k_s, x_own, x_sib)

    s_own, g_own, to_sib = edge_call(
        z_s, (eg0, eg1, eg2), (b6, b7), dest, src, factor, wigner, x_own, x_sib, (wz, wo, wt)
    )

    got = across(to_sib, 1)
    s_got = got[:1024].reshape(8, 128, 128)
    s_own = s_own.reshape(8, 128, 128)
    send = jnp.concatenate([s_own, s_got], axis=0)
    groups = [
        [
            (2 * (2 * zb + (k ^ p)) + h) * 16 + 2 * zl + k
            for p in range(2)
            for zb in range(8)
        ]
        for h in range(2)
        for zl in range(8)
        for k in range(2)
    ]
    pieces = lax.all_to_all(send, ("brick", "chan"), 0, 0, axis_index_groups=groups)
    summed = pieces.astype(F32).sum(axis=0).reshape(16, 2, 4, 128)
    mine = jnp.where(high == 0, summed[:, 0], summed[:, 1])
    other = jnp.where(high == 0, summed[:, 1], summed[:, 0])

    g_all = g_own + got[1024:].astype(F32)
    left, right = g_all[400:512].astype(BF), g_all[512:624].astype(BF)
    near_rim = jnp.where(high == 0, right, left)
    far_rim = shift(jnp.where(high == 0, left, right), False)

    crossed = cross(jnp.concatenate([near_rim, far_rim, other.astype(BF).reshape(64, 128)], axis=0))
    grad_x, zero, one, second = pl.pallas_call(
        end_kernel,
        out_shape=(
            sds((49, 8, 128), F32),
            sds((7, 7, 4, 8), F32),
            sds((2, 6, 6, 4, 8), F32),
            sds((2, 5, 5, 4, 8), F32),
        ),
        grid=(1,),
        in_specs=[smem(), whole((624, 128)), whole((64, 128)), whole((288, 128))],
        out_specs=(
            whole((49, 8, 128)),
            whole((7, 7, 4, 8)),
            whole((2, 6, 6, 4, 8)),
            whole((2, 5, 5, 4, 8)),
        ),
        compiler_params=params(),
        name="end",
    )(h_s, g_all, mine.reshape(64, 128), crossed)
    grad_zero = zero.transpose(0, 3, 1, 2)
    grad_one = one.transpose(0, 1, 4, 2, 3)
    grad_two = second.transpose(0, 1, 4, 2, 3)
    return grad_x, grad_zero, grad_one, grad_two


def solution(mesh):
    in_specs = (
        P(None, "chan", "brick"),
        P(None, "chan", "brick"),
        P(None, "brick"),
        P("brick"),
        P("brick"),
        P("brick"),
        P("brick"),
        P(None, "chan", None, None),
        P(None, None, "chan", None, None),
        P(None, None, "chan", None, None),
    )
    out_specs = (
        P(None, "chan", "brick"),
        P(None, "chan", None, "brick"),
        P(None, None, "chan", None, "brick"),
        P(None, None, "chan", None, "brick"),
    )
    return jax.shard_map(body, mesh=mesh, in_specs=in_specs, out_specs=out_specs, check_vma=False)
```

```python
import functools

import jax
import jax.numpy as jnp
from jax import lax
from jax.experimental import pallas as pl
from jax.experimental.pallas import tpu as pltpu
from jax.sharding import PartitionSpec as P

BF = jnp.bfloat16
F32 = jnp.float32
EB = 256
LANES = 128
VMEM_LIMIT = 28 * 1024 * 1024
PACK_VMEM = 60 * 1024 * 1024
X_ROWS = 2048
ZORD = (0, 2, 4, 6, 1, 3, 5)

NN = (((1,), (0,)), ((), ()))
NT = (((1,), (1,)), ((), ()))


def mm(a, b, dims=NN):
    return lax.dot_general(a, b, dims, preferred_element_type=F32)


def kept_row(degree, azimuth):
    if azimuth == 0:
        return degree
    if azimuth == 1:
        return 6 + degree
    if azimuth == -1:
        return 12 + degree
    if azimuth == 2:
        return 17 + degree
    return 22 + degree


def wig_row(degree, azimuth, column):
    start = sum((2 * min(k, 2) + 1) * (2 * k + 1) for k in range(degree))
    return start + (azimuth + min(degree, 2)) * (2 * degree + 1) + column


def orders(degree):
    reach = min(degree, 2)
    return range(-reach, reach + 1)


def eg_place(row):
    return ZORD.index(row) if row < 7 else row


def x_place(row):
    if row < 7:
        return row * 8
    if row < 13:
        return 64 + (row - 7) * 8
    if row < 19:
        return 112 + (row - 13) * 8
    if row < 24:
        return 160 + (row - 19) * 8
    return 208 + (row - 24) * 8


def iota(shape, axis):
    return lax.broadcasted_iota(jnp.int32, shape, axis)


def hot(match):
    return jnp.where(match, 1.0, 0.0).astype(BF)


def source_hots(src):
    width = src.shape[1]
    atom = iota((LANES, width), 0)
    own = hot(atom == src - 32)
    before = [hot(atom == jnp.where(src < 32, src + 32 * q, -1)) for q in range(4)]
    after = [hot(atom == jnp.where(src >= 160, src - 160 + 32 * q, -1)) for q in range(4)]
    return own, before, after


def pack_kernel(node_ref, cot_ref, zero_ref, one_ref, two_ref, node_out, cot_out, rim_out, weight_out):
    blank = jnp.zeros((8, LANES), F32)

    def rows(ref):
        return jnp.concatenate([ref[...].astype(F32).reshape(392, LANES), blank], axis=0).astype(BF)

    cot_out[...] = rows(cot_ref)
    node = rows(node_ref)
    node_out[...] = node
    atom, lane = iota((LANES, LANES), 0), iota((LANES, LANES), 1)
    parts = []
    for q in range(4):
        inside = (lane >= 32 * q) & (lane < 32 * q + 32)
        last = hot(inside & (atom == lane - 32 * q + 96))
        first = hot(inside & (atom == lane - 32 * q))
        parts.append(mm(node, jnp.concatenate([last, first], axis=1)))
    total = []
    for g in range(13):
        members = [parts[q][(4 * g + q) * 8 : (4 * g + q) * 8 + 8] for q in range(4) if 4 * g + q < 49]
        total.append(sum(members[1:], members[0]))
    total.append(jnp.zeros((8, 2 * LANES), F32))
    packed = jnp.concatenate(total, axis=0).astype(BF)
    rim_out[:112] = packed[:, :LANES]
    rim_out[112:] = packed[:, LANES:]
    parts = [ref[...].astype(F32).reshape(-1, LANES) for ref in (zero_ref, one_ref, two_ref)]
    weight_out[...] = jnp.concatenate(parts + [blank], axis=0).astype(BF)


def edge_in_kernel(
    h_ref, count_ref, node_ref, near_ref, far_ref, weight_ref, src_ref, dst_ref, scale_ref, wig_ref,
    x_ref, factor_ref, dest_ref, rot, gathered, sem,
):
    step = pl.program_id(0)
    copy = pltpu.make_async_copy(weight_ref, x_ref.at[pl.ds(X_ROWS, 1376)], sem)

    @pl.when(step == 0)
    def _():
        copy.start()

    factor_ref[...] = edge_factor(step, count_ref, scale_ref)
    dest_ref[...] = dst_ref[...]
    h = h_ref[0]
    src = src_ref[...]
    own, before, after = source_hots(src)
    gathered[...] = mm(node_ref[...], own)
    rot[...] = wig_ref[...].astype(F32)
    far = far_ref[...]
    from_before = jnp.where(h == 0, far, near_ref[:112])
    from_after = jnp.where(h == 0, near_ref[112:], far)
    for q in range(4):
        part = mm(from_before, before[q]) + mm(from_after, after[q])
        for g in range(13):
            coef = 4 * g + q
            if coef < 49:
                gathered[coef * 8 : coef * 8 + 8, :] += part[g * 8 : g * 8 + 8]
    rows = {}
    for degree in range(7):
        span = 2 * degree + 1
        vals = [gathered[(degree * degree + j) * 8 : (degree * degree + j + 1) * 8, :] for j in range(span)]
        for m in orders(degree):
            total = None
            for j in range(span):
                at = wig_row(degree, m, j)
                term = rot[at : at + 1, :] * vals[j]
                total = term if total is None else total + term
            rows[kept_row(degree, m)] = total
    blank = jnp.zeros((8, EB), F32)
    groups = [
        (0, [rows[r] for r in range(7)] + [blank]),
        (64, [rows[r] for r in range(7, 13)]),
        (112, [rows[r] for r in range(13, 19)]),
        (160, [rows[r] for r in range(19, 24)] + [blank]),
        (208, [rows[r] for r in range(24, 29)] + [blank]),
    ]
    for start, members in groups:
        block = jnp.concatenate(members, axis=0).astype(BF)
        for half in range(EB // LANES):
            row = pl.multiple_of(step * (256 * EB // LANES) + 256 * half + start, 16)
            x_ref[pl.ds(row, 8 * len(members)), :] = block[:, half * LANES : half * LANES + LANES]

    @pl.when(step == pl.num_programs(0) - 1)
    def _():
        copy.wait()


def weight_kernel(k_ref, own_ref, sib_ref, zero_ref, one_ref, two_ref):
    k = k_ref[0]
    chan, lane = iota((LANES, LANES), 0), iota((LANES, LANES), 1)

    def pick(offset):
        spot = lane - offset
        wanted = (spot // 8) * 16 + k * 8 + spot % 8
        return hot((spot >= 0) & (spot < 64) & (chan == wanted))

    low, high = pick(0), pick(64)
    own, sib = own_ref[X_ROWS:], sib_ref[X_ROWS:]
    sides = [(mm(own, low), mm(own, high)), (mm(sib, low), mm(sib, high))]

    def tile(entries, place):
        halves = []
        for side in sides:
            total = None
            for half, entry in enumerate(entries):
                if entry is None:
                    continue
                sign, at = entry
                piece = side[half][at * 8 : at * 8 + 8]
                piece = piece if sign > 0 else -piece
                total = piece if total is None else total + piece
            halves.append(total)
        return jnp.concatenate(halves, axis=0).astype(BF)

    for lp in range(7):
        for p in range(4):
            entries = [
                (1, lp * 7 + ZORD[n]) if n < 7 else None for n in (2 * p, 2 * p + 1)
            ]
            zero_ref[lp * 16 : lp * 16 + 16, p * 128 : p * 128 + 128] = tile(entries, p)
    for ref, count, base in ((one_ref, 6, 49), (two_ref, 5, 121)):
        for out in range(2):
            for lp in range(count):
                for p in range(count):
                    entries = []
                    for n in (2 * p, 2 * p + 1):
                        inp, l = n // count, n % count
                        which = 0 if inp == out else 1
                        sign = -1 if (out == 1 and inp == 0) else 1
                        entries.append((sign, base + which * count * count + lp * count + l))
                    row = (out * count + lp) * 16
                    ref[row : row + 16, p * 128 : p * 128 + 128] = tile(entries, p)


def rotate_pair(z, near_ref, far_ref, dest, rot, gathered, store):
    gathered[z % 2] = mm(near_ref[...], dest)
    gathered[1 - z % 2] = mm(far_ref[...], dest)
    for half in range(EB // LANES):
        lanes = slice(half * LANES, half * LANES + LANES)
        for degree in range(7):
            span = 2 * degree + 1
            at0 = degree * degree
            cols = [
                [gathered[side, (at0 + j) * 8 : (at0 + j + 1) * 8, lanes] for j in range(span)]
                for side in range(2)
            ]
            for m in orders(degree):
                totals = [None, None]
                for j in range(span):
                    at = wig_row(degree, m, j)
                    coeff = jnp.broadcast_to(rot[at : at + 1, lanes], (8, LANES))
                    for side in range(2):
                        term = coeff * cols[side][j]
                        totals[side] = term if totals[side] is None else totals[side] + term
                place = eg_place(kept_row(degree, m))
                store(place, lanes, jnp.concatenate(totals, axis=0).astype(BF))


def edge_factor(step, count_ref, scale_ref):
    slot = step * EB + iota((1, EB), 1)
    return jnp.where(slot < count_ref[0], 0.25 * scale_ref[...], 0.0)


def rotate_kernel(pairs, z_ref, *refs):
    blocks, (dst_ref, factor_ref, wig_ref), outs = refs[: 2 * pairs], refs[2 * pairs : 2 * pairs + 3], refs[2 * pairs + 3 : -2]
    gathered, rot = refs[-2:]
    rot[...] = wig_ref[...].astype(F32) * factor_ref[...]
    dest = hot(iota((LANES, EB), 0) == dst_ref[...])
    for pair, eg_ref in enumerate(outs):

        def store(place, lanes, tile, eg_ref=eg_ref):
            eg_ref[place * 16 : place * 16 + 16, lanes] = tile

        near_ref, far_ref = blocks[2 * pair : 2 * pair + 2]
        rotate_pair(z_ref[0], near_ref, far_ref, dest, rot, gathered.at[pair], store)


def edge_kernel(
    z_ref, eg0, eg1, eg2, near_ref, far_ref,
    dst_ref, src_ref, factor_ref, wig_ref, xo_ref, xs_ref, zero_ref, one_ref, two_ref,
    so_ref, go_ref, sib_ref,
    gathered, rot, plain, eg, acc, back, full, atoms, rims,
):
    step = pl.program_id(0)

    @pl.when(step == 0)
    def _():
        acc[...] = jnp.zeros_like(acc)
        atoms[...] = jnp.zeros_like(atoms)
        rims[...] = jnp.zeros_like(rims)

    z = z_ref[0]
    entries = wig_ref[...].astype(F32)
    plain[...] = entries
    rot[...] = entries * factor_ref[...]
    dest = hot(iota((LANES, EB), 0) == dst_ref[...])

    def rows_of(place, n):
        return pl.ds(pl.multiple_of(place * 64 + ((z // 2) ^ n) * 16, 16), 16)

    def store(place, lanes, tile):
        eg[rows_of(place, 3), lanes] = tile

    rotate_pair(z, near_ref, far_ref, dest, rot, gathered, store)
    for n, ref in ((0, eg0), (1, eg1), (2, eg2)):
        for place in range(29):
            eg[rows_of(place, n), :] = ref[place * 16 : place * 16 + 16]

    def stacked(*pieces):
        return jnp.concatenate(pieces, axis=0)

    def blank(rows):
        return jnp.zeros((rows, EB), BF)

    def tiles_of(ref):
        return jnp.concatenate([ref[256 * n : 256 * n + 256] for n in range(EB // LANES)], axis=1)

    xo, xs = tiles_of(xo_ref), tiles_of(xs_ref)
    acc[0:448] += mm(eg[0:448], stacked(xo[:64], blank(64), xs[:64], blank(64)), NT)
    for start, count, plus, minus in ((448, 6, 64, 112), (1216, 5, 160, 208)):
        ahead = stacked(
            xo[plus : plus + 48], -xo[minus : minus + 48], blank(32),
            xs[plus : plus + 48], -xs[minus : minus + 48], blank(32),
        )
        cross = stacked(
            xo[minus : minus + 48], xo[plus : plus + 48], blank(32),
            xs[minus : minus + 48], xs[plus : plus + 48], blank(32),
        )
        size = count * 64
        at = 448 if count == 6 else 832
        acc[at : at + size] += mm(eg[start : start + size], ahead, NT) + mm(
            eg[start + size : start + 2 * size], cross, NT
        )

    back[0:112] = mm(zero_ref[:, 0:448], eg[0:448])
    back[112:304] = mm(one_ref[...], eg[448:1216])
    back[304:464] = mm(two_ref[...], eg[1216:1856])
    quarter_start = (0, 13, 25, 37)
    for half in range(EB // LANES):
        lanes = slice(half * LANES, half * LANES + LANES)
        for degree in range(7):
            vals_m = {
                m: back[kept_row(degree, m) * 16 : kept_row(degree, m) * 16 + 16, lanes]
                for m in orders(degree)
            }
            for j in range(2 * degree + 1):
                total = None
                for m in orders(degree):
                    at = wig_row(degree, m, j)
                    term = plain[at : at + 1, lanes] * vals_m[m]
                    total = term if total is None else total + term
                coef = degree * degree + j
                row = (quarter_start[coef % 4] + coef // 4) * 16
                full[row : row + 16, lanes] = total.astype(BF)
    own, before, after = source_hots(src_ref[...])
    for q in range(4):
        start, size = quarter_start[q] * 16, (13 if q == 0 else 12) * 16
        rows = full[start : start + size]
        atoms[start : start + size] += mm(rows, own, NT)
        rims[0:size] += mm(rows, jnp.concatenate([before[q], after[q]], axis=0), NT)

    @pl.when(step == pl.num_programs(0) - 1)
    def _():
        for zb in range(8):
            tiles = []
            spot = zb * 8
            for t in range(4):
                tile = acc[t * 64 + spot : t * 64 + spot + 8]
                if t < 3:
                    odd = acc[256 + t * 64 + spot : 256 + t * 64 + spot + 8]
                    halves = [pltpu.roll(odd[:, n : n + LANES], 64, 1) for n in (0, LANES)]
                    tile = tile + jnp.concatenate(halves, axis=1)
                tiles.append(tile)
            for n in range(11):
                tiles.append(acc[448 + n * 64 + spot : 448 + n * 64 + spot + 8])
            tiles.append(jnp.zeros((8, 2 * LANES), F32))
            whole_tile = jnp.concatenate(tiles, axis=0).astype(BF)
            so_ref[zb * 128 : zb * 128 + 128] = whole_tile[:, :LANES]
            sib_ref[zb * 128 : zb * 128 + 128] = whole_tile[:, LANES:]
        for side in range(2):
            tiles = []
            for coef in range(49):
                row = (quarter_start[coef % 4] + coef // 4) * 16 + side * 8
                tiles.append(atoms[row : row + 8])
            tiles.append(jnp.zeros((8, LANES), F32))
            for rim in range(2):
                for g in range(13):
                    row = g * 16 + side * 8
                    tiles.append(rims[row : row + 8, rim * LANES : rim * LANES + LANES])
                tiles.append(jnp.zeros((8, LANES), F32))
            if side == 0:
                go_ref[...] = jnp.concatenate(tiles, axis=0)
            else:
                sib_ref[1024:1648] = jnp.concatenate(tiles, axis=0).astype(BF)


def row_spec():
    return pl.BlockSpec((1, EB), lambda i: (0, i))


def wig_spec():
    return pl.BlockSpec((235, EB), lambda i: (0, i))


def rotate_call(z_s, blocks, dst, factor, wigner):
    slots = dst.shape[1]
    pairs = len(blocks) // 2
    return pl.pallas_call(
        functools.partial(rotate_kernel, pairs),
        out_shape=[sds((464, slots), BF)] * pairs,
        grid=(slots // EB,),
        in_specs=[smem()] + [whole((400, 128))] * len(blocks) + [row_spec(), row_spec(), wig_spec()],
        out_specs=[pl.BlockSpec((464, EB), lambda i: (0, i))] * pairs,
        scratch_shapes=[pltpu.VMEM((pairs, 2, 400, EB), F32), pltpu.VMEM((235, EB), F32)],
        compiler_params=params(),
        name="rotate",
    )(z_s, *blocks, dst, factor, wigner)


def edge_call(z_s, egs, pair, dst, src, factor, wigner, x_own, x_sib, weights):
    slots = dst.shape[1]
    x_spec = pl.BlockSpec((256 * EB // LANES, LANES), lambda i: (i, 0))
    return pl.pallas_call(
        edge_kernel,
        out_shape=(sds((1024, 128), BF), sds((624, 128), F32), sds((1648, 128), BF)),
        grid=(slots // EB,),
        in_specs=[smem()]
        + [pl.BlockSpec((464, EB), lambda i: (0, i))] * 3
        + [whole((400, 128)), whole((400, 128)), row_spec(), row_spec(), row_spec(), wig_spec(), x_spec, x_spec]
        + [whole((112, 512)), whole((192, 768)), whole((160, 640))],
        out_specs=(whole((1024, 128)), whole((624, 128)), whole((1648, 128))),
        scratch_shapes=[
            pltpu.VMEM((2, 400, EB), F32),
            pltpu.VMEM((235, EB), F32),
            pltpu.VMEM((235, EB), F32),
            pltpu.VMEM((1856, EB), BF),
            pltpu.VMEM((1152, 256), F32),
            pltpu.VMEM((464, EB), F32),
            pltpu.VMEM((784, EB), BF),
            pltpu.VMEM((784, LANES), F32),
            pltpu.VMEM((208, 2 * LANES), F32),
        ],
        compiler_params=params(),
        name="edge",
    )(z_s, *egs, *pair, dst, src, factor, wigner, x_own, x_sib, *weights)


def finish(mine_ref, got_ref, zero_ref, one_ref, two_ref):
    total = mine_ref[...] + got_ref[224:288].astype(F32)

    def moved(lane):
        return total if lane == 0 else pltpu.roll(total, LANES - lane, 1)

    for lp in range(7):
        even, odd = moved(lp * 8), moved(64 + lp * 8)
        for n, l in enumerate(ZORD):
            source, row = (even, n * 4) if n < 4 else (odd, (n - 4) * 4)
            zero_ref[lp, l] = source[row : row + 4, 0:8]
    for ref, count, first, stride in ((one_ref, 6, 4, 48), (two_ref, 5, 10, 48)):
        for w in range(2):
            for lp in range(count):
                source = moved(w * stride + lp * 8)
                for l in range(count):
                    row = (first + l) * 4
                    ref[w, lp, l] = source[row : row + 4, 0:8]


def end_kernel(h_ref, own_ref, mine_ref, rim_ref, out_ref, zero_ref, one_ref, two_ref):
    finish(mine_ref, rim_ref, zero_ref, one_ref, two_ref)
    h = h_ref[0]
    base_a = jnp.where(h == 0, 96, 0)
    base_b = 96 - base_a
    lane, atom = iota((LANES, LANES), 0), iota((LANES, LANES), 1)
    ra, rb = rim_ref[0:112], rim_ref[112:224]
    for q in range(4):
        inside = (lane >= 32 * q) & (lane < 32 * q + 32)
        put_a = hot(inside & (atom == lane - 32 * q + base_a))
        put_b = hot(inside & (atom == lane - 32 * q + base_b))
        part = mm(ra, put_a) + mm(rb, put_b)
        for g in range(13):
            coef = 4 * g + q
            if coef < 49:
                out_ref[coef] = own_ref[coef * 8 : coef * 8 + 8] + part[g * 8 : g * 8 + 8]


def smem():
    return pl.BlockSpec(memory_space=pltpu.SMEM)


def params():
    return pltpu.CompilerParams(vmem_limit_bytes=VMEM_LIMIT)


def light():
    return pl.CostEstimate(flops=1, bytes_accessed=1, transcendentals=0)


def whole(shape):
    return pl.BlockSpec(shape, lambda *_: (0,) * len(shape))


def sds(shape, dtype):
    return jax.ShapeDtypeStruct(shape, dtype)


def body(
    node_x, cotangent, wigner, src_index, dst_index, edge_scale, edge_count, w_zero, w_one, w_two
):
    chan = lax.axis_index("chan")
    brick = lax.axis_index("brick")
    z, core = chan // 2, chan % 2
    high = brick % 2
    z_s = z.astype(jnp.int32).reshape(1)
    k_s = core.astype(jnp.int32).reshape(1)
    h_s = high.astype(jnp.int32).reshape(1)
    slots = src_index.shape[0]
    steps = slots // EB
    src = src_index.reshape(1, slots)
    dst = dst_index.reshape(1, slots)
    scale = edge_scale.reshape(1, slots)

    def across(x, mask):
        return lax.ppermute(x, "chan", [(i, i ^ mask) for i in range(16)])

    def cross(x):
        return lax.ppermute(x, "brick", [(i, i ^ 1) for i in range(32)])

    def shift(x, away):
        route = [(i, (i + (2 if (i % 2 == 0) == away else -2)) % 32) for i in range(32)]
        return lax.ppermute(x, "brick", route)

    w_tiles = (
        w_zero.transpose(0, 2, 1, 3).reshape(49, 8, 128),
        w_one.transpose(0, 1, 3, 2, 4).reshape(72, 8, 128),
        w_two.transpose(0, 1, 3, 2, 4).reshape(50, 8, 128),
    )
    node, b0, rims, w_own = pl.pallas_call(
        pack_kernel,
        out_shape=(sds((400, 128), BF), sds((400, 128), BF), sds((224, 128), BF), sds((1376, 128), BF)),
        in_specs=[whole((n, 8, 128)) for n in (49, 49, 49, 72, 50)],
        out_specs=(whole((400, 128)), whole((400, 128)), whole((224, 128)), whole((1376, 128))),
        grid=(1,),
        compiler_params=pltpu.CompilerParams(vmem_limit_bytes=PACK_VMEM),
        cost_estimate=light(),
        name="pack",
    )(node_x, cotangent, *w_tiles)
    near = cross(rims)

    def rotated(*blocks):
        return rotate_call(z_s, blocks, dest, factor, wigner)

    b4 = across(b0, 8)
    b2 = across(b0, 4)
    b1 = across(b0, 2)
    far = shift(lax.dynamic_slice_in_dim(near, 112 * high, 112, 0), True)

    x_own, factor, dest = pl.pallas_call(
        edge_in_kernel,
        out_shape=(sds((X_ROWS + 1376, 128), BF), sds((1, slots), F32), sds((1, slots), jnp.int32)),
        grid=(steps,),
        in_specs=[smem(), smem(), whole((400, 128)), whole((224, 128)), whole((112, 128))]
        + [pl.BlockSpec(memory_space=pltpu.HBM), row_spec(), row_spec(), row_spec(), wig_spec()],
        out_specs=(whole((X_ROWS + 1376, 128)), row_spec(), row_spec()),
        scratch_shapes=[pltpu.VMEM((235, EB), F32), pltpu.VMEM((400, EB), F32), pltpu.SemaphoreType.DMA],
        compiler_params=params(),
        cost_estimate=light(),
        name="edge_in",
    )(h_s, edge_count, node, near, far, w_own, src, dst, scale, wigner)
    b4, b2, b1, x_own = lax.optimization_barrier((b4, b2, b1, x_own))
    b6 = across(b4, 4)
    b5 = across(b4, 2)
    b3 = across(b2, 2)
    (eg0,) = rotated(b0, b1)

    b6, b5, b3, x_own, eg0 = lax.optimization_barrier((b6, b5, b3, x_own, eg0))
    b7 = across(b6, 2)
    (eg1,) = rotated(b2, b3)
    (eg2,) = rotated(b4, b5)
    x_sib = across(x_own, 1)

    wz, wo, wt = pl.pallas_call(
        weight_kernel,
        out_shape=(sds((112, 512), BF), sds((192, 768), BF), sds((160, 640), BF)),
        grid=(1,),
        in_specs=[smem(), whole((X_ROWS + 1376, 128)), whole((X_ROWS + 1376, 128))],
        out_specs=(whole((112, 512)), whole((192, 768)), whole((160, 640))),
        compiler_params=params(),
        cost_estimate=light(),
        name="weights",
    )(k_s, x_own, x_sib)

    s_own, g_own, to_sib = edge_call(
        z_s, (eg0, eg1, eg2), (b6, b7), dest, src, factor, wigner, x_own, x_sib, (wz, wo, wt)
    )

    got = across(to_sib, 1)
    s_got = got[:1024].reshape(8, 128, 128)
    s_own = s_own.reshape(8, 128, 128)
    send = jnp.concatenate([s_own, s_got], axis=0)
    groups = [
        [
            (2 * (2 * zb + (k ^ p)) + h) * 16 + 2 * zl + k
            for p in range(2)
            for zb in range(8)
        ]
        for h in range(2)
        for zl in range(8)
        for k in range(2)
    ]
    pieces = lax.all_to_all(send, ("brick", "chan"), 0, 0, axis_index_groups=groups)
    summed = pieces.astype(F32).sum(axis=0).reshape(16, 2, 4, 128)
    mine = jnp.where(high == 0, summed[:, 0], summed[:, 1])
    other = jnp.where(high == 0, summed[:, 1], summed[:, 0])

    g_all = g_own + got[1024:].astype(F32)
    left, right = g_all[400:512].astype(BF), g_all[512:624].astype(BF)
    near_rim = jnp.where(high == 0, right, left)
    far_rim = shift(jnp.where(high == 0, left, right), False)

    crossed = cross(jnp.concatenate([near_rim, far_rim, other.astype(BF).reshape(64, 128)], axis=0))
    grad_x, zero, one, second = pl.pallas_call(
        end_kernel,
        out_shape=(
            sds((49, 8, 128), F32),
            sds((7, 7, 4, 8), F32),
            sds((2, 6, 6, 4, 8), F32),
            sds((2, 5, 5, 4, 8), F32),
        ),
        grid=(1,),
        in_specs=[smem(), whole((624, 128)), whole((64, 128)), whole((288, 128))],
        out_specs=(
            whole((49, 8, 128)),
            whole((7, 7, 4, 8)),
            whole((2, 6, 6, 4, 8)),
            whole((2, 5, 5, 4, 8)),
        ),
        compiler_params=params(),
        name="end",
    )(h_s, g_all, mine.reshape(64, 128), crossed)
    grad_zero = zero.transpose(0, 3, 1, 2)
    grad_one = one.transpose(0, 1, 4, 2, 3)
    grad_two = second.transpose(0, 1, 4, 2, 3)
    return grad_x, grad_zero, grad_one, grad_two


def solution(mesh):
    in_specs = (
        P(None, "chan", "brick"),
        P(None, "chan", "brick"),
        P(None, "brick"),
        P("brick"),
        P("brick"),
        P("brick"),
        P("brick"),
        P(None, "chan", None, None),
        P(None, None, "chan", None, None),
        P(None, None, "chan", None, None),
    )
    out_specs = (
        P(None, "chan", "brick"),
        P(None, "chan", None, "brick"),
        P(None, None, "chan", None, "brick"),
        P(None, None, "chan", None, "brick"),
    )
    return jax.shard_map(body, mesh=mesh, in_specs=in_specs, out_specs=out_specs, check_vma=False)
```
